32 devices in a mesh: dp: 8 (over y, x, core), expert: 4 (over z).
Axes of the slice: x: 2, y: 2, z: 4, core: 2. Of those that a mesh axis runs over, the one named last changes fastest.
Arguments:
- hidden_in: bfloat16 [16, 1024, 2048], P('dp', 'expert'), may hold values from -6 to 6
- cotangent: bfloat16 [16, 1024, 2048], P('dp', 'expert'), may hold values from -6 to 6
- block_ids: int32 [16, 1024], P('dp'), may hold values from 0 to 7, never falling along the last dimension, each value on 1 to 256 neighbouring positions
- attn_routes: int32 [16, 1024, 2], P('dp', 'expert'), may hold values from 0 to 7, all different within a row; in each aligned block of 256 rows (0 to 255, 256 to 511, ..., all dimensions but the last counted through in order) at most 68 rows name the same one
- mlp_routes: int32 [16, 1024, 2], P('dp', 'expert'), may hold values from 0 to 7, all different within a row; in each aligned block of 256 rows (0 to 255, 256 to 511, ..., all dimensions but the last counted through in order) at most 68 rows name the same one
- adapter_index: int32 [16], P('dp'), may hold values from 0 to 7
- attn_gain: float32 [2048], replicated, may hold values from 0.5 to 1.5
- mlp_gain: float32 [2048], replicated, may hold values from 0.1 to 1.9
- attn_router: bfloat16 [2048, 8], replicated, may hold values from -0.125 to 0.125
- mlp_router: bfloat16 [2048, 8], replicated, may hold values from -0.125 to 0.125
- kv_weight: bfloat16 [2048, 4096], P('dp'), may hold values from -0.125 to 0.125
- query_weight: bfloat16 [8, 2048, 2048], P('expert', 'dp'), may hold values from -0.125 to 0.125
- output_weight: bfloat16 [8, 2048, 2048], P('expert', 'dp'), may hold values from -1 to 1
- inner_weight: bfloat16 [8, 2048, 11264], P('expert', 'dp'), may hold values from -0.125 to 0.125
- down_weight: bfloat16 [8, 5632, 2048], P('expert', 'dp'), may hold values from -0.21875 to 0.21875
- adapt_down: bfloat16 [2048, 128], replicated, may hold values from -0.125 to 0.125
- adapt_up: bfloat16 [4096, 128], replicated, may hold values from -1.5 to 1.5
Outputs:
- layer_out: bfloat16 [16, 1024, 2048], P('dp', 'expert')
- input_grad: float32 [16, 1024, 2048], P('dp', 'expert')
- down_grad: float32 [2048, 128], P(('dp', 'expert'))
- up_grad: float32 [4096, 128], P(('dp', 'expert'))
The draws below stay inside these ranges and needn't reach their ends.
Inputs may be any that keep to these rules, and one draw needn't show every extreme that they name: `attn_routes`: each token names 2 different experts. In each aligned block of 256 positions of a sequence no expert is named more than 68 times, and in some block some expert exactly 68 times. `mlp_routes`: each token names 2 different experts. In each aligned block of 256 positions of a sequence no expert is named more than 68 times, and in some block some expert exactly 68 times. `block_ids`: along each sequence the block numbers never fall; each block holds 1 to 256 positions, some block exactly 256.
All inputs are finite; a program needn't handle non-finite values.
Results may differ from the reference program's by a relative error of at most 0.03.
Values may be sent and summed in bfloat16 or wider, within the bound.
No kernel may reach another device: no remote copies, remote signals or barrier semaphores. Data moves between devices by JAX's collectives and lax.ppermute only.
A program may use at most 640 MiB of HBM per device.

```python
import math
import jax
import jax.numpy as jnp
import numpy as np
from jax import lax

D = 2048
HEADS = 16
HDIM = 128
FF = 5632
EXPERTS = 8
TOP = 2
RANK = 16
NADAPT = 8
BLOCK = 256
SEQLEN = 1024
ROWS = 256
SEQS = 16
CAP = 68
BLOCKS = 8


def with_ends(values, rng, least, high):
    spot = [jax.random.randint(jax.random.fold_in(rng, axis), (), 0, length) for axis, length in enumerate(values.shape)]
    main_axis = values.shape.index(max(values.shape))
    next_to = spot[:main_axis] + [(spot[main_axis] + 1) % values.shape[main_axis]] + spot[main_axis + 1:]
    return values.at[tuple(spot)].set(least).at[tuple(next_to)].set(high)


def block_levels(rng, extent, pieces, low, top_value):
    def one(position, blocks):
        steps = jax.random.uniform(jax.random.fold_in(jax.random.fold_in(rng, 6), position), (blocks,), jnp.float32, low / len(pieces), top_value / len(pieces))
        return jnp.repeat(jnp.exp(steps), extent[position] // blocks).reshape((-1,) + (1,) * (len(extent) - position - 1))

    loudness = one(*pieces[0])
    for cut in pieces[1:]:
        loudness = loudness * one(*cut)
    return loudness


def profile(amount, total, reach, skew):
    loads = [(1 << 20) // math.isqrt(standing ** skew) + 1 for standing in range(2, amount + 1)]
    spare, counts = total - reach - (amount - 1), [1] * (amount - 1)
    while spare > 0:
        candidates = [i for i in range(amount - 1) if counts[i] < reach]
        whole, budget = sum([loads[i] for i in candidates]), spare
        for i in candidates:
            extra = min(reach - counts[i], max(1, budget * loads[i] // whole), spare)
            counts[i] = counts[i] + extra
            spare = spare - extra
    return np.array([reach] + counts)


def ragged(key, count, total, limit, lean):
    if count == 2:
        one = jax.random.randint(key, (), max(1, total - limit), min(limit, total - 1) + 1)
        return jnp.stack([one, total - one])
    sizes = jnp.asarray(profile(count, total, limit, lean), jnp.int32)
    couples = (count - 1) // 2
    source_of, receiver = sizes[1:1 + 2 * couples:2], sizes[2:2 + 2 * couples:2]
    room = jnp.minimum(source_of - 1, limit - receiver)
    passed = jax.random.randint(jax.random.fold_in(key, 1), (couples,), 0, 1 << 20) % (room + 1)
    sizes = sizes.at[1:1 + 2 * couples:2].set(source_of - passed).at[2:2 + 2 * couples:2].set(receiver + passed)
    return sizes[jax.random.permutation(jax.random.fold_in(key, 2), count)]


def assign_block(rng, own, number, rows, count, top, reach, skew):
    order = jax.random.permutation(rng, count)
    crowded, usual = portions_of(count, rows * top, reach, skew, True), portions_of(count, rows * top, reach, skew, False)
    places = jnp.arange(count)

    def named(sizes, turn):
        used = int((sizes > 0).sum())
        fixed = max(1, used // 4)
        passed = fixed + (places - fixed + turn * (used - fixed)) % max(1, count - fixed)
        return jnp.zeros((count,), jnp.int32).at[order[jnp.where(places < fixed, places, passed)]].set(jnp.asarray(sizes, jnp.int32))

    sizes = jnp.where(number % 4 == 0, named(crowded, number // 4), named(usual, number - number // 4 - 1))
    mixed = jax.random.permutation(jax.random.fold_in(own, 3), count)
    giver, sink = mixed[0:count // 2 * 2:2], mixed[1:count // 2 * 2:2]
    slack = jnp.minimum(sizes[giver] - 1, reach - sizes[sink]) // 2
    slack = jnp.where((giver == order[0]) | (sink == order[0]) | (sizes[sink] == 0), 0, jnp.maximum(slack, 0))
    passed = jax.random.randint(jax.random.fold_in(own, 4), (count // 2,), 0, 1 << 20) % (slack + 1)
    sizes = sizes.at[giver].add(-passed).at[sink].add(passed)
    members = jnp.searchsorted(jnp.cumsum(sizes), jnp.arange(rows * top), side="right").astype(jnp.int32)
    listing = members.reshape(top, rows).T
    listing = listing[jax.random.permutation(jax.random.fold_in(own, 1), rows)]
    turn = jax.random.randint(jax.random.fold_in(own, 2), (rows, 1), 0, top)
    return jnp.take_along_axis(listing, (jnp.arange(top)[None, :] + turn) % top, axis=1)


def portions_of(number_of, total, limit, lean, full):
    portions = [(1 << 20) // math.isqrt(grade ** lean) + 1 for grade in range(1, number_of + 1)]
    largest = limit if full else min(limit, max(-(-total // number_of), total * portions[0] // sum(portions)))
    least = 1 if total - largest >= number_of - 1 else 0
    given, spare = [largest] + [least] * (number_of - 1), total - largest - least * (number_of - 1)
    while spare > 0:
        candidates = [i for i in range(1, number_of) if given[i] < largest] or [i for i in range(1, number_of) if given[i] < limit]
        whole, left = sum([portions[i] for i in candidates]), spare
        for i in candidates:
            addition = min(limit - given[i], max(1, left * portions[i] // whole), spare)
            given[i] = given[i] + addition
            spare = spare - addition
    return np.array(given)


def bell_draw(key, dims, scale, reach, cuts=(), kind=jnp.bfloat16):
    level = block_levels(key, dims, cuts, -0.22, 0.18) if cuts else 1.0
    values = jax.random.normal(key, dims, jnp.float32) * scale * level
    return jnp.minimum(jnp.maximum(values, -reach), reach).astype(kind)


def setup_inputs(seed: int = 0) -> dict:
    arg_keys = jax.random.split(jax.random.key(seed), 18)
    hidden_in = bell_draw(arg_keys[0], (SEQS, SEQLEN, D), 1.0, 6.0, ((0, 8), (1, 4)))
    cotangent = bell_draw(arg_keys[1], (SEQS, SEQLEN, D), 1.0, 6.0, ((0, 8), (1, 4)))
    block_ids = jax.vmap(lambda own: jnp.searchsorted(jnp.cumsum(ragged(own, BLOCKS, SEQLEN, BLOCK, 1)), jnp.arange(SEQLEN), side="right"))(jax.random.split(arg_keys[2], SEQS)).reshape((SEQS, SEQLEN)).astype(jnp.int32)
    attn_routes_keys = jax.random.split(jax.random.fold_in(arg_keys[3], 1), SEQS * SEQLEN // ROWS)
    attn_routes_turns = jax.random.permutation(jax.random.fold_in(arg_keys[3], 3), SEQS * SEQLEN // ROWS)
    attn_routes = jax.vmap(lambda own, number: assign_block(jax.random.fold_in(arg_keys[3], 2), own, number, ROWS, EXPERTS, TOP, CAP, 1))(attn_routes_keys, attn_routes_turns).reshape((SEQS, SEQLEN, TOP))
    mlp_routes_keys = jax.random.split(jax.random.fold_in(arg_keys[4], 1), SEQS * SEQLEN // ROWS)
    mlp_routes_turns = jax.random.permutation(jax.random.fold_in(arg_keys[4], 3), SEQS * SEQLEN // ROWS)
    mlp_routes = jax.vmap(lambda own, number: assign_block(jax.random.fold_in(arg_keys[4], 2), own, number, ROWS, EXPERTS, TOP, CAP, 1))(mlp_routes_keys, mlp_routes_turns).reshape((SEQS, SEQLEN, TOP))
    adapter_index = with_ends(jax.random.randint(arg_keys[5], (SEQS,), 0, NADAPT), jax.random.fold_in(arg_keys[5], 1), 0, NADAPT - 1).astype(jnp.int32)
    attn_gain = jnp.clip(1.0 + 0.1 * jax.random.normal(arg_keys[6], (D,), jnp.float32), 0.5, 1.5)
    mlp_gain = jnp.clip(1.0 + 0.18 * jax.random.normal(arg_keys[7], (D,), jnp.float32), 0.1, 1.9)
    attn_router = bell_draw(arg_keys[8], (D, EXPERTS), D ** -0.5, 0.125)
    mlp_router = bell_draw(arg_keys[9], (D, EXPERTS), D ** -0.5, 0.125)
    kv_weight = bell_draw(arg_keys[10], (D, 2 * D), D ** -0.5, 0.125, ((0, 8),))
    query_weight = bell_draw(arg_keys[11], (EXPERTS, D, D), D ** -0.5, 0.125, ((0, 4), (1, 8)))
    output_weight = bell_draw(arg_keys[12], (EXPERTS, D, D), (D // 64) ** -0.5, 1.0, ((0, 4), (1, 8)))
    inner_weight = bell_draw(arg_keys[13], (EXPERTS, D, 2 * FF), D ** -0.5, 0.125, ((0, 4), (1, 8)))
    down_weight = bell_draw(arg_keys[14], (EXPERTS, FF, D), (FF // 8) ** -0.5, 0.21875, ((0, 4), (1, 8)))
    adapt_down = bell_draw(arg_keys[15], (D, NADAPT * RANK), D ** -0.5, 0.125)
    adapt_up = bell_draw(arg_keys[16], (2 * D, NADAPT * RANK), RANK ** -0.5, 1.5)
    return {"hidden_in": hidden_in, "cotangent": cotangent, "block_ids": block_ids, "attn_routes": attn_routes, "mlp_routes": mlp_routes, "adapter_index": adapter_index, "attn_gain": attn_gain, "mlp_gain": mlp_gain, "attn_router": attn_router, "mlp_router": mlp_router, "kv_weight": kv_weight, "query_weight": query_weight, "output_weight": output_weight, "inner_weight": inner_weight, "down_weight": down_weight, "adapt_down": adapt_down, "adapt_up": adapt_up}


PRECISE = lax.Precision.HIGHEST
EPSILON = 1e-06
ROPE_BASE = 10000.0
MASKED_SCORE = -1e+30

@jax.custom_vjp
def low(v):
    return lax.optimization_barrier(v.astype(jnp.bfloat16)).astype(jnp.float32)

@jax.custom_vjp
def low_back(v):
    return v

def low_keep(v):
    return (low(v), None)

def low_pass(kept, grad):
    return (grad,)

def back_keep(v):
    return (v, None)

def back_low(kept, grad):
    return (low(grad),)
low.defvjp(low_keep, low_pass)
low_back.defvjp(back_keep, back_low)

def rms_scale(values):
    return lax.rsqrt(lax.optimization_barrier(jnp.mean(values * values, axis=-1, keepdims=True)) + EPSILON)

def angle_tables(positions):
    half_dim = HDIM // 2
    frequency = ROPE_BASE ** (-(jnp.arange(half_dim, dtype=jnp.float32) * (2.0 / HDIM)))
    angles = positions.astype(jnp.float32)[:, None] * frequency[None, :]
    return (jnp.cos(angles), jnp.sin(angles))

def rotate(values, cos_tab, sin_tab):
    half_dim = HDIM // 2
    first_half = values[..., :half_dim]
    second_half = values[..., half_dim:]
    return jnp.concatenate([first_half * cos_tab - second_half * sin_tab, second_half * cos_tab + first_half * sin_tab], axis=-1)

def pair_gates(logits, route_ids):
    picked = jnp.take_along_axis(logits, route_ids, axis=1)
    logit_gap = picked[:, 0] - picked[:, 1]
    return jnp.stack([jax.nn.sigmoid(logit_gap), jax.nn.sigmoid(-logit_gap)], axis=1)

def layer(seq_in, blocks_in, attn_route, mlp_route, down_sel, up_sel, weights):
    attn_gain, mlp_gain, attn_router, mlp_router, kv_weight, query_weight, output_weight, inner_weight, down_weight = weights
    length = seq_in.shape[0]
    positions = jnp.arange(length, dtype=jnp.int32)
    cos_tab, sin_tab = angle_tables(positions)
    scale_qk = 1.0 / math.sqrt(HDIM)
    normed = seq_in * rms_scale(seq_in) * attn_gain
    normed_low = low(normed)
    gate_pair_a = pair_gates(jnp.dot(normed, attn_router, precision=PRECISE), attn_route)
    low_rank = low(low_back(jnp.dot(normed_low, down_sel, precision=PRECISE)))
    key_value = low_back(jnp.dot(normed_low, kv_weight, precision=PRECISE) + jnp.dot(low_rank, up_sel.T, precision=PRECISE))
    key_rows = low(low_back(rotate(key_value[:, :D].reshape(length, HEADS, HDIM), cos_tab[:, None, :], sin_tab[:, None, :])))
    value_rows = low(low_back(key_value[:, D:].reshape(length, HEADS, HDIM)))
    queries = []
    for expert in range(EXPERTS):
        source = low_back(normed_low)
        queries.append(low_back(low(jnp.dot(source, query_weight[expert], precision=PRECISE))))
    queries = jnp.stack(queries)
    picked = queries[attn_route, positions[:, None]].reshape(length, TOP, HEADS, HDIM)
    query_rot = low(rotate(picked, cos_tab[:, None, None, :], sin_tab[:, None, None, :]))
    scores = low_back(jnp.einsum('tjhd,khd->hjtk', query_rot, key_rows, precision=PRECISE) * scale_qk)
    visible = blocks_in[None, :] <= blocks_in[:, None]
    masked = jnp.where(visible, scores, MASKED_SCORE)
    row_max = lax.optimization_barrier(jnp.max(masked, axis=-1, keepdims=True))
    log_total = row_max + jnp.log(lax.optimization_barrier(jnp.sum(jnp.exp(masked - row_max), axis=-1, keepdims=True)))
    attn_probs = jnp.where(visible, jnp.exp(masked - log_total), 0.0)
    attended = low(jnp.einsum('hjtk,khd->tjhd', low(attn_probs), value_rows, precision=PRECISE)).reshape(length, TOP, D)
    attn_total = jnp.zeros_like(seq_in)
    for expert in range(EXPERTS):
        chosen = attn_route == expert
        source = low_back(lax.optimization_barrier(jnp.sum(jnp.where(chosen[:, :, None], attended, 0.0), axis=1)))
        result = low_back(low(jnp.dot(source, output_weight[expert], precision=PRECISE)))
        portion = lax.optimization_barrier(jnp.sum(jnp.where(chosen, gate_pair_a, 0.0), axis=1))
        attn_total = attn_total + portion[:, None] * result
    middle = seq_in + attn_total
    normed_two = middle * rms_scale(middle) * mlp_gain
    normed_two_low = low(normed_two)
    gate_pair_m = pair_gates(jnp.dot(normed_two, mlp_router, precision=PRECISE), mlp_route)
    row_limit = SEQLEN // ROWS * CAP
    mlp_total = jnp.zeros_like(seq_in)
    for expert in range(EXPERTS):
        chosen = mlp_route == expert
        member = jnp.any(chosen, axis=1).astype(jnp.int32)
        rank_in = jnp.cumsum(member).astype(jnp.int32) - member
        target = jnp.where(member == 1, rank_in, row_limit).astype(jnp.int32)
        row_index = jnp.zeros((row_limit,), jnp.int32).at[target].set(positions, mode='drop')
        portion = lax.optimization_barrier(jnp.sum(jnp.where(chosen, gate_pair_m, 0.0), axis=1))
        is_valid = jnp.arange(row_limit, dtype=jnp.int32) < jnp.sum(member).astype(jnp.int32)
        weight_rows = jnp.where(is_valid, portion[row_index], 0.0)
        source = low_back(normed_two_low[row_index])
        inner_out = low_back(jnp.dot(source, inner_weight[expert], precision=PRECISE))
        hidden = low(jax.nn.silu(inner_out[:, :FF]) * inner_out[:, FF:])
        result = low_back(low(jnp.dot(hidden, down_weight[expert], precision=PRECISE)))
        mlp_total = mlp_total.at[row_index].add(weight_rows[:, None] * result)
    return middle + mlp_total

def reference(hidden_in, cotangent, block_ids, attn_routes, mlp_routes, adapter_index, attn_gain, mlp_gain, attn_router, mlp_router, kv_weight, query_weight, output_weight, inner_weight, down_weight, adapt_down, adapt_up):
    weights = tuple((w.astype(jnp.float32) for w in (attn_gain, mlp_gain, attn_router, mlp_router, kv_weight, query_weight, output_weight, inner_weight, down_weight)))
    run_layer = jax.checkpoint(layer)

    def forward(inputs, down_all, up_all):

        def scan_step(state_in, per_seq):
            seq_in, blocks_in, attn_route, mlp_route, which = per_seq
            adapt_start = (which * RANK).astype(jnp.int32)
            down_sel = lax.dynamic_slice_in_dim(down_all, adapt_start, RANK, 1)
            up_sel = lax.dynamic_slice_in_dim(up_all, adapt_start, RANK, 1)
            return (state_in, run_layer(seq_in, blocks_in, attn_route, mlp_route, down_sel, up_sel, weights))
        state_out, outputs = lax.scan(scan_step, jnp.zeros((), jnp.float32), (inputs, block_ids, attn_routes, mlp_routes, adapter_index))
        return outputs
    outputs, pullback = jax.vjp(forward, hidden_in.astype(jnp.float32), adapt_down.astype(jnp.float32), adapt_up.astype(jnp.float32))
    input_grad, down_grad, up_grad = pullback(cotangent.astype(jnp.float32))
    return (outputs.astype(jnp.bfloat16), input_grad, down_grad, up_grad)
```

```python
import functools
import math

import jax
import jax.numpy as jnp
import numpy as np
from jax import lax
from jax.experimental import pallas as pl
from jax.experimental.pallas import tpu as pltpu
from jax.sharding import PartitionSpec as P

HEADS = 16
HDIM = 128
FF = 5632
EXPERTS = 8
TOP = 2
RANK = 16
NADAPT = 8

PRECISE = lax.Precision.HIGHEST
EPSILON = 1e-06
ROPE_BASE = 10000.0
MASKED_SCORE = -1e30
SCALE_QK = 1.0 / math.sqrt(HDIM)
BF16 = jnp.bfloat16
F32 = jnp.float32
VMEM_LIMIT = 58 * 1024 * 1024

NN = (((1,), (0,)), ((), ()))
NT = (((1,), (1,)), ((), ()))
TN = (((0,), (0,)), ((), ()))


def mm(left, right, dims=NN):
    return lax.dot_general(left, right, dims, preferred_element_type=F32)


def params(*semantics):
    return pltpu.CompilerParams(dimension_semantics=semantics, vmem_limit_bytes=VMEM_LIMIT)


def once(shape, index_map):
    return pl.BlockSpec(shape, index_map, pipeline_mode=pl.Buffered(1))


def rms_scale(values):
    return lax.rsqrt(jnp.mean(values * values, axis=-1, keepdims=True) + EPSILON)


def norm_back(values, scale_rows, norm_gain, grad_rows):
    scaled_grad = norm_gain * grad_rows
    return scale_rows * (
        scaled_grad
        - values * scale_rows * scale_rows * jnp.mean(scaled_grad * values, axis=-1, keepdims=True)
    )


def angle_tables(positions):
    half_dim = HDIM // 2
    frequency = ROPE_BASE ** (-(jnp.arange(half_dim, dtype=F32) * (2.0 / HDIM)))
    frequency = jnp.concatenate([frequency, frequency])
    sign = jnp.concatenate([-jnp.ones((half_dim,), F32), jnp.ones((half_dim,), F32)])
    angles = positions.astype(F32)[..., None] * frequency
    return (jnp.cos(angles), jnp.sin(angles) * sign)


def three_parts(values):
    first = values.astype(BF16)
    rest = values - first.astype(F32)
    second = rest.astype(BF16)
    third = (rest - second.astype(F32)).astype(BF16)
    return first, second, third


def gather_line(block, axis, size, put, start):
    here = lax.axis_index(axis)
    rightward = [(i, i + 1) for i in range(size - 1)]
    leftward = [(i + 1, i) for i in range(size - 1)]
    from_left, from_right = [block], [block]
    for _ in range(size - 1):
        from_left.append(lax.ppermute(from_left[-1], axis, rightward))
        from_right.append(lax.ppermute(from_right[-1], axis, leftward))
    total = put(start, block, here)
    for step in range(1, size):
        piece = jnp.where(here >= step, from_left[step], from_right[size - step])
        total = put(total, piece, lax.rem(here - step + size, size))
    return total


def send(buffer):
    return lax.all_to_all(buffer, "expert", split_axis=0, concat_axis=0, tiled=True)


def kv_body(seqs, seq_len, key_tiles, x_ref, low_ref, w_ref, up_ref, cos_ref, sin_ref, out_ref):
    is_key = pl.program_id(0) < key_tiles
    for s in range(seqs):
        rows = pl.ds(s * seq_len, seq_len)
        made = mm(x_ref[rows, :], w_ref[...]) + mm(low_ref[rows, :], up_ref[...], NT)

        @pl.when(is_key)
        def _(made=made, rows=rows):
            for h in range(made.shape[1] // HDIM):
                cols = slice(h * HDIM, (h + 1) * HDIM)
                part = made[:, cols]
                turned = part * cos_ref[...] + pltpu.roll(part, HDIM // 2, 1) * sin_ref[...]
                out_ref[rows, cols] = turned.astype(BF16)

        @pl.when(jnp.logical_not(is_key))
        def _(made=made, rows=rows):
            out_ref[rows, :] = made.astype(BF16)


def make_key_value(normed_low, low_rank, kv_full, adapt_up, cos_k, sin_k, seqs):
    rows, width = normed_low.shape
    seq_len = rows // seqs
    tile = 512
    return pl.pallas_call(
        functools.partial(kv_body, seqs, seq_len, width // tile),
        grid=(2 * width // tile,),
        in_specs=[
            once((rows, width), lambda i: (0, 0)),
            once((rows, low_rank.shape[1]), lambda i: (0, 0)),
            pl.BlockSpec((width, tile), lambda i: (0, i)),
            pl.BlockSpec((tile, low_rank.shape[1]), lambda i: (i, 0)),
            once((seq_len, HDIM), lambda i: (0, 0)),
            once((seq_len, HDIM), lambda i: (0, 0)),
        ],
        out_specs=pl.BlockSpec((rows, tile), lambda i: (0, i)),
        out_shape=jax.ShapeDtypeStruct((rows, 2 * width), BF16),
        compiler_params=params("arbitrary"),
        name="key_value",
    )(normed_low, low_rank, kv_full, adapt_up, cos_k, sin_k)


def attend_body(q_ref, k_ref, v_ref, cos_ref, sin_ref, qb_ref, kb_ref, rot_ref, out_ref, lse_ref):
    locals_, _, slots, _ = q_ref.shape
    rows = locals_ * slots
    q = q_ref[...].reshape(rows, HDIM).astype(F32)
    cos, sin = cos_ref[...].reshape(rows, HDIM), sin_ref[...].reshape(rows, HDIM)
    rot = (q * cos + pltpu.roll(q, HDIM // 2, 1) * sin).astype(BF16)
    rot_ref[...] = rot.reshape(rot_ref.shape)
    k, v = k_ref[0], v_ref[0]
    kb = kb_ref[0]
    for l in range(locals_):
        part = rot[l * slots : (l + 1) * slots]
        visible = kb <= qb_ref[l, 0]
        masked = jnp.where(visible, mm(part, k, NT), MASKED_SCORE)
        top = jnp.max(masked, axis=-1, keepdims=True)
        terms = jnp.exp((masked - top) * SCALE_QK)
        total = jnp.sum(terms, axis=-1, keepdims=True)
        out = mm(terms.astype(BF16), v) * (1.0 / total)
        out_ref[l, 0] = out.astype(BF16)
        lse_ref[l, 0, 0] = top * SCALE_QK + jnp.log(total)


def attend(queries, key_value, cos_q, sin_q, query_blocks, key_blocks):
    locals_, seqs, slots, width = queries.shape
    seq_len = key_value.shape[1]
    q_spec = pl.BlockSpec((locals_, 1, slots, HDIM), lambda s, h: (0, s, 0, h))
    tab_spec = pl.BlockSpec((locals_, 1, slots, HDIM), lambda s, h: (0, s, 0, 0))
    return pl.pallas_call(
        attend_body,
        grid=(seqs, HEADS),
        in_specs=[
            q_spec,
            pl.BlockSpec((1, seq_len, HDIM), lambda s, h: (s, 0, h)),
            pl.BlockSpec((1, seq_len, HDIM), lambda s, h: (s, 0, HEADS + h)),
            tab_spec,
            tab_spec,
            pl.BlockSpec((locals_, 1, slots, 1), lambda s, h: (0, s, 0, 0)),
            pl.BlockSpec((1, 1, seq_len), lambda s, h: (s, 0, 0)),
        ],
        out_specs=[
            q_spec,
            q_spec,
            pl.BlockSpec((locals_, 1, 1, slots, 1), lambda s, h: (0, s, h, 0, 0)),
        ],
        out_shape=[
            jax.ShapeDtypeStruct(queries.shape, BF16),
            jax.ShapeDtypeStruct(queries.shape, BF16),
            jax.ShapeDtypeStruct((locals_, seqs, HEADS, slots, 1), F32),
        ],
        compiler_params=params("arbitrary", "arbitrary"),
        name="attend",
    )(queries, key_value, key_value, cos_q, sin_q, query_blocks, key_blocks)


def attend_back_body(
    q_ref, k_ref, v_ref, g_ref, lse_ref, cos_ref, sin_ref, qb_ref, kb_ref, ck_ref, sk_ref, dq_ref, dk_ref, dv_ref
):
    locals_, _, slots, _ = q_ref.shape
    k, v = k_ref[0], v_ref[0]
    kb = kb_ref[0]
    dk = dv = None
    for l in range(locals_):
        q, grad = q_ref[l, 0], g_ref[l]
        visible = kb <= qb_ref[l, 0]
        scores = mm(q, k, NT) * SCALE_QK - lse_ref[l, 0, 0]
        probs = jnp.where(visible, jnp.exp(jnp.where(visible, scores, MASKED_SCORE)), 0.0)
        grad_probs = mm(grad, v, NT)
        weighed = probs * grad_probs
        delta = jnp.sum(weighed, axis=-1, keepdims=True)
        grad_scores = (weighed - probs * delta).astype(BF16)
        dq = mm(grad_scores, k) * SCALE_QK
        dq = dq * cos_ref[l, 0] - pltpu.roll(dq, HDIM // 2, 1) * sin_ref[l, 0]
        dq_ref[l] = dq.astype(BF16)
        dk_part = mm(grad_scores, q, TN)
        dv_part = mm(probs.astype(BF16), grad, TN)
        dk = dk_part if dk is None else dk + dk_part
        dv = dv_part if dv is None else dv + dv_part
    dk = dk * SCALE_QK
    dk_ref[...] = (dk * ck_ref[...] - pltpu.roll(dk, HDIM // 2, 1) * sk_ref[...]).astype(BF16)
    dv_ref[...] = dv.astype(BF16)


def attend_back(s, query_rot, key_value, grad, lse, cos_q, sin_q, query_blocks, key_blocks, cos_k, sin_k):
    locals_, _, slots, width = query_rot.shape
    seq_len = key_value.shape[1]
    tab_spec = pl.BlockSpec((locals_, 1, slots, HDIM), lambda h: (0, s, 0, 0))
    key_tab = pl.BlockSpec((seq_len, HDIM), lambda h: (0, 0))
    grad_spec = pl.BlockSpec((locals_, slots, HDIM), lambda h: (0, 0, h))
    key_spec = pl.BlockSpec((seq_len, HDIM), lambda h: (0, h))
    return pl.pallas_call(
        attend_back_body,
        grid=(HEADS,),
        in_specs=[
            pl.BlockSpec((locals_, 1, slots, HDIM), lambda h: (0, s, 0, h)),
            pl.BlockSpec((1, seq_len, HDIM), lambda h: (s, 0, h)),
            pl.BlockSpec((1, seq_len, HDIM), lambda h: (s, 0, HEADS + h)),
            grad_spec,
            pl.BlockSpec((locals_, 1, 1, slots, 1), lambda h: (0, s, h, 0, 0)),
            tab_spec,
            tab_spec,
            pl.BlockSpec((locals_, 1, slots, 1), lambda h: (0, s, 0, 0)),
            pl.BlockSpec((1, 1, seq_len), lambda h: (s, 0, 0)),
            key_tab,
            key_tab,
        ],
        out_specs=[grad_spec, key_spec, key_spec],
        out_shape=[
            jax.ShapeDtypeStruct((locals_, slots, width), BF16),
            jax.ShapeDtypeStruct((seq_len, width), BF16),
            jax.ShapeDtypeStruct((seq_len, width), BF16),
        ],
        compiler_params=params("arbitrary"),
        name="attend_back",
    )(query_rot, key_value, key_value, grad, lse, cos_q, sin_q, query_blocks, key_blocks, cos_k, sin_k)


def expert_body(has_start, x_ref, c_ref, wg_ref, wu_ref, wd_ref, *refs):
    out_ref, gs_ref = refs[-2:]

    @pl.when(pl.program_id(0) == 0)
    def _():
        if has_start:
            out_ref[...] = refs[0][...]
            gs_ref[...] = refs[1][...]
        else:
            out_ref[...] = jnp.zeros_like(out_ref)
            gs_ref[...] = jnp.zeros_like(gs_ref)

    x, c = x_ref[...], c_ref[...]
    wg, wu, wd = wg_ref[...], wu_ref[...], wd_ref[...]
    gate, up = mm(x, wg), mm(x, wu)
    sig = jax.nn.sigmoid(gate)
    silu = gate * sig
    out_ref[...] += mm((silu * up).astype(BF16), wd)
    grad = mm(c, wd, NT)
    grad_gate = (grad * up * sig * (1.0 + gate * (1.0 - sig))).astype(BF16)
    grad_up = (grad * silu).astype(BF16)
    gs_ref[...] += mm(grad_gate, wg, NT) + mm(grad_up, wu, NT)


def expert_pass(rows_in, grad_in, inner, down, down_from, start=None):
    rows, width = rows_in.shape
    units = inner.shape[1] // 2
    tile = 512 if units % 512 == 0 and down_from % 512 == 0 else 256
    whole = once((rows, width), lambda i: (0, 0))
    first = down_from // tile
    more = [] if start is None else list(start)
    return pl.pallas_call(
        functools.partial(expert_body, start is not None),
        grid=(units // tile,),
        in_specs=[
            whole,
            whole,
            pl.BlockSpec((width, tile), lambda i: (0, i)),
            pl.BlockSpec((width, tile), lambda i: (0, units // tile + i)),
            pl.BlockSpec((tile, width), lambda i: (first + i, 0)),
        ]
        + [whole] * len(more),
        out_specs=[pl.BlockSpec((rows, width), lambda i: (0, 0))] * 2,
        out_shape=[jax.ShapeDtypeStruct((rows, width), F32)] * 2,
        compiler_params=params("arbitrary"),
        name="expert",
    )(rows_in, grad_in, inner, inner, down, *more)


def last_body(dk_ref, dv_ref, w_ref, table_ref, gs_ref, low_ref, down_ref, out_ref):
    width = dk_ref.shape[1]
    total = mm(dk_ref[...], w_ref[:, :width], NT) + mm(dv_ref[...], w_ref[:, width:], NT)
    total += mm(table_ref[...], gs_ref[...])
    total += mm(low_ref[...], down_ref[...], NT)
    out_ref[...] = total.astype(BF16)


def last_grad(dk, dv, kv_full, table, grad_source, grad_low, adapt_down):
    seq_len, width = dk.shape
    slots = grad_source.shape[0]
    tile = 512
    return pl.pallas_call(
        last_body,
        grid=(width // tile,),
        in_specs=[
            once((seq_len, width), lambda i: (0, 0)),
            once((seq_len, width), lambda i: (0, 0)),
            pl.BlockSpec((tile, 2 * width), lambda i: (i, 0)),
            once((seq_len, slots), lambda i: (0, 0)),
            pl.BlockSpec((slots, tile), lambda i: (0, i)),
            once((seq_len, grad_low.shape[1]), lambda i: (0, 0)),
            pl.BlockSpec((tile, grad_low.shape[1]), lambda i: (i, 0)),
        ],
        out_specs=pl.BlockSpec((seq_len, tile), lambda i: (0, i)),
        out_shape=jax.ShapeDtypeStruct((seq_len, width), BF16),
        compiler_params=params("arbitrary"),
        name="last_grad",
    )(dk, dv, kv_full, table, grad_source, grad_low, adapt_down)


def per_device(
    hidden_in,
    cotangent,
    block_ids,
    attn_routes,
    mlp_routes,
    adapter_index,
    attn_gain,
    mlp_gain,
    attn_router,
    mlp_router,
    kv_weight,
    query_weight,
    output_weight,
    inner_weight,
    down_weight,
    adapt_down,
    adapt_up,
):
    seqs, row_count, width = hidden_in.shape
    seq_len = block_ids.shape[1]
    ranks = seq_len // row_count
    locals_ = query_weight.shape[0]
    capacity = (17 * row_count * TOP + 16 * EXPERTS - 1) // (16 * EXPERTS)
    slots = ranks * capacity
    here = lax.axis_index("expert")

    kv_full = lax.all_gather(kv_weight, "dp", axis=0, tiled=True)
    query_full = lax.all_gather(query_weight, "dp", axis=1, tiled=True)
    output_full = lax.all_gather(output_weight, "dp", axis=1, tiled=True)
    cut = (FF * 3 // 4) // 256 * 256
    expert_weights = []
    for l in range(locals_):
        down_full = lax.all_gather(down_weight[l], "dp", axis=0, tiled=True)
        if l + 1 < locals_:
            pieces = [(0, lax.all_gather(inner_weight[l], "dp", axis=0, tiled=True))]
        else:
            pieces = []
            for low, high in ((0, cut), (cut, FF)):
                part = jnp.concatenate(
                    [inner_weight[l, :, low:high], inner_weight[l, :, FF + low : FF + high]], axis=1
                )
                pieces.append((low, lax.all_gather(part, "dp", axis=0, tiled=True)))
        expert_weights.append((down_full, pieces))

    routes = lax.all_gather(
        jnp.concatenate([attn_routes, mlp_routes], axis=-1), "expert", axis=1, tiled=True
    ).reshape(seqs, ranks, row_count, 2, TOP)
    adapters = lax.all_gather(adapter_index, "dp", axis=0, tiled=True)
    expert_ids = jnp.arange(EXPERTS, dtype=jnp.int32)
    onehot = (routes[..., None] == expert_ids).astype(F32)
    hits = jnp.sum(onehot, axis=4)
    earlier = (
        jnp.arange(row_count)[:, None] > jnp.arange(row_count)[None, :]
    ).astype(BF16)
    before = jnp.einsum("ut,sptke->spuke", earlier, hits.astype(BF16), preferred_element_type=F32)
    place = jnp.sum(onehot * before[..., None, :], axis=-1).astype(jnp.int32)
    attn_all, mlp_all = routes[:, :, :, 0], routes[:, :, :, 1]
    attn_place, mlp_place = place[:, :, :, 0], place[:, :, :, 1]
    source = jnp.arange(ranks, dtype=jnp.int32)[None, :, None, None]
    which = jnp.arange(seqs, dtype=jnp.int32)[:, None, None, None]

    local_a = attn_all - here * locals_
    is_local = (local_a >= 0) & (local_a < locals_)
    slot_a = jnp.where(is_local, local_a * slots + source * capacity + attn_place, -1)
    slot_a = slot_a.reshape(seqs, seq_len, TOP)
    slot_iota = jnp.arange(locals_ * slots, dtype=jnp.int32)
    spread_a = (
        (slot_iota[None, :, None] == slot_a[:, None, :, 0])
        | (slot_iota[None, :, None] == slot_a[:, None, :, 1])
    ).astype(BF16)
    collect_a = (
        (slot_iota[None, None, :] == slot_a[:, :, 0, None])
        | (slot_iota[None, None, :] == slot_a[:, :, 1, None])
    ).astype(BF16)

    def own(array):
        return lax.dynamic_index_in_dim(array, here, 1, keepdims=False)

    attn_own, attn_own_place = own(attn_all), own(attn_place)
    mlp_own, mlp_own_place = own(mlp_all), own(mlp_place)
    own_slot = attn_own * capacity + attn_own_place
    own_iota = jnp.arange(EXPERTS * capacity, dtype=jnp.int32)
    own_spread_a = (
        (own_iota[None, :, None] == own_slot[:, None, :, 0])
        | (own_iota[None, :, None] == own_slot[:, None, :, 1])
    ).astype(BF16)
    own_collect_a = (
        (own_iota[None, None, :] == own_slot[:, :, 0, None])
        | (own_iota[None, None, :] == own_slot[:, :, 1, None])
    ).astype(BF16)
    mlp_rows = ranks * seqs * capacity
    mlp_iota = jnp.arange(mlp_rows, dtype=jnp.int32)
    own_spread_m, own_collect_m, other_sum = [], [], []
    for l in range(locals_):
        ids = jnp.where(
            mlp_own % locals_ == l,
            (mlp_own // locals_) * (seqs * capacity) + which[:, 0] * capacity + mlp_own_place,
            -1,
        ).reshape(seqs * row_count, TOP)
        own_spread_m.append(
            ((mlp_iota[:, None] == ids[None, :, 0]) | (mlp_iota[:, None] == ids[None, :, 1])).astype(BF16)
        )
        own_collect_m.append(
            ((mlp_iota[None, :] == ids[:, 0, None]) | (mlp_iota[None, :] == ids[:, 1, None])).astype(BF16)
        )
        ids = jnp.where(
            mlp_all == here * locals_ + l,
            source * (seqs * capacity) + which * capacity + mlp_place,
            -1,
        ).reshape(seqs * seq_len, TOP)
        table = (
            (mlp_iota[:, None] == ids[None, :, 0]) | (mlp_iota[:, None] == ids[None, :, 1])
        ).astype(BF16)
        both = jnp.sum(mlp_all, axis=-1).reshape(seqs * seq_len, 1).astype(BF16)
        sums = mm(table, jnp.concatenate([both, jnp.ones_like(both)], axis=1))
        other_sum.append((sums[:, :1], sums[:, 1:]))

    flat_cot = cotangent.reshape(seqs * row_count, width)
    cot_rows = [send(mm(own_spread_m[l], flat_cot).astype(BF16)) for l in range(locals_)]

    everyone = gather_line(
        hidden_in,
        "expert",
        ranks,
        lambda total, piece, at: lax.dynamic_update_slice(total, piece[:, None], (0, at, 0, 0)),
        jnp.zeros((seqs, ranks, row_count, width), BF16),
    ).reshape(seqs, seq_len, width)
    tokens_all = everyone.astype(F32)
    scale_all = rms_scale(tokens_all)
    normed_low = (tokens_all * scale_all * attn_gain).astype(BF16)
    router_parts = jnp.concatenate(three_parts(attn_gain[:, None] * attn_router.astype(F32)), axis=1)
    parts = mm(everyone.reshape(seqs * seq_len, width), router_parts).reshape(seqs, seq_len, 3, EXPERTS)
    logits = scale_all * (parts[:, :, 0] + (parts[:, :, 1] + parts[:, :, 2]))
    onehot_a = onehot[:, :, :, 0].reshape(seqs, seq_len, TOP, EXPERTS)
    gap = jnp.sum((onehot_a[:, :, 0] - onehot_a[:, :, 1]) * logits, axis=-1)

    flat_routes = attn_all.reshape(seqs, seq_len, TOP)
    places = jnp.arange(seq_len, dtype=jnp.int32)
    columns = [
        block_ids,
        jnp.broadcast_to(places // 128, block_ids.shape),
        jnp.broadcast_to(places % 128, block_ids.shape),
        jnp.sum(flat_routes, axis=-1),
        flat_routes[..., 0],
    ]
    known = jnp.stack([c.astype(BF16) for c in columns] + list(three_parts(gap)), axis=-1)
    known = jnp.einsum("srt,stc->src", spread_a, known, preferred_element_type=F32)
    known = known.reshape(seqs, locals_, slots, known.shape[-1]).transpose(1, 0, 2, 3)
    self_id = (here * locals_ + jnp.arange(locals_)).astype(F32)[:, None, None]
    slot_blocks = known[..., 0].astype(jnp.int32)
    slot_place = known[..., 1] * 128.0 + known[..., 2]
    slot_other = known[..., 3] - self_id
    slot_gap = known[..., 5] + (known[..., 6] + known[..., 7])
    slot_gap = jnp.where(known[..., 4] == self_id, slot_gap, -slot_gap)
    gate_a = jax.nn.sigmoid(slot_gap)
    expert_f = expert_ids.astype(F32)
    pick_a = (expert_f == self_id[..., None]).astype(F32) - (expert_f == slot_other[..., None]).astype(F32)
    weigh_a = pick_a * (gate_a * jax.nn.sigmoid(-slot_gap))[..., None]
    cos_q, sin_q = angle_tables(slot_place)
    cos_k, sin_k = angle_tables(places)
    query_blocks = slot_blocks[..., None]
    key_blocks = block_ids[:, None, :]

    flat_low = normed_low.reshape(seqs * seq_len, width)
    own_adapter = (
        jnp.arange(NADAPT * RANK, dtype=jnp.int32)[None, :] // RANK == adapter_index[:, None]
    )
    low_rank = mm(flat_low, adapt_down).reshape(seqs, seq_len, NADAPT * RANK)
    low_rank = jnp.where(own_adapter[:, None, :], low_rank, 0.0).astype(BF16)
    key_value = make_key_value(
        flat_low, low_rank.reshape(seqs * seq_len, -1), kv_full, adapt_up, cos_k, sin_k, seqs
    ).reshape(seqs, seq_len, 2 * width)

    picked = jnp.einsum(
        "slrt,std->lsrd",
        spread_a.reshape(seqs, locals_, slots, seq_len),
        normed_low,
        preferred_element_type=F32,
    ).astype(BF16)
    queries = jnp.stack(
        [mm(picked[l].reshape(seqs * slots, width), query_full[l]).astype(BF16) for l in range(locals_)]
    ).reshape(locals_, seqs, slots, width)
    query_rot, attended, lse = attend(queries, key_value, cos_q, sin_q, query_blocks, key_blocks)
    projected = [
        mm(attended[l].reshape(seqs * slots, width), output_full[l]).reshape(seqs, slots, width)
        for l in range(locals_)
    ]
    order = np.arange(locals_ * slots).reshape(locals_, ranks, capacity).transpose(1, 0, 2).reshape(-1)
    to_send = jnp.asarray(np.eye(locals_ * slots)[order], BF16)
    to_slots = jnp.asarray(np.eye(locals_ * slots)[order].T, BF16)
    tokens = hidden_in.astype(F32)
    upstream = cotangent.astype(F32)
    middles = []
    for s in range(seqs):
        gated = jnp.concatenate(
            [(projected[l][s] * gate_a[l, s][:, None]).astype(BF16) for l in range(locals_)], axis=0
        )
        back = send(mm(to_send, gated).astype(BF16))
        middles.append(tokens[s] + mm(own_collect_a[s], back))
    projected_low = [p.astype(BF16) for p in projected]
    middle = jnp.stack(middles)
    scale_two = rms_scale(middle)
    normed_two_low = (middle * scale_two * mlp_gain).astype(BF16).reshape(seqs * row_count, width)

    final = middle.reshape(seqs * row_count, width)
    grad_normed_two = jnp.zeros((seqs * row_count, width), F32)
    mlp_back = []
    for l in range(locals_):
        rows_in = send(mm(own_spread_m[l], normed_two_low).astype(BF16))
        slot_logits = mm(rows_in, mlp_router)
        me = (here * locals_ + l).astype(F32)
        pick_m = (expert_f[None, :] == me).astype(F32) - (
            expert_f[None, :] == other_sum[l][0] - me
        ).astype(F32)
        gap_m = jnp.sum(pick_m * slot_logits, axis=-1, keepdims=True)
        gate_m = jax.nn.sigmoid(gap_m)
        cot = cot_rows[l].astype(F32)
        grad_rows = (gate_m * cot).astype(BF16)
        down_full, pieces = expert_weights[l]
        made = None
        for low, inner_full in pieces:
            made = expert_pass(rows_in, grad_rows, inner_full, down_full, low, made)
        expert_out, grad_source = made
        dots = jnp.sum(cot * expert_out, axis=-1, keepdims=True)
        weigh_m = pick_m * (dots * gate_m * jax.nn.sigmoid(-gap_m))
        grad_source = grad_source + jnp.dot(weigh_m, mlp_router.astype(F32).T, precision=PRECISE)
        grad_back = send(grad_source.astype(BF16))
        grad_normed_two = grad_normed_two + mm(own_collect_m[l], grad_back)
        mlp_back.append((gate_m * expert_out).astype(BF16))
    for l in range(locals_):
        final = final + mm(own_collect_m[l], send(mlp_back[l]))
    layer_out = final.astype(BF16).reshape(seqs, row_count, width)
    grad_normed_two = grad_normed_two.reshape(seqs, row_count, width)
    grad_middle = upstream + norm_back(middle, scale_two, mlp_gain, grad_normed_two)

    input_grads, down_pieces, up_pieces = [], [], []
    attn_router_f = attn_router.astype(F32)
    for s in range(seqs):
        arrived = send(mm(own_spread_a[s], grad_middle[s].astype(BF16)).astype(BF16))
        grad_rows = mm(to_slots, arrived).reshape(locals_, slots, width)
        grad_attended, extra = [], []
        for l in range(locals_):
            grad_projected = (grad_rows[l] * gate_a[l, s][:, None]).astype(BF16)
            grad_attended.append(mm(grad_projected, output_full[l], NT).astype(BF16))
            dots = jnp.sum(grad_rows[l] * projected_low[l][s].astype(F32), axis=-1, keepdims=True)
            extra.append(weigh_a[l, s] * dots)
        dq, dk, dv = attend_back(
            s, query_rot, key_value, jnp.stack(grad_attended), lse, cos_q, sin_q, query_blocks,
            key_blocks, cos_k, sin_k,
        )
        grad_source = jnp.concatenate(
            [
                (
                    mm(dq[l], query_full[l], NT) + jnp.dot(extra[l], attn_router_f.T, precision=PRECISE)
                ).astype(BF16)
                for l in range(locals_)
            ],
            axis=0,
        )
        grad_low = mm(dk, adapt_up[:width]) + mm(dv, adapt_up[width:])
        grad_low = jnp.where(own_adapter[s][None, :], grad_low, 0.0).astype(BF16)
        part = last_grad(dk, dv, kv_full, collect_a[s], grad_source, grad_low, adapt_down)
        grad_normed = lax.psum_scatter(part, "expert", scatter_dimension=0, tiled=True).astype(F32)
        input_grads.append(
            grad_middle[s] + norm_back(tokens[s], rms_scale(tokens[s]), attn_gain, grad_normed)
        )
        first = adapter_index[s] * RANK
        down_pieces.append(lax.dynamic_slice_in_dim(mm(grad_low, normed_low[s], TN), first, RANK, 0))
        up_piece = jnp.concatenate([mm(low_rank[s], dk, TN), mm(low_rank[s], dv, TN)], axis=1)
        up_pieces.append(lax.dynamic_slice_in_dim(up_piece, first, RANK, 0))

    groups = adapters.shape[0] // seqs
    down_part = width // (groups * ranks)
    pieces = jnp.concatenate(
        [
            jnp.stack(down_pieces).reshape(seqs, RANK, groups, ranks, down_part),
            jnp.stack(up_pieces).reshape(seqs, RANK, groups, ranks, 2 * down_part),
        ],
        axis=-1,
    )
    pieces = pieces.transpose(3, 2, 0, 1, 4).reshape(ranks, groups * seqs * RANK, 3 * down_part)
    pieces = jnp.sum(send(pieces), axis=0).reshape(groups, seqs * RANK, 3 * down_part)
    pieces = lax.all_to_all(pieces, "dp", split_axis=0, concat_axis=0, tiled=True)
    pieces = pieces.reshape(groups * seqs, RANK, 3 * down_part)
    belongs = (adapters[:, None] == jnp.arange(NADAPT, dtype=jnp.int32)[None, :]).astype(F32)
    sums = jnp.einsum("qkf,qa->fak", pieces, belongs, precision=PRECISE).reshape(3 * down_part, NADAPT * RANK)
    return (layer_out, jnp.stack(input_grads), sums[:down_part], sums[down_part:])


def solution(mesh):
    return jax.shard_map(
        per_device,
        mesh=mesh,
        in_specs=(
            P("dp", "expert", None),
            P("dp", "expert", None),
            P("dp", None),
            P("dp", "expert", None),
            P("dp", "expert", None),
            P("dp"),
            P(),
            P(),
            P(),
            P(),
            P("dp", None),
            P("expert", "dp", None),
            P("expert", "dp", None),
            P("expert", "dp", None),
            P("expert", "dp", None),
            P(),
            P(),
        ),
        out_specs=(
            P("dp", "expert", None),
            P("dp", "expert", None),
            P(("dp", "expert"), None),
            P(("dp", "expert"), None),
        ),
        check_vma=False,
    )
```

```python
import functools
import math

import jax
import jax.numpy as jnp
import numpy as np
from jax import lax
from jax.experimental import pallas as pl
from jax.experimental.pallas import tpu as pltpu
from jax.sharding import PartitionSpec as P

HEADS = 16
HDIM = 128
FF = 5632
EXPERTS = 8
TOP = 2
RANK = 16
NADAPT = 8

PRECISE = lax.Precision.HIGHEST
EPSILON = 1e-06
ROPE_BASE = 10000.0
MASKED_SCORE = -1e30
SCALE_QK = 1.0 / math.sqrt(HDIM)
BF16 = jnp.bfloat16
F32 = jnp.float32
VMEM_LIMIT = 58 * 1024 * 1024

NN = (((1,), (0,)), ((), ()))
NT = (((1,), (1,)), ((), ()))
TN = (((0,), (0,)), ((), ()))


def mm(left, right, dims=NN):
    return lax.dot_general(left, right, dims, preferred_element_type=F32)


def params(*semantics):
    return pltpu.CompilerParams(dimension_semantics=semantics, vmem_limit_bytes=VMEM_LIMIT)


def once(shape, index_map):
    return pl.BlockSpec(shape, index_map, pipeline_mode=pl.Buffered(1))


def rms_scale(values):
    return lax.rsqrt(jnp.mean(values * values, axis=-1, keepdims=True) + EPSILON)


def norm_back(values, scale_rows, norm_gain, grad_rows):
    scaled_grad = norm_gain * grad_rows
    return scale_rows * (
        scaled_grad
        - values * scale_rows * scale_rows * jnp.mean(scaled_grad * values, axis=-1, keepdims=True)
    )


def angle_tables(positions):
    half_dim = HDIM // 2
    frequency = ROPE_BASE ** (-(jnp.arange(half_dim, dtype=F32) * (2.0 / HDIM)))
    frequency = jnp.concatenate([frequency, frequency])
    sign = jnp.concatenate([-jnp.ones((half_dim,), F32), jnp.ones((half_dim,), F32)])
    angles = positions.astype(F32)[..., None] * frequency
    return (jnp.cos(angles), jnp.sin(angles) * sign)


def three_parts(values):
    first = values.astype(BF16)
    rest = values - first.astype(F32)
    second = rest.astype(BF16)
    third = (rest - second.astype(F32)).astype(BF16)
    return first, second, third


def gather_line(block, axis, size, put, start):
    here = lax.axis_index(axis)
    rightward = [(i, i + 1) for i in range(size - 1)]
    leftward = [(i + 1, i) for i in range(size - 1)]
    from_left, from_right = [block], [block]
    for _ in range(size - 1):
        from_left.append(lax.ppermute(from_left[-1], axis, rightward))
        from_right.append(lax.ppermute(from_right[-1], axis, leftward))
    total = put(start, block, here)
    for step in range(1, size):
        piece = jnp.where(here >= step, from_left[step], from_right[size - step])
        total = put(total, piece, lax.rem(here - step + size, size))
    return total


def send(buffer):
    return lax.all_to_all(buffer, "expert", split_axis=0, concat_axis=0, tiled=True)


def kv_body(seqs, seq_len, key_tiles, x_ref, low_ref, w_ref, up_ref, cos_ref, sin_ref, out_ref):
    is_key = pl.program_id(0) < key_tiles
    for s in range(seqs):
        rows = pl.ds(s * seq_len, seq_len)
        made = mm(x_ref[rows, :], w_ref[...]) + mm(low_ref[rows, :], up_ref[...], NT)

        @pl.when(is_key)
        def _(made=made, rows=rows):
            for h in range(made.shape[1] // HDIM):
                cols = slice(h * HDIM, (h + 1) * HDIM)
                part = made[:, cols]
                turned = part * cos_ref[...] + pltpu.roll(part, HDIM // 2, 1) * sin_ref[...]
                out_ref[rows, cols] = turned.astype(BF16)

        @pl.when(jnp.logical_not(is_key))
        def _(made=made, rows=rows):
            out_ref[rows, :] = made.astype(BF16)


def make_key_value(normed_low, low_rank, weights, adapt_up, cos_k, sin_k, seqs):
    rows, width = normed_low.shape
    seq_len = rows // seqs
    tile = 512
    return pl.pallas_call(
        functools.partial(kv_body, seqs, seq_len, width // tile),
        grid=(2 * width // tile,),
        in_specs=[
            once((rows, width), lambda i: (0, 0)),
            once((rows, low_rank.shape[1]), lambda i: (0, 0)),
            pl.BlockSpec((width, tile), lambda i: (0, i)),
            pl.BlockSpec((tile, low_rank.shape[1]), lambda i: (i, 0)),
            once((seq_len, HDIM), lambda i: (0, 0)),
            once((seq_len, HDIM), lambda i: (0, 0)),
        ],
        out_specs=pl.BlockSpec((rows, tile), lambda i: (0, i)),
        out_shape=jax.ShapeDtypeStruct((rows, 2 * width), BF16),
        compiler_params=params("arbitrary"),
        name="key_value",
    )(normed_low, low_rank, weights, adapt_up, cos_k, sin_k)


def project_body(x_ref, w_ref, *refs):
    made = mm(x_ref[...], w_ref[...])
    if len(refs) == 1:
        refs[0][...] = made.astype(BF16)
    else:
        gate_ref, out_ref, gated_ref = refs
        out_ref[...] = made.astype(BF16)
        gated_ref[...] = (made * gate_ref[...]).astype(BF16)


def project(values, weights, from_column, gate=None):
    locals_, rows, width = values.shape
    tile = 512
    first, step = from_column // tile, width // tile
    out_spec = pl.BlockSpec((None, rows, tile), lambda l, i: (l, 0, i))
    out_shape = jax.ShapeDtypeStruct(values.shape, BF16)
    in_specs = [
        pl.BlockSpec((None, rows, width), lambda l, i: (l, 0, 0)),
        pl.BlockSpec((width, tile), lambda l, i: (0, first + step * l + i)),
    ]
    more = []
    if gate is not None:
        in_specs.append(pl.BlockSpec((None, rows, 1), lambda l, i: (l, 0, 0)))
        more = [gate]
    return pl.pallas_call(
        project_body,
        grid=(locals_, step),
        in_specs=in_specs,
        out_specs=out_spec if gate is None else [out_spec] * 2,
        out_shape=out_shape if gate is None else [out_shape] * 2,
        compiler_params=params("arbitrary", "arbitrary"),
        name="project",
    )(values, weights, *more)


def attend_body(q_ref, k_ref, v_ref, cos_ref, sin_ref, qb_ref, kb_ref, rot_ref, out_ref, probs_ref):
    locals_, _, slots, _ = q_ref.shape
    rows = locals_ * slots
    q = q_ref[...].reshape(rows, HDIM).astype(F32)
    cos, sin = cos_ref[...].reshape(rows, HDIM), sin_ref[...].reshape(rows, HDIM)
    rot = (q * cos + pltpu.roll(q, HDIM // 2, 1) * sin).astype(BF16)
    rot_ref[...] = rot.reshape(rot_ref.shape)
    k, v = k_ref[0], v_ref[0]
    kb = kb_ref[0]
    for l in range(locals_):
        part = rot[l * slots : (l + 1) * slots]
        visible = kb <= qb_ref[l, 0]
        masked = jnp.where(visible, mm(part, k, NT), MASKED_SCORE)
        top = jnp.max(masked, axis=-1, keepdims=True)
        terms = jnp.exp((masked - top) * SCALE_QK)
        total = jnp.sum(terms, axis=-1, keepdims=True)
        probs = (terms * (1.0 / total)).astype(BF16)
        probs_ref[l, 0, 0] = probs
        out_ref[l, 0] = mm(probs, v).astype(BF16)


def attend(queries, key_value, cos_q, sin_q, query_blocks, key_blocks):
    locals_, seqs, slots, width = queries.shape
    seq_len = key_value.shape[1]
    q_spec = pl.BlockSpec((locals_, 1, slots, HDIM), lambda s, h: (0, s, 0, h))
    tab_spec = pl.BlockSpec((locals_, 1, slots, HDIM), lambda s, h: (0, s, 0, 0))
    return pl.pallas_call(
        attend_body,
        grid=(seqs, HEADS),
        in_specs=[
            q_spec,
            pl.BlockSpec((1, seq_len, HDIM), lambda s, h: (s, 0, h)),
            pl.BlockSpec((1, seq_len, HDIM), lambda s, h: (s, 0, HEADS + h)),
            tab_spec,
            tab_spec,
            pl.BlockSpec((locals_, 1, slots, 1), lambda s, h: (0, s, 0, 0)),
            pl.BlockSpec((1, 1, seq_len), lambda s, h: (s, 0, 0)),
        ],
        out_specs=[
            q_spec,
            q_spec,
            pl.BlockSpec((locals_, 1, 1, slots, seq_len), lambda s, h: (0, s, h, 0, 0)),
        ],
        out_shape=[
            jax.ShapeDtypeStruct(queries.shape, BF16),
            jax.ShapeDtypeStruct(queries.shape, BF16),
            jax.ShapeDtypeStruct((locals_, seqs, HEADS, slots, seq_len), BF16),
        ],
        compiler_params=params("arbitrary", "arbitrary"),
        name="attend",
    )(queries, key_value, key_value, cos_q, sin_q, query_blocks, key_blocks)


def attend_back_body(q_ref, k_ref, v_ref, g_ref, p_ref, cos_ref, sin_ref, ck_ref, sk_ref, dq_ref, dk_ref, dv_ref):
    locals_, _, slots, _ = q_ref.shape
    rows = locals_ * slots
    k, v = k_ref[0], v_ref[0]
    q = q_ref[...].reshape(rows, HDIM)
    grad = g_ref[...].reshape(rows, HDIM)
    probs = p_ref[...].reshape(rows, k.shape[0])
    weighed = probs.astype(F32) * mm(grad, v, NT)
    delta = jnp.sum(weighed, axis=-1, keepdims=True)
    grad_scores = (weighed - probs.astype(F32) * delta).astype(BF16)
    dq = mm(grad_scores, k) * SCALE_QK
    cos, sin = cos_ref[...].reshape(rows, HDIM), sin_ref[...].reshape(rows, HDIM)
    dq = dq * cos - pltpu.roll(dq, HDIM // 2, 1) * sin
    dq_ref[...] = dq.astype(BF16).reshape(dq_ref.shape)
    dk = mm(grad_scores, q, TN) * SCALE_QK
    dk_ref[...] = (dk * ck_ref[...] - pltpu.roll(dk, HDIM // 2, 1) * sk_ref[...]).astype(BF16)
    dv_ref[...] = mm(probs, grad, TN).astype(BF16)


def attend_back(s, query_rot, key_value, grad, probs, cos_q, sin_q, cos_k, sin_k):
    locals_, _, slots, width = query_rot.shape
    seq_len = key_value.shape[1]
    tab_spec = pl.BlockSpec((locals_, 1, slots, HDIM), lambda h: (0, s, 0, 0))
    key_tab = pl.BlockSpec((seq_len, HDIM), lambda h: (0, 0))
    grad_spec = pl.BlockSpec((locals_, slots, HDIM), lambda h: (0, 0, h))
    key_spec = pl.BlockSpec((seq_len, HDIM), lambda h: (0, h))
    return pl.pallas_call(
        attend_back_body,
        grid=(HEADS,),
        in_specs=[
            pl.BlockSpec((locals_, 1, slots, HDIM), lambda h: (0, s, 0, h)),
            pl.BlockSpec((1, seq_len, HDIM), lambda h: (s, 0, h)),
            pl.BlockSpec((1, seq_len, HDIM), lambda h: (s, 0, HEADS + h)),
            grad_spec,
            pl.BlockSpec((locals_, 1, 1, slots, seq_len), lambda h: (0, s, h, 0, 0)),
            tab_spec,
            tab_spec,
            key_tab,
            key_tab,
        ],
        out_specs=[grad_spec, key_spec, key_spec],
        out_shape=[
            jax.ShapeDtypeStruct((locals_, slots, width), BF16),
            jax.ShapeDtypeStruct((seq_len, width), BF16),
            jax.ShapeDtypeStruct((seq_len, width), BF16),
        ],
        compiler_params=params("arbitrary"),
        name="attend_back",
    )(query_rot, key_value, key_value, grad, probs, cos_q, sin_q, cos_k, sin_k)


def expert_body(has_start, is_last, x_ref, c_ref, wg_ref, wu_ref, wd_ref, *refs):
    refs = list(refs)
    start = [refs.pop(0), refs.pop(0)] if has_start else None
    if is_last:
        cot_ref, gate_ref, pick_ref, router_ref, low_ref, back_ref, out_ref, gs_ref = refs
    else:
        out_ref, gs_ref = refs

    @pl.when(pl.program_id(0) == 0)
    def _():
        if has_start:
            out_ref[...] = start[0][...]
            gs_ref[...] = start[1][...]
        else:
            out_ref[...] = jnp.zeros_like(out_ref)
            gs_ref[...] = jnp.zeros_like(gs_ref)

    x, c = x_ref[...], c_ref[...]
    wg, wu, wd = wg_ref[...], wu_ref[...], wd_ref[...]
    gate, up = mm(x, wg), mm(x, wu)
    sig = jax.nn.sigmoid(gate)
    silu = gate * sig
    out_ref[...] += mm((silu * up).astype(BF16), wd)
    grad = mm(c, wd, NT)
    grad_gate = (grad * up * sig * (1.0 + gate * (1.0 - sig))).astype(BF16)
    grad_up = (grad * silu).astype(BF16)
    gs_ref[...] += mm(grad_gate, wg, NT) + mm(grad_up, wu, NT)

    if is_last:

        @pl.when(pl.program_id(0) == pl.num_programs(0) - 1)
        def _():
            made = out_ref[...]
            share = gate_ref[...]
            dots = jnp.sum(cot_ref[...].astype(F32) * made, axis=-1, keepdims=True)
            weigh = pick_ref[...] * (dots * share * (1.0 - share))
            high = weigh.astype(BF16)
            low = (weigh - high.astype(F32)).astype(BF16)
            router = router_ref[...]
            back_ref[...] = (gs_ref[...] + mm(high, router, NT) + mm(low, router, NT)).astype(BF16)
            low_ref[...] = (share * made).astype(BF16)


def expert_pass(rows_in, grad_in, inner, down, l, down_from, start=None, last=None):
    rows, width = rows_in.shape
    units = inner.shape[1] // 2
    tile = 512 if units % 512 == 0 and down_from % 512 == 0 else 256
    first = down_from // tile

    def whole(array):
        return once(array.shape, lambda i: (0,) * array.ndim)

    more = ([] if start is None else list(start)) + ([] if last is None else list(last))
    kind = F32 if last is None else BF16
    return pl.pallas_call(
        functools.partial(expert_body, start is not None, last is not None),
        grid=(units // tile,),
        in_specs=[
            whole(rows_in),
            whole(grad_in),
            pl.BlockSpec((width, tile), lambda i: (0, i)),
            pl.BlockSpec((width, tile), lambda i: (0, units // tile + i)),
            pl.BlockSpec((None, tile, width), lambda i: (l, first + i, 0)),
        ]
        + [whole(m) for m in more],
        out_specs=[pl.BlockSpec((rows, width), lambda i: (0, 0))] * 2,
        out_shape=[jax.ShapeDtypeStruct((rows, width), kind)] * 2,
        scratch_shapes=[] if last is None else [pltpu.VMEM((rows, width), F32)] * 2,
        compiler_params=params("arbitrary"),
        name="expert",
    )(rows_in, grad_in, inner, inner, down, *more)


def out_back_body(locals_, arrived_ref, order_ref, gate_ref, projected_ref, *refs):
    w_refs, (out_ref, dots_ref, rows_ref) = refs[:locals_], refs[locals_:]
    slots = projected_ref.shape[1]

    @pl.when(pl.program_id(0) == 0)
    def _():
        for l in range(locals_):
            rows = mm(order_ref[pl.ds(l * slots, slots), :], arrived_ref[...])
            dots_ref[l] = jnp.sum(rows * projected_ref[l].astype(F32), axis=-1, keepdims=True)
            rows_ref[l] = (rows * gate_ref[l]).astype(BF16)

    for l in range(locals_):
        out_ref[l] = mm(rows_ref[l], w_refs[l][...], NT).astype(BF16)


def out_back(s, arrived, order, gate, projected, weights, from_column):
    locals_, slots = gate.shape[0], gate.shape[2]
    rows, width = arrived.shape
    tile = 512
    return pl.pallas_call(
        functools.partial(out_back_body, locals_),
        grid=(width // tile,),
        in_specs=[
            once((rows, width), lambda i: (0, 0)),
            once((rows, rows), lambda i: (0, 0)),
            once((locals_, None, slots, 1), lambda i: (0, s, 0, 0)),
            once((locals_, None, slots, width), lambda i: (0, s, 0, 0)),
        ]
        + [
            pl.BlockSpec((tile, width), lambda i, l=l: (i, from_column // width + l))
            for l in range(locals_)
        ],
        out_specs=[
            pl.BlockSpec((locals_, slots, tile), lambda i: (0, 0, i)),
            pl.BlockSpec((locals_, slots, 1), lambda i: (0, 0, 0)),
        ],
        out_shape=[
            jax.ShapeDtypeStruct((locals_, slots, width), BF16),
            jax.ShapeDtypeStruct((locals_, slots, 1), F32),
        ],
        scratch_shapes=[pltpu.VMEM((locals_, slots, width), BF16)],
        compiler_params=params("arbitrary"),
        name="out_back",
    )(arrived, order, gate, projected, *([weights] * locals_))


def last_body(
    locals_, seq_len, dk_ref, dv_ref, dq_ref, table_ref, dots_ref, weigh_ref, mask_ref, up_ref, router_ref, down_ref, w_ref, *refs
):
    wq_refs, (out_ref, low_ref) = refs[:locals_], refs[locals_:]
    width = dk_ref.shape[1]
    slots = dq_ref.shape[1]

    @pl.when(pl.program_id(0) == 0)
    def _():
        low = mm(dk_ref[...], up_ref[:width, :]) + mm(dv_ref[...], up_ref[width:, :])
        low_ref[...] = (low * mask_ref[...]).astype(BF16)

    total = mm(dk_ref[...], w_ref[:, :width], NT) + mm(dv_ref[...], w_ref[:, width:], NT)
    total += mm(low_ref[...], down_ref[...], NT)
    router = router_ref[...]
    for l in range(locals_):
        weigh = weigh_ref[l] * dots_ref[l]
        high = weigh.astype(BF16)
        low = (weigh - high.astype(F32)).astype(BF16)
        source = mm(dq_ref[l], wq_refs[l][...], NT) + mm(high, router, NT) + mm(low, router, NT)
        total += mm(table_ref[0, :, pl.ds(l * slots, slots)], source.astype(BF16))
    out_ref[...] = total.astype(BF16)


def last_grad(s, dk, dv, dq, table, dots, weigh, mask, adapt_up, router, adapt_down, weights, query_column):
    seq_len, width = dk.shape
    locals_, slots, _ = dq.shape
    tile = 256
    ranks = adapt_up.shape[1]
    return pl.pallas_call(
        functools.partial(last_body, locals_, seq_len),
        grid=(width // tile,),
        in_specs=[
            once((seq_len, width), lambda i: (0, 0)),
            once((seq_len, width), lambda i: (0, 0)),
            once((locals_, slots, width), lambda i: (0, 0, 0)),
            once((1, seq_len, locals_ * slots), lambda i: (s, 0, 0)),
            once((locals_, slots, 1), lambda i: (0, 0, 0)),
            once((locals_, None, slots, EXPERTS), lambda i: (0, s, 0, 0)),
            once((None, 1, ranks), lambda i: (s, 0, 0)),
            once((2 * width, ranks), lambda i: (0, 0)),
            pl.BlockSpec((tile, EXPERTS), lambda i: (i, 0)),
            pl.BlockSpec((tile, ranks), lambda i: (i, 0)),
            pl.BlockSpec((tile, 2 * width), lambda i: (i, 0)),
        ]
        + [
            pl.BlockSpec((tile, width), lambda i, l=l: (i, query_column // width + l))
            for l in range(locals_)
        ],
        out_specs=[
            pl.BlockSpec((seq_len, tile), lambda i: (0, i)),
            pl.BlockSpec((seq_len, ranks), lambda i: (0, 0)),
        ],
        out_shape=[
            jax.ShapeDtypeStruct((seq_len, width), BF16),
            jax.ShapeDtypeStruct((seq_len, ranks), BF16),
        ],
        compiler_params=params("arbitrary"),
        name="last_grad",
    )(dk, dv, dq, table, dots, weigh, mask, adapt_up, router, adapt_down, weights, *([weights] * locals_))


def per_device(
    hidden_in,
    cotangent,
    block_ids,
    attn_routes,
    mlp_routes,
    adapter_index,
    attn_gain,
    mlp_gain,
    attn_router,
    mlp_router,
    kv_weight,
    query_weight,
    output_weight,
    inner_weight,
    down_weight,
    adapt_down,
    adapt_up,
):
    seqs, row_count, width = hidden_in.shape
    seq_len = block_ids.shape[1]
    ranks = seq_len // row_count
    locals_ = query_weight.shape[0]
    capacity = (17 * row_count * TOP + 16 * EXPERTS - 1) // (16 * EXPERTS)
    slots = ranks * capacity
    here = lax.axis_index("expert")

    query_column = 2 * width
    output_column = query_column + locals_ * width
    near = jnp.concatenate(
        [kv_weight]
        + [query_weight[l] for l in range(locals_)]
        + [output_weight[l] for l in range(locals_)],
        axis=1,
    )
    near_full = lax.all_gather(near, "dp", axis=0, tiled=True)
    down_full = lax.all_gather(down_weight, "dp", axis=1, tiled=True)
    cut = (FF * 3 // 4) // 512 * 512
    inner_full = []
    for l in range(locals_):
        if l + 1 < locals_:
            pieces = [(0, lax.all_gather(inner_weight[l], "dp", axis=0, tiled=True))]
        else:
            pieces = []
            for low, high in ((0, cut), (cut, FF)):
                part = jnp.concatenate(
                    [inner_weight[l, :, low:high], inner_weight[l, :, FF + low : FF + high]], axis=1
                )
                pieces.append((low, lax.all_gather(part, "dp", axis=0, tiled=True)))
        inner_full.append(pieces)

    routes = lax.all_gather(
        jnp.concatenate([attn_routes, mlp_routes], axis=-1), "expert", axis=1, tiled=True
    ).reshape(seqs, ranks, row_count, 2, TOP)
    adapters = lax.all_gather(adapter_index, "dp", axis=0, tiled=True)
    expert_ids = jnp.arange(EXPERTS, dtype=jnp.int32)
    onehot = (routes[..., None] == expert_ids).astype(F32)
    hits = jnp.sum(onehot, axis=4)
    earlier = (
        jnp.arange(row_count)[:, None] > jnp.arange(row_count)[None, :]
    ).astype(BF16)
    before = jnp.einsum("ut,sptke->spuke", earlier, hits.astype(BF16), preferred_element_type=F32)
    place = jnp.sum(onehot * before[..., None, :], axis=-1).astype(jnp.int32)
    attn_all, mlp_all = routes[:, :, :, 0], routes[:, :, :, 1]
    attn_place, mlp_place = place[:, :, :, 0], place[:, :, :, 1]
    source = jnp.arange(ranks, dtype=jnp.int32)[None, :, None, None]
    which = jnp.arange(seqs, dtype=jnp.int32)[:, None, None, None]

    local_a = attn_all - here * locals_
    is_local = (local_a >= 0) & (local_a < locals_)
    slot_a = jnp.where(is_local, local_a * slots + source * capacity + attn_place, -1)
    slot_a = slot_a.reshape(seqs, seq_len, TOP)
    slot_iota = jnp.arange(locals_ * slots, dtype=jnp.int32)
    spread_a = (
        (slot_iota[None, :, None] == slot_a[:, None, :, 0])
        | (slot_iota[None, :, None] == slot_a[:, None, :, 1])
    ).astype(BF16)
    collect_a = (
        (slot_iota[None, None, :] == slot_a[:, :, 0, None])
        | (slot_iota[None, None, :] == slot_a[:, :, 1, None])
    ).astype(BF16)

    def own(array):
        return lax.dynamic_index_in_dim(array, here, 1, keepdims=False)

    attn_own, attn_own_place = own(attn_all), own(attn_place)
    mlp_own, mlp_own_place = own(mlp_all), own(mlp_place)
    own_slot = attn_own * capacity + attn_own_place
    own_iota = jnp.arange(EXPERTS * capacity, dtype=jnp.int32)
    own_spread_a = (
        (own_iota[None, :, None] == own_slot[:, None, :, 0])
        | (own_iota[None, :, None] == own_slot[:, None, :, 1])
    ).astype(BF16)
    own_collect_a = (
        (own_iota[None, None, :] == own_slot[:, :, 0, None])
        | (own_iota[None, None, :] == own_slot[:, :, 1, None])
    ).astype(BF16)
    mlp_rows = ranks * seqs * capacity
    mlp_iota = jnp.arange(mlp_rows, dtype=jnp.int32)
    own_spread_m, own_collect_m, other_sum = [], [], []
    for l in range(locals_):
        ids = jnp.where(
            mlp_own % locals_ == l,
            (mlp_own // locals_) * (seqs * capacity) + which[:, 0] * capacity + mlp_own_place,
            -1,
        ).reshape(seqs * row_count, TOP)
        own_spread_m.append(
            ((mlp_iota[:, None] == ids[None, :, 0]) | (mlp_iota[:, None] == ids[None, :, 1])).astype(BF16)
        )
        own_collect_m.append(
            ((mlp_iota[None, :] == ids[:, 0, None]) | (mlp_iota[None, :] == ids[:, 1, None])).astype(BF16)
        )
        ids = jnp.where(
            mlp_all == here * locals_ + l,
            source * (seqs * capacity) + which * capacity + mlp_place,
            -1,
        ).reshape(seqs * seq_len, TOP)
        table = (
            (mlp_iota[:, None] == ids[None, :, 0]) | (mlp_iota[:, None] == ids[None, :, 1])
        ).astype(BF16)
        both = jnp.sum(mlp_all, axis=-1).reshape(seqs * seq_len, 1).astype(BF16)
        sums = mm(table, jnp.concatenate([both, jnp.ones_like(both)], axis=1))
        other_sum.append((sums[:, :1], sums[:, 1:]))

    hidden_first, routes = lax.optimization_barrier((hidden_in, routes))
    everyone = gather_line(
        hidden_first,
        "expert",
        ranks,
        lambda total, piece, at: lax.dynamic_update_slice(total, piece[:, None], (0, at, 0, 0)),
        jnp.zeros((seqs, ranks, row_count, width), BF16),
    ).reshape(seqs, seq_len, width)

    flat_cot, everyone = lax.optimization_barrier((cotangent, everyone))
    flat_cot = flat_cot.reshape(seqs * row_count, width)
    cot_rows = [send(mm(own_spread_m[l], flat_cot).astype(BF16)) for l in range(locals_)]

    tokens_all = everyone.astype(F32)
    scale_all = rms_scale(tokens_all)
    normed_low = (tokens_all * scale_all * attn_gain).astype(BF16)
    router_parts = jnp.concatenate(three_parts(attn_gain[:, None] * attn_router.astype(F32)), axis=1)
    parts = mm(everyone.reshape(seqs * seq_len, width), router_parts).reshape(seqs, seq_len, 3, EXPERTS)
    logits = scale_all * (parts[:, :, 0] + (parts[:, :, 1] + parts[:, :, 2]))
    onehot_a = onehot[:, :, :, 0].reshape(seqs, seq_len, TOP, EXPERTS)
    gap = jnp.sum((onehot_a[:, :, 0] - onehot_a[:, :, 1]) * logits, axis=-1)

    flat_routes = attn_all.reshape(seqs, seq_len, TOP)
    places = jnp.arange(seq_len, dtype=jnp.int32)
    columns = [
        block_ids,
        jnp.broadcast_to(places // 128, block_ids.shape),
        jnp.broadcast_to(places % 128, block_ids.shape),
        jnp.sum(flat_routes, axis=-1),
        flat_routes[..., 0],
    ]
    known = jnp.stack([c.astype(BF16) for c in columns] + list(three_parts(gap)), axis=-1)
    known = jnp.einsum("srt,stc->src", spread_a, known, preferred_element_type=F32)
    known = known.reshape(seqs, locals_, slots, known.shape[-1]).transpose(1, 0, 2, 3)
    self_id = (here * locals_ + jnp.arange(locals_)).astype(F32)[:, None, None]
    slot_blocks = known[..., 0].astype(jnp.int32)
    slot_place = known[..., 1] * 128.0 + known[..., 2]
    slot_other = known[..., 3] - self_id
    slot_gap = known[..., 5] + (known[..., 6] + known[..., 7])
    slot_gap = jnp.where(known[..., 4] == self_id, slot_gap, -slot_gap)
    gate_a = jax.nn.sigmoid(slot_gap)
    expert_f = expert_ids.astype(F32)
    pick_a = (expert_f == self_id[..., None]).astype(F32) - (expert_f == slot_other[..., None]).astype(F32)
    weigh_a = pick_a * (gate_a * jax.nn.sigmoid(-slot_gap))[..., None]
    cos_q, sin_q = angle_tables(slot_place)
    cos_k, sin_k = angle_tables(places)
    query_blocks = slot_blocks[..., None]
    key_blocks = block_ids[:, None, :]

    flat_low = normed_low.reshape(seqs * seq_len, width)
    own_adapter = (
        jnp.arange(NADAPT * RANK, dtype=jnp.int32)[None, :] // RANK == adapter_index[:, None]
    )
    low_rank = mm(flat_low, adapt_down).reshape(seqs, seq_len, NADAPT * RANK)
    low_rank = jnp.where(own_adapter[:, None, :], low_rank, 0.0).astype(BF16)
    key_value = make_key_value(
        flat_low, low_rank.reshape(seqs * seq_len, -1), near_full, adapt_up, cos_k, sin_k, seqs
    ).reshape(seqs, seq_len, 2 * width)

    picked = jnp.einsum(
        "slrt,std->lsrd",
        spread_a.reshape(seqs, locals_, slots, seq_len),
        normed_low,
        preferred_element_type=F32,
    ).astype(BF16)
    queries = project(picked.reshape(locals_, seqs * slots, width), near_full, query_column)
    query_rot, attended, probs = attend(
        queries.reshape(locals_, seqs, slots, width), key_value, cos_q, sin_q, query_blocks, key_blocks
    )
    gate_rows = gate_a[..., None]
    projected, gated = project(
        attended.reshape(locals_, seqs * slots, width),
        near_full,
        output_column,
        gate_rows.reshape(locals_, seqs * slots, 1),
    )
    projected = projected.reshape(locals_, seqs, slots, width)
    gated = gated.reshape(locals_, seqs, slots, width)
    order = np.arange(locals_ * slots).reshape(locals_, ranks, capacity).transpose(1, 0, 2).reshape(-1)
    to_send = jnp.asarray(np.eye(locals_ * slots)[order], BF16)
    to_slots = jnp.asarray(np.eye(locals_ * slots)[order].T, BF16)
    tokens = hidden_in.astype(F32)
    upstream = cotangent.astype(F32)
    middles = []
    for s in range(seqs):
        back = send(mm(to_send, gated[:, s].reshape(locals_ * slots, width)).astype(BF16))
        middles.append(tokens[s] + mm(own_collect_a[s], back))
    middle = jnp.stack(middles)
    scale_two = rms_scale(middle)
    normed_two_low = (middle * scale_two * mlp_gain).astype(BF16).reshape(seqs * row_count, width)

    final = middle.reshape(seqs * row_count, width)
    grad_normed_two = jnp.zeros((seqs * row_count, width), F32)
    held = None
    for l in range(locals_):
        rows_in = send(mm(own_spread_m[l], normed_two_low).astype(BF16))
        slot_logits = mm(rows_in, mlp_router)
        me = (here * locals_ + l).astype(F32)
        pick_m = (expert_f[None, :] == me).astype(F32) - (
            expert_f[None, :] == other_sum[l][0] - me
        ).astype(F32)
        gate_m = jax.nn.sigmoid(jnp.sum(pick_m * slot_logits, axis=-1, keepdims=True))
        grad_rows = (gate_m * cot_rows[l].astype(F32)).astype(BF16)
        made = None
        for at, (low, inner) in enumerate(inner_full[l]):
            ends = (cot_rows[l], gate_m, pick_m, mlp_router) if at + 1 == len(inner_full[l]) else None
            made = expert_pass(rows_in, grad_rows, inner, down_full, l, low, made, ends)
        gated_out, grad_source = made
        if held is not None:
            final = final + mm(own_collect_m[l - 1], held)
            grad_source, final = lax.optimization_barrier((grad_source, final))
        grad_back = send(grad_source)
        grad_normed_two = grad_normed_two + mm(own_collect_m[l], grad_back)
        held = send(gated_out) if l + 1 < locals_ else gated_out
    grad_normed_two = grad_normed_two.reshape(seqs, row_count, width)
    grad_middle = upstream + norm_back(middle, scale_two, mlp_gain, grad_normed_two)

    arrived = [send(mm(own_spread_a[s], grad_middle[s].astype(BF16)).astype(BF16)) for s in range(seqs)]
    input_grads, down_pieces, up_pieces = [], [], []
    mask = own_adapter.astype(F32)[:, None, :]
    for s in range(seqs):
        grad_attended, dots = out_back(
            s, arrived[s], to_slots, gate_rows, projected, near_full, output_column
        )
        dq, dk, dv = attend_back(s, query_rot, key_value, grad_attended, probs, cos_q, sin_q, cos_k, sin_k)
        part, grad_low = last_grad(
            s, dk, dv, dq, collect_a, dots, weigh_a, mask, adapt_up, attn_router, adapt_down, near_full,
            query_column,
        )
        if s + 1 < seqs:
            part, arrived[s + 1] = lax.optimization_barrier((part, arrived[s + 1]))
        if s + 2 == seqs:
            held, part = lax.optimization_barrier((held, part))
        grad_normed = lax.psum_scatter(part, "expert", scatter_dimension=0, tiled=True).astype(F32)
        input_grads.append(
            grad_middle[s] + norm_back(tokens[s], rms_scale(tokens[s]), attn_gain, grad_normed)
        )
        first = adapter_index[s] * RANK
        down_pieces.append(lax.dynamic_slice_in_dim(mm(grad_low, normed_low[s], TN), first, RANK, 0))
        up_piece = jnp.concatenate([mm(low_rank[s], dk, TN), mm(low_rank[s], dv, TN)], axis=1)
        up_pieces.append(lax.dynamic_slice_in_dim(up_piece, first, RANK, 0))
    final = final + mm(own_collect_m[locals_ - 1], send(held))
    layer_out = final.astype(BF16).reshape(seqs, row_count, width)

    groups = adapters.shape[0] // seqs
    down_part = width // (groups * ranks)
    pieces = jnp.concatenate(
        [
            jnp.stack(down_pieces).reshape(seqs, RANK, groups, ranks, down_part),
            jnp.stack(up_pieces).reshape(seqs, RANK, groups, ranks, 2 * down_part),
        ],
        axis=-1,
    )
    pieces = pieces.transpose(3, 2, 0, 1, 4).reshape(ranks, groups * seqs * RANK, 3 * down_part)
    pieces = jnp.sum(send(pieces), axis=0).reshape(groups, seqs * RANK, 3 * down_part)
    pieces = lax.all_to_all(pieces, "dp", split_axis=0, concat_axis=0, tiled=True)
    pieces = pieces.reshape(groups * seqs, RANK, 3 * down_part)
    belongs = (adapters[:, None] == jnp.arange(NADAPT, dtype=jnp.int32)[None, :]).astype(F32)
    sums = jnp.einsum("qkf,qa->fak", pieces, belongs, precision=PRECISE).reshape(3 * down_part, NADAPT * RANK)
    return (layer_out, jnp.stack(input_grads), sums[:down_part], sums[down_part:])


def solution(mesh):
    return jax.shard_map(
        per_device,
        mesh=mesh,
        in_specs=(
            P("dp", "expert", None),
            P("dp", "expert", None),
            P("dp", None),
            P("dp", "expert", None),
            P("dp", "expert", None),
            P("dp"),
            P(),
            P(),
            P(),
            P(),
            P("dp", None),
            P("expert", "dp", None),
            P("expert", "dp", None),
            P("expert", "dp", None),
            P("expert", "dp", None),
            P(),
            P(),
        ),
        out_specs=(
            P("dp", "expert", None),
            P("dp", "expert", None),
            P(("dp", "expert"), None),
            P(("dp", "expert"), None),
        ),
        check_vma=False,
    )
```

```python
import functools
import math

import jax
import jax.numpy as jnp
import numpy as np
from jax import lax
from jax.experimental import pallas as pl
from jax.experimental.pallas import tpu as pltpu
from jax.sharding import PartitionSpec as P

HEADS = 16
HDIM = 128
FF = 5632
EXPERTS = 8
TOP = 2
RANK = 16
NADAPT = 8

PRECISE = lax.Precision.HIGHEST
EPSILON = 1e-06
ROPE_BASE = 10000.0
MASKED_SCORE = -1e30
SCALE_QK = 1.0 / math.sqrt(HDIM)
BF16 = jnp.bfloat16
F32 = jnp.float32
VMEM_LIMIT = 58 * 1024 * 1024

NN = (((1,), (0,)), ((), ()))
NT = (((1,), (1,)), ((), ()))
TN = (((0,), (0,)), ((), ()))


def mm(left, right, dims=NN):
    return lax.dot_general(left, right, dims, preferred_element_type=F32)


def params(*semantics):
    return pltpu.CompilerParams(dimension_semantics=semantics, vmem_limit_bytes=VMEM_LIMIT)


def once(shape, index_map):
    return pl.BlockSpec(shape, index_map, pipeline_mode=pl.Buffered(1))


def rms_scale(values):
    return lax.rsqrt(jnp.mean(values * values, axis=-1, keepdims=True) + EPSILON)


def norm_back(values, scale_rows, norm_gain, grad_rows):
    scaled_grad = norm_gain * grad_rows
    return scale_rows * (
        scaled_grad
        - values * scale_rows * scale_rows * jnp.mean(scaled_grad * values, axis=-1, keepdims=True)
    )


def angle_tables(positions):
    half_dim = HDIM // 2
    frequency = ROPE_BASE ** (-(jnp.arange(half_dim, dtype=F32) * (2.0 / HDIM)))
    frequency = jnp.concatenate([frequency, frequency])
    sign = jnp.concatenate([-jnp.ones((half_dim,), F32), jnp.ones((half_dim,), F32)])
    angles = positions.astype(F32)[..., None] * frequency
    return (jnp.cos(angles), jnp.sin(angles) * sign)


def three_parts(values):
    first = values.astype(BF16)
    rest = values - first.astype(F32)
    second = rest.astype(BF16)
    third = (rest - second.astype(F32)).astype(BF16)
    return first, second, third


def gather_line(block, axis, size, put, start):
    here = lax.axis_index(axis)
    rightward = [(i, i + 1) for i in range(size - 1)]
    leftward = [(i + 1, i) for i in range(size - 1)]
    from_left, from_right = [block], [block]
    for _ in range(size - 1):
        from_left.append(lax.ppermute(from_left[-1], axis, rightward))
        from_right.append(lax.ppermute(from_right[-1], axis, leftward))
    total = put(start, block, here)
    for step in range(1, size):
        piece = jnp.where(here >= step, from_left[step], from_right[size - step])
        total = put(total, piece, lax.rem(here - step + size, size))
    return total


def exchange(total, axis, size, bit):
    other = lax.ppermute(total, axis, [(i, i ^ bit) for i in range(size)])
    low = jnp.bitwise_and(lax.axis_index(axis), bit) == 0
    return jnp.stack([jnp.where(low, total, other), jnp.where(low, other, total)])


def halves_bits(size):
    bits = [1 << k for k in range(1, size.bit_length() - 1)]
    return [bits + [1], bits[::-1] + [1]]


def in_order(halves, orders, size):
    made = []
    for total, bits in zip(halves, orders):
        count = len(bits)
        order = sorted(range(count), key=lambda d: -bits[count - 1 - d])
        total = total.transpose(*order, *range(count, total.ndim))
        made.append(total.reshape(size, *total.shape[count:]))
    whole = jnp.stack(made, axis=1)
    return whole.reshape(-1, whole.shape[-1])


def send(buffer):
    return lax.all_to_all(buffer, "expert", split_axis=0, concat_axis=0, tiled=True)


def kv_body(seqs, seq_len, key_tiles, x_ref, low_ref, w_ref, up_ref, cos_ref, sin_ref, out_ref):
    is_key = pl.program_id(0) < key_tiles
    for s in range(seqs):
        rows = pl.ds(s * seq_len, seq_len)
        made = mm(x_ref[rows, :], w_ref[...]) + mm(low_ref[rows, :], up_ref[...], NT)

        @pl.when(is_key)
        def _(made=made, rows=rows):
            for h in range(made.shape[1] // HDIM):
                cols = slice(h * HDIM, (h + 1) * HDIM)
                part = made[:, cols]
                turned = part * cos_ref[...] + pltpu.roll(part, HDIM // 2, 1) * sin_ref[...]
                out_ref[rows, cols] = turned.astype(BF16)

        @pl.when(jnp.logical_not(is_key))
        def _(made=made, rows=rows):
            out_ref[rows, :] = made.astype(BF16)


def make_key_value(normed_low, low_rank, weights, adapt_up, cos_k, sin_k, seqs):
    rows, width = normed_low.shape
    seq_len = rows // seqs
    tile = 512
    return pl.pallas_call(
        functools.partial(kv_body, seqs, seq_len, width // tile),
        grid=(2 * width // tile,),
        in_specs=[
            once((rows, width), lambda i: (0, 0)),
            once((rows, low_rank.shape[1]), lambda i: (0, 0)),
            pl.BlockSpec((width, tile), lambda i: (0, i)),
            pl.BlockSpec((tile, low_rank.shape[1]), lambda i: (i, 0)),
            once((seq_len, HDIM), lambda i: (0, 0)),
            once((seq_len, HDIM), lambda i: (0, 0)),
        ],
        out_specs=pl.BlockSpec((rows, tile), lambda i: (0, i)),
        out_shape=jax.ShapeDtypeStruct((rows, 2 * width), BF16),
        compiler_params=params("arbitrary"),
        name="key_value",
    )(normed_low, low_rank, weights, adapt_up, cos_k, sin_k)


def project_body(x_ref, w_ref, *refs):
    made = mm(x_ref[...], w_ref[...])
    if len(refs) == 1:
        refs[0][...] = made.astype(BF16)
    else:
        gate_ref, out_ref, gated_ref = refs
        out_ref[...] = made.astype(BF16)
        gated_ref[...] = (made * gate_ref[...]).astype(BF16)


def project(values, weights, from_column, gate=None):
    locals_, rows, width = values.shape
    tile = 512
    first, step = from_column // tile, width // tile
    out_spec = pl.BlockSpec((None, rows, tile), lambda l, i: (l, 0, i))
    out_shape = jax.ShapeDtypeStruct(values.shape, BF16)
    in_specs = [
        pl.BlockSpec((None, rows, width), lambda l, i: (l, 0, 0)),
        pl.BlockSpec((width, tile), lambda l, i: (0, first + step * l + i)),
    ]
    more = []
    if gate is not None:
        in_specs.append(pl.BlockSpec((None, rows, 1), lambda l, i: (l, 0, 0)))
        more = [gate]
    return pl.pallas_call(
        project_body,
        grid=(locals_, step),
        in_specs=in_specs,
        out_specs=out_spec if gate is None else [out_spec] * 2,
        out_shape=out_shape if gate is None else [out_shape] * 2,
        compiler_params=params("arbitrary", "arbitrary"),
        name="project",
    )(values, weights, *more)


def attend_body(q_ref, k_ref, v_ref, cos_ref, sin_ref, qb_ref, kb_ref, rot_ref, out_ref, probs_ref):
    locals_, _, slots, _ = q_ref.shape
    rows = locals_ * slots
    q = q_ref[...].reshape(rows, HDIM).astype(F32)
    cos, sin = cos_ref[...].reshape(rows, HDIM), sin_ref[...].reshape(rows, HDIM)
    rot = (q * cos + pltpu.roll(q, HDIM // 2, 1) * sin).astype(BF16)
    rot_ref[...] = rot.reshape(rot_ref.shape)
    k, v = k_ref[0], v_ref[0]
    kb = kb_ref[0]
    for l in range(locals_):
        part = rot[l * slots : (l + 1) * slots]
        visible = kb <= qb_ref[l, 0]
        masked = jnp.where(visible, mm(part, k, NT), MASKED_SCORE)
        top = jnp.max(masked, axis=-1, keepdims=True)
        terms = jnp.exp((masked - top) * SCALE_QK)
        total = jnp.sum(terms, axis=-1, keepdims=True)
        probs = (terms * (1.0 / total)).astype(BF16)
        probs_ref[l, 0, 0] = probs
        out_ref[l, 0] = mm(probs, v).astype(BF16)


def attend(queries, key_value, cos_q, sin_q, query_blocks, key_blocks):
    locals_, seqs, slots, width = queries.shape
    seq_len = key_value.shape[1]
    q_spec = pl.BlockSpec((locals_, 1, slots, HDIM), lambda s, h: (0, s, 0, h))
    tab_spec = pl.BlockSpec((locals_, 1, slots, HDIM), lambda s, h: (0, s, 0, 0))
    return pl.pallas_call(
        attend_body,
        grid=(seqs, HEADS),
        in_specs=[
            q_spec,
            pl.BlockSpec((1, seq_len, HDIM), lambda s, h: (s, 0, h)),
            pl.BlockSpec((1, seq_len, HDIM), lambda s, h: (s, 0, HEADS + h)),
            tab_spec,
            tab_spec,
            pl.BlockSpec((locals_, 1, slots, 1), lambda s, h: (0, s, 0, 0)),
            pl.BlockSpec((1, 1, seq_len), lambda s, h: (s, 0, 0)),
        ],
        out_specs=[
            q_spec,
            q_spec,
            pl.BlockSpec((locals_, 1, 1, slots, seq_len), lambda s, h: (0, s, h, 0, 0)),
        ],
        out_shape=[
            jax.ShapeDtypeStruct(queries.shape, BF16),
            jax.ShapeDtypeStruct(queries.shape, BF16),
            jax.ShapeDtypeStruct((locals_, seqs, HEADS, slots, seq_len), BF16),
        ],
        compiler_params=params("arbitrary", "arbitrary"),
        name="attend",
    )(queries, key_value, key_value, cos_q, sin_q, query_blocks, key_blocks)


def attend_back_body(q_ref, k_ref, v_ref, g_ref, p_ref, cos_ref, sin_ref, ck_ref, sk_ref, dq_ref, dk_ref, dv_ref):
    locals_, _, slots, _ = q_ref.shape
    rows = locals_ * slots
    k, v = k_ref[0], v_ref[0]
    q = q_ref[...].reshape(rows, HDIM)
    grad = g_ref[...].reshape(rows, HDIM)
    probs = p_ref[...].reshape(rows, k.shape[0])
    weighed = probs.astype(F32) * mm(grad, v, NT)
    delta = jnp.sum(weighed, axis=-1, keepdims=True)
    grad_scores = (weighed - probs.astype(F32) * delta).astype(BF16)
    dq = mm(grad_scores, k) * SCALE_QK
    cos, sin = cos_ref[...].reshape(rows, HDIM), sin_ref[...].reshape(rows, HDIM)
    dq = dq * cos - pltpu.roll(dq, HDIM // 2, 1) * sin
    dq_ref[...] = dq.astype(BF16).reshape(dq_ref.shape)
    dk = mm(grad_scores, q, TN) * SCALE_QK
    dk_ref[...] = (dk * ck_ref[...] - pltpu.roll(dk, HDIM // 2, 1) * sk_ref[...]).astype(BF16)
    dv_ref[...] = mm(probs, grad, TN).astype(BF16)


def attend_back(s, query_rot, key_value, grad, probs, cos_q, sin_q, cos_k, sin_k):
    locals_, _, slots, width = query_rot.shape
    seq_len = key_value.shape[1]
    tab_spec = pl.BlockSpec((locals_, 1, slots, HDIM), lambda h: (0, s, 0, 0))
    key_tab = pl.BlockSpec((seq_len, HDIM), lambda h: (0, 0))
    grad_spec = pl.BlockSpec((locals_, slots, HDIM), lambda h: (0, 0, h))
    key_spec = pl.BlockSpec((seq_len, HDIM), lambda h: (0, h))
    return pl.pallas_call(
        attend_back_body,
        grid=(HEADS,),
        in_specs=[
            pl.BlockSpec((locals_, 1, slots, HDIM), lambda h: (0, s, 0, h)),
            pl.BlockSpec((1, seq_len, HDIM), lambda h: (s, 0, h)),
            pl.BlockSpec((1, seq_len, HDIM), lambda h: (s, 0, HEADS + h)),
            grad_spec,
            pl.BlockSpec((locals_, 1, 1, slots, seq_len), lambda h: (0, s, h, 0, 0)),
            tab_spec,
            tab_spec,
            key_tab,
            key_tab,
        ],
        out_specs=[grad_spec, key_spec, key_spec],
        out_shape=[
            jax.ShapeDtypeStruct((locals_, slots, width), BF16),
            jax.ShapeDtypeStruct((seq_len, width), BF16),
            jax.ShapeDtypeStruct((seq_len, width), BF16),
        ],
        compiler_params=params("arbitrary"),
        name="attend_back",
    )(query_rot, key_value, key_value, grad, probs, cos_q, sin_q, cos_k, sin_k)


def expert_body(has_start, is_last, x_ref, c_ref, wg_ref, wu_ref, wd_ref, *refs):
    refs = list(refs)
    start = [refs.pop(0), refs.pop(0)] if has_start else None
    if is_last:
        cot_ref, gate_ref, pick_ref, router_ref, low_ref, back_ref, out_ref, gs_ref = refs
    else:
        out_ref, gs_ref = refs

    @pl.when(pl.program_id(0) == 0)
    def _():
        if has_start:
            out_ref[...] = start[0][...]
            gs_ref[...] = start[1][...]
        else:
            out_ref[...] = jnp.zeros_like(out_ref)
            gs_ref[...] = jnp.zeros_like(gs_ref)

    x, c = x_ref[...], c_ref[...]
    wg, wu, wd = wg_ref[...], wu_ref[...], wd_ref[...]
    gate, up = mm(x, wg), mm(x, wu)
    sig = jax.nn.sigmoid(gate)
    silu = gate * sig
    out_ref[...] += mm((silu * up).astype(BF16), wd)
    grad = mm(c, wd, NT)
    grad_gate = (grad * up * sig * (1.0 + gate * (1.0 - sig))).astype(BF16)
    grad_up = (grad * silu).astype(BF16)
    gs_ref[...] += mm(grad_gate, wg, NT) + mm(grad_up, wu, NT)

    if is_last:

        @pl.when(pl.program_id(0) == pl.num_programs(0) - 1)
        def _():
            made = out_ref[...]
            share = gate_ref[...]
            dots = jnp.sum(cot_ref[...].astype(F32) * made, axis=-1, keepdims=True)
            weigh = pick_ref[...] * (dots * share * (1.0 - share))
            high = weigh.astype(BF16)
            low = (weigh - high.astype(F32)).astype(BF16)
            router = router_ref[...]
            back_ref[...] = (gs_ref[...] + mm(high, router, NT) + mm(low, router, NT)).astype(BF16)
            low_ref[...] = (share * made).astype(BF16)


def expert_pass(rows_in, grad_in, inner, down, l, down_from, start=None, last=None):
    rows, width = rows_in.shape
    units = inner.shape[1] // 2
    tile = 512 if units % 512 == 0 and down_from % 512 == 0 else 256
    first = down_from // tile

    def whole(array):
        return once(array.shape, lambda i: (0,) * array.ndim)

    more = ([] if start is None else list(start)) + ([] if last is None else list(last))
    kind = F32 if last is None else BF16
    return pl.pallas_call(
        functools.partial(expert_body, start is not None, last is not None),
        grid=(units // tile,),
        in_specs=[
            whole(rows_in),
            whole(grad_in),
            pl.BlockSpec((width, tile), lambda i: (0, i)),
            pl.BlockSpec((width, tile), lambda i: (0, units // tile + i)),
            pl.BlockSpec((None, tile, width), lambda i: (l, first + i, 0)),
        ]
        + [whole(m) for m in more],
        out_specs=[pl.BlockSpec((rows, width), lambda i: (0, 0))] * 2,
        out_shape=[jax.ShapeDtypeStruct((rows, width), kind)] * 2,
        scratch_shapes=[] if last is None else [pltpu.VMEM((rows, width), F32)] * 2,
        compiler_params=params("arbitrary"),
        name="expert",
    )(rows_in, grad_in, inner, inner, down, *more)


def out_back_body(locals_, arrived_ref, order_ref, gate_ref, projected_ref, *refs):
    w_refs, (out_ref, dots_ref, rows_ref) = refs[:locals_], refs[locals_:]
    slots = projected_ref.shape[1]

    @pl.when(pl.program_id(0) == 0)
    def _():
        for l in range(locals_):
            rows = mm(order_ref[pl.ds(l * slots, slots), :], arrived_ref[...])
            dots_ref[l] = jnp.sum(rows * projected_ref[l].astype(F32), axis=-1, keepdims=True)
            rows_ref[l] = (rows * gate_ref[l]).astype(BF16)

    for l in range(locals_):
        out_ref[l] = mm(rows_ref[l], w_refs[l][...], NT).astype(BF16)


def out_back(s, arrived, order, gate, projected, weights, from_column):
    locals_, slots = gate.shape[0], gate.shape[2]
    rows, width = arrived.shape
    tile = 512
    return pl.pallas_call(
        functools.partial(out_back_body, locals_),
        grid=(width // tile,),
        in_specs=[
            once((rows, width), lambda i: (0, 0)),
            once((rows, rows), lambda i: (0, 0)),
            once((locals_, None, slots, 1), lambda i: (0, s, 0, 0)),
            once((locals_, None, slots, width), lambda i: (0, s, 0, 0)),
        ]
        + [
            pl.BlockSpec((tile, width), lambda i, l=l: (i, from_column // width + l))
            for l in range(locals_)
        ],
        out_specs=[
            pl.BlockSpec((locals_, slots, tile), lambda i: (0, 0, i)),
            pl.BlockSpec((locals_, slots, 1), lambda i: (0, 0, 0)),
        ],
        out_shape=[
            jax.ShapeDtypeStruct((locals_, slots, width), BF16),
            jax.ShapeDtypeStruct((locals_, slots, 1), F32),
        ],
        scratch_shapes=[pltpu.VMEM((locals_, slots, width), BF16)],
        compiler_params=params("arbitrary"),
        name="out_back",
    )(arrived, order, gate, projected, *([weights] * locals_))


def last_body(
    locals_, seq_len, dk_ref, dv_ref, dq_ref, table_ref, dots_ref, weigh_ref, mask_ref, up_ref, router_ref, down_ref, w_ref, *refs
):
    wq_refs, (out_ref, low_ref, source_ref, weigh_low_ref) = refs[:locals_], refs[locals_:]
    width = dk_ref.shape[1]
    slots = dq_ref.shape[1]

    @pl.when(pl.program_id(0) == 0)
    def _():
        low = mm(dk_ref[...], up_ref[:width, :]) + mm(dv_ref[...], up_ref[width:, :])
        low_ref[...] = (low * mask_ref[...]).astype(BF16)
        for l in range(locals_):
            weigh = weigh_ref[l] * dots_ref[l]
            high = weigh.astype(BF16)
            weigh_low_ref[l, :, :EXPERTS] = high
            weigh_low_ref[l, :, EXPERTS:] = (weigh - high.astype(F32)).astype(BF16)

    router = jnp.concatenate([router_ref[...]] * 2, axis=1)
    for l in range(locals_):
        source = mm(dq_ref[l], wq_refs[l][...], NT) + mm(weigh_low_ref[l], router, NT)
        source_ref[pl.ds(l * slots, slots), :] = source.astype(BF16)
    total = mm(dk_ref[...], w_ref[:, :width], NT) + mm(dv_ref[...], w_ref[:, width:], NT)
    total += mm(low_ref[...], down_ref[...], NT)
    total += mm(table_ref[0], source_ref[...])
    out_ref[...] = total.astype(BF16)


def last_grad(s, dk, dv, dq, table, dots, weigh, mask, adapt_up, router, adapt_down, weights, query_column):
    seq_len, width = dk.shape
    locals_, slots, _ = dq.shape
    tile = 256
    ranks = adapt_up.shape[1]
    return pl.pallas_call(
        functools.partial(last_body, locals_, seq_len),
        grid=(width // tile,),
        in_specs=[
            once((seq_len, width), lambda i: (0, 0)),
            once((seq_len, width), lambda i: (0, 0)),
            once((locals_, slots, width), lambda i: (0, 0, 0)),
            once((1, seq_len, locals_ * slots), lambda i: (s, 0, 0)),
            once((locals_, slots, 1), lambda i: (0, 0, 0)),
            once((locals_, None, slots, EXPERTS), lambda i: (0, s, 0, 0)),
            once((None, 1, ranks), lambda i: (s, 0, 0)),
            once((2 * width, ranks), lambda i: (0, 0)),
            pl.BlockSpec((tile, EXPERTS), lambda i: (i, 0)),
            pl.BlockSpec((tile, ranks), lambda i: (i, 0)),
            pl.BlockSpec((tile, 2 * width), lambda i: (i, 0)),
        ]
        + [
            pl.BlockSpec((tile, width), lambda i, l=l: (i, query_column // width + l))
            for l in range(locals_)
        ],
        out_specs=[
            pl.BlockSpec((seq_len, tile), lambda i: (0, i)),
            pl.BlockSpec((seq_len, ranks), lambda i: (0, 0)),
        ],
        out_shape=[
            jax.ShapeDtypeStruct((seq_len, width), BF16),
            jax.ShapeDtypeStruct((seq_len, ranks), BF16),
        ],
        scratch_shapes=[
            pltpu.VMEM((locals_ * slots, tile), BF16),
            pltpu.VMEM((locals_, slots, 2 * EXPERTS), BF16),
        ],
        compiler_params=params("arbitrary"),
        name="last_grad",
    )(dk, dv, dq, table, dots, weigh, mask, adapt_up, router, adapt_down, weights, *([weights] * locals_))


def middle_back_body(back_ref, table_ref, part_ref, middle_ref, cot_ref, gain_ref, spread_ref, out_ref, rows_ref):
    middle = middle_ref[...]
    scale = rms_scale(middle)
    grad = part_ref[...] + mm(table_ref[...], back_ref[...])
    out = cot_ref[...].astype(F32) + norm_back(middle, scale, gain_ref[...], grad)
    out_ref[...] = out
    rows_ref[...] = mm(spread_ref[...], out.astype(BF16)).astype(BF16)


def middle_back(s, back, table, part, middle, cotangent, gain, spread):
    _, rows, width = middle.shape
    slots = spread.shape[1]

    def one(array):
        return once((None, *array.shape[1:]), lambda i: (s, 0, 0))

    return pl.pallas_call(
        middle_back_body,
        grid=(1,),
        in_specs=[
            once(back.shape, lambda i: (0, 0)),
            one(table),
            one(part),
            one(middle),
            one(cotangent),
            once(gain.shape, lambda i: (0, 0)),
            one(spread),
        ],
        out_specs=[once((rows, width), lambda i: (0, 0)), once((slots, width), lambda i: (0, 0))],
        out_shape=[
            jax.ShapeDtypeStruct((rows, width), F32),
            jax.ShapeDtypeStruct((slots, width), BF16),
        ],
        compiler_params=params("arbitrary"),
        name="middle_back",
    )(back, table, part, middle, cotangent, gain, spread)


def input_back_body(grad_ref, middle_ref, tokens_ref, gain_ref, *refs):
    tokens = tokens_ref[...].astype(F32)
    refs[-1][...] = middle_ref[...] + norm_back(
        tokens, rms_scale(tokens), gain_ref[...], grad_ref[...].astype(F32)
    )


def input_back(s, grad, grad_middle, tokens, gain, total):
    seqs, rows, width = tokens.shape
    tile = 128
    flat = pl.BlockSpec((tile, width), lambda i: (i, 0))
    one = pl.BlockSpec((None, tile, width), lambda i: (s, i, 0))
    return pl.pallas_call(
        input_back_body,
        grid=(rows // tile,),
        in_specs=[flat, flat, one, pl.BlockSpec((1, width), lambda i: (0, 0))]
        + ([] if total is None else [pl.BlockSpec(memory_space=pl.ANY)]),
        out_specs=one,
        out_shape=jax.ShapeDtypeStruct(tokens.shape, F32),
        input_output_aliases={} if total is None else {4: 0},
        compiler_params=params("arbitrary"),
        name="input_back",
    )(grad, grad_middle, tokens, gain, *([] if total is None else [total]))


def per_device(
    hidden_in,
    cotangent,
    block_ids,
    attn_routes,
    mlp_routes,
    adapter_index,
    attn_gain,
    mlp_gain,
    attn_router,
    mlp_router,
    kv_weight,
    query_weight,
    output_weight,
    inner_weight,
    down_weight,
    adapt_down,
    adapt_up,
):
    seqs, row_count, width = hidden_in.shape
    seq_len = block_ids.shape[1]
    ranks = seq_len // row_count
    locals_ = query_weight.shape[0]
    capacity = (17 * row_count * TOP + 16 * EXPERTS - 1) // (16 * EXPERTS)
    slots = ranks * capacity
    here = lax.axis_index("expert")

    query_column = 2 * width
    output_column = query_column + locals_ * width
    near = jnp.concatenate(
        [kv_weight]
        + [query_weight[l] for l in range(locals_)]
        + [output_weight[l] for l in range(locals_)],
        axis=1,
    )
    near_full = lax.all_gather(near, "dp", axis=0, tiled=True)
    down_full = lax.all_gather(down_weight, "dp", axis=1, tiled=True)
    groups = width // kv_weight.shape[0]

    def stretch(array, l, low, high):
        return jnp.concatenate([array[l, :, low:high], array[l, :, FF + low : FF + high]], axis=1)

    inner_full, beside = [], []
    for l in range(locals_):
        pieces = []
        cut = 3 * 512 if l + 1 < locals_ else FF * 3 // 4 // 512 * 512
        if l + 1 < locals_:
            pieces.append((0, None))
            beside.append(stretch(inner_weight, l, 0, cut))
        else:
            pieces.append((0, lax.all_gather(stretch(inner_weight, l, 0, cut), "dp", axis=0, tiled=True)))
        pieces.append((cut, lax.all_gather(stretch(inner_weight, l, cut, FF), "dp", axis=0, tiled=True)))
        inner_full.append(pieces)

    routes = lax.all_gather(
        jnp.concatenate([attn_routes, mlp_routes], axis=-1), "expert", axis=1, tiled=True
    ).reshape(seqs, ranks, row_count, 2, TOP)
    adapters = lax.all_gather(adapter_index, "dp", axis=0, tiled=True)
    expert_ids = jnp.arange(EXPERTS, dtype=jnp.int32)
    onehot = (routes[..., None] == expert_ids).astype(F32)
    hits = jnp.sum(onehot, axis=4)
    earlier = (
        jnp.arange(row_count)[:, None] > jnp.arange(row_count)[None, :]
    ).astype(BF16)
    before = jnp.einsum("ut,sptke->spuke", earlier, hits.astype(BF16), preferred_element_type=F32)
    place = jnp.sum(onehot * before[..., None, :], axis=-1).astype(jnp.int32)
    attn_all, mlp_all = routes[:, :, :, 0], routes[:, :, :, 1]
    attn_place, mlp_place = place[:, :, :, 0], place[:, :, :, 1]
    source = jnp.arange(ranks, dtype=jnp.int32)[None, :, None, None]
    which = jnp.arange(seqs, dtype=jnp.int32)[:, None, None, None]

    local_a = attn_all - here * locals_
    is_local = (local_a >= 0) & (local_a < locals_)
    slot_a = jnp.where(is_local, local_a * slots + source * capacity + attn_place, -1)
    slot_a = slot_a.reshape(seqs, seq_len, TOP)
    slot_iota = jnp.arange(locals_ * slots, dtype=jnp.int32)
    spread_a = (
        (slot_iota[None, :, None] == slot_a[:, None, :, 0])
        | (slot_iota[None, :, None] == slot_a[:, None, :, 1])
    ).astype(BF16)
    collect_a = (
        (slot_iota[None, None, :] == slot_a[:, :, 0, None])
        | (slot_iota[None, None, :] == slot_a[:, :, 1, None])
    ).astype(BF16)

    def own(array):
        return lax.dynamic_index_in_dim(array, here, 1, keepdims=False)

    attn_own, attn_own_place = own(attn_all), own(attn_place)
    mlp_own, mlp_own_place = own(mlp_all), own(mlp_place)
    own_slot = attn_own * capacity + attn_own_place
    own_iota = jnp.arange(EXPERTS * capacity, dtype=jnp.int32)
    own_spread_a = (
        (own_iota[None, :, None] == own_slot[:, None, :, 0])
        | (own_iota[None, :, None] == own_slot[:, None, :, 1])
    ).astype(BF16)
    own_collect_a = (
        (own_iota[None, None, :] == own_slot[:, :, 0, None])
        | (own_iota[None, None, :] == own_slot[:, :, 1, None])
    ).astype(BF16)
    mlp_rows = ranks * seqs * capacity
    mlp_iota = jnp.arange(mlp_rows, dtype=jnp.int32)
    own_spread_m, own_collect_m, other_sum = [], [], []
    for l in range(locals_):
        ids = jnp.where(
            mlp_own % locals_ == l,
            (mlp_own // locals_) * (seqs * capacity) + which[:, 0] * capacity + mlp_own_place,
            -1,
        ).reshape(seqs * row_count, TOP)
        own_spread_m.append(
            ((mlp_iota[:, None] == ids[None, :, 0]) | (mlp_iota[:, None] == ids[None, :, 1])).astype(BF16)
        )
        own_collect_m.append(
            ((mlp_iota[None, :] == ids[:, 0, None]) | (mlp_iota[None, :] == ids[:, 1, None])).astype(BF16)
        )
        ids = jnp.where(
            mlp_all == here * locals_ + l,
            source * (seqs * capacity) + which * capacity + mlp_place,
            -1,
        ).reshape(seqs * seq_len, TOP)
        table = (
            (mlp_iota[:, None] == ids[None, :, 0]) | (mlp_iota[:, None] == ids[None, :, 1])
        ).astype(BF16)
        both = jnp.sum(mlp_all, axis=-1).reshape(seqs * seq_len, 1).astype(BF16)
        sums = mm(table, jnp.concatenate([both, jnp.ones_like(both)], axis=1))
        other_sum.append((sums[:, :1], sums[:, 1:]))

    hidden_first, routes, adapters = lax.optimization_barrier((hidden_in, routes, adapters))
    everyone = gather_line(
        hidden_first,
        "expert",
        ranks,
        lambda total, piece, at: lax.dynamic_update_slice(total, piece[:, None], (0, at, 0, 0)),
        jnp.zeros((seqs, ranks, row_count, width), BF16),
    ).reshape(seqs, seq_len, width)

    flat_cot, everyone = lax.optimization_barrier((cotangent, everyone))
    orders = halves_bits(groups)
    beside = [[block[: block.shape[0] // 2], block[block.shape[0] // 2 :]] for block in beside]

    def exchange_all(step):
        return [
            [exchange(half, "dp", groups, bits[step]) for half, bits in zip(halves, orders)]
            for halves in beside
        ]

    flat_cot = flat_cot.reshape(seqs * row_count, width)
    cot_rows = [send(mm(own_spread_m[l], flat_cot).astype(BF16)) for l in range(locals_)]

    tokens_all = everyone.astype(F32)
    scale_all = rms_scale(tokens_all)
    normed_low = (tokens_all * scale_all * attn_gain).astype(BF16)
    router_parts = jnp.concatenate(three_parts(attn_gain[:, None] * attn_router.astype(F32)), axis=1)
    parts = mm(everyone.reshape(seqs * seq_len, width), router_parts).reshape(seqs, seq_len, 3, EXPERTS)
    logits = scale_all * (parts[:, :, 0] + (parts[:, :, 1] + parts[:, :, 2]))
    onehot_a = onehot[:, :, :, 0].reshape(seqs, seq_len, TOP, EXPERTS)
    gap = jnp.sum((onehot_a[:, :, 0] - onehot_a[:, :, 1]) * logits, axis=-1)

    flat_routes = attn_all.reshape(seqs, seq_len, TOP)
    places = jnp.arange(seq_len, dtype=jnp.int32)
    columns = [
        block_ids,
        jnp.broadcast_to(places // 128, block_ids.shape),
        jnp.broadcast_to(places % 128, block_ids.shape),
        jnp.sum(flat_routes, axis=-1),
        flat_routes[..., 0],
    ]
    known = jnp.stack([c.astype(BF16) for c in columns] + list(three_parts(gap)), axis=-1)
    known = jnp.einsum("srt,stc->src", spread_a, known, preferred_element_type=F32)
    known = known.reshape(seqs, locals_, slots, known.shape[-1]).transpose(1, 0, 2, 3)
    self_id = (here * locals_ + jnp.arange(locals_)).astype(F32)[:, None, None]
    slot_blocks = known[..., 0].astype(jnp.int32)
    slot_place = known[..., 1] * 128.0 + known[..., 2]
    slot_other = known[..., 3] - self_id
    slot_gap = known[..., 5] + (known[..., 6] + known[..., 7])
    slot_gap = jnp.where(known[..., 4] == self_id, slot_gap, -slot_gap)
    gate_a = jax.nn.sigmoid(slot_gap)
    expert_f = expert_ids.astype(F32)
    pick_a = (expert_f == self_id[..., None]).astype(F32) - (expert_f == slot_other[..., None]).astype(F32)
    weigh_a = pick_a * (gate_a * jax.nn.sigmoid(-slot_gap))[..., None]
    cos_q, sin_q = angle_tables(slot_place)
    cos_k, sin_k = angle_tables(places)
    query_blocks = slot_blocks[..., None]
    key_blocks = block_ids[:, None, :]

    flat_low = normed_low.reshape(seqs * seq_len, width)
    own_adapter = (
        jnp.arange(NADAPT * RANK, dtype=jnp.int32)[None, :] // RANK == adapter_index[:, None]
    )
    low_rank = mm(flat_low, adapt_down).reshape(seqs, seq_len, NADAPT * RANK)
    low_rank = jnp.where(own_adapter[:, None, :], low_rank, 0.0).astype(BF16)
    key_value = make_key_value(
        flat_low, low_rank.reshape(seqs * seq_len, -1), near_full, adapt_up, cos_k, sin_k, seqs
    ).reshape(seqs, seq_len, 2 * width)

    picked = jnp.einsum(
        "slrt,std->lsrd",
        spread_a.reshape(seqs, locals_, slots, seq_len),
        normed_low,
        preferred_element_type=F32,
    ).astype(BF16)
    queries = project(picked.reshape(locals_, seqs * slots, width), near_full, query_column)
    query_rot, attended, probs = attend(
        queries.reshape(locals_, seqs, slots, width), key_value, cos_q, sin_q, query_blocks, key_blocks
    )
    beside, attended = lax.optimization_barrier((beside, attended))
    for step in range(len(orders[0])):
        beside = exchange_all(step)
    for l, halves in enumerate(beside):
        inner_full[l][0] = (0, in_order(halves, orders, groups))
    gate_rows = gate_a[..., None]
    projected, gated = project(
        attended.reshape(locals_, seqs * slots, width),
        near_full,
        output_column,
        gate_rows.reshape(locals_, seqs * slots, 1),
    )
    projected = projected.reshape(locals_, seqs, slots, width)
    gated = gated.reshape(locals_, seqs, slots, width)
    order = np.arange(locals_ * slots).reshape(locals_, ranks, capacity).transpose(1, 0, 2).reshape(-1)
    to_send = jnp.asarray(np.eye(locals_ * slots)[order], BF16)
    to_slots = jnp.asarray(np.eye(locals_ * slots)[order].T, BF16)
    tokens = hidden_in.astype(F32)
    middles = []
    for s in range(seqs):
        back = send(mm(to_send, gated[:, s].reshape(locals_ * slots, width)).astype(BF16))
        middles.append(tokens[s] + mm(own_collect_a[s], back))
    middle = jnp.stack(middles)
    scale_two = rms_scale(middle)
    normed_two_low = (middle * scale_two * mlp_gain).astype(BF16).reshape(seqs * row_count, width)

    final = middle.reshape(seqs * row_count, width)
    grad_normed_two = jnp.zeros((seqs * row_count, width), F32)
    held = None
    for l in range(locals_):
        rows_in = send(mm(own_spread_m[l], normed_two_low).astype(BF16))
        slot_logits = mm(rows_in, mlp_router)
        me = (here * locals_ + l).astype(F32)
        pick_m = (expert_f[None, :] == me).astype(F32) - (
            expert_f[None, :] == other_sum[l][0] - me
        ).astype(F32)
        gate_m = jax.nn.sigmoid(jnp.sum(pick_m * slot_logits, axis=-1, keepdims=True))
        grad_rows = (gate_m * cot_rows[l].astype(F32)).astype(BF16)
        made = None
        for at, (low, inner) in enumerate(inner_full[l]):
            if held is not None and at + 1 == len(inner_full[l]):
                held, made = lax.optimization_barrier((held, made))
                final = final + mm(own_collect_m[l - 1], held)
            ends = (cot_rows[l], gate_m, pick_m, mlp_router) if at + 1 == len(inner_full[l]) else None
            made = expert_pass(rows_in, grad_rows, inner, down_full, l, low, made, ends)
        gated_out, grad_source = made
        grad_back = send(grad_source)
        if l + 1 < locals_:
            grad_normed_two = grad_normed_two + mm(own_collect_m[l], grad_back)
        held = send(gated_out) if l + 1 < locals_ else gated_out
    grad_normed_two = grad_normed_two.reshape(seqs, row_count, width)
    late = (collect_a, own_adapter.astype(F32)[:, None, :], weigh_a, attn_router, to_slots)
    (collect_a, mask, weigh_a, router_near, to_slots), grad_normed_two = lax.optimization_barrier(
        (late, grad_normed_two)
    )
    back_table = own_collect_m[locals_ - 1].reshape(seqs, row_count, mlp_rows)
    grad_middle, leaving = [], []
    for s in range(seqs):
        grad, rows = middle_back(
            s, grad_back, back_table, grad_normed_two, middle, cotangent, mlp_gain[None], own_spread_a
        )
        grad_middle.append(grad)
        leaving.append(rows)

    arrived = [send(leaving[0])]
    arrived[0], held, leaving[1:] = lax.optimization_barrier((arrived[0], held, leaving[1:]))
    held = send(held)
    down_pieces, up_pieces = [], []
    input_grad = None
    for s in range(seqs):
        grad_attended, dots = out_back(
            s, arrived[s], to_slots, gate_rows, projected, near_full, output_column
        )
        dq, dk, dv = attend_back(s, query_rot, key_value, grad_attended, probs, cos_q, sin_q, cos_k, sin_k)
        if s + 1 < seqs:
            leaving[s + 1], held, dk = lax.optimization_barrier((leaving[s + 1], held, dk))
            arrived.append(send(leaving[s + 1]))
        part, grad_low = last_grad(
            s, dk, dv, dq, collect_a, dots, weigh_a, mask, adapt_up, router_near, adapt_down, near_full,
            query_column,
        )
        if s + 1 < seqs:
            arrived[s + 1], part = lax.optimization_barrier((arrived[s + 1], part))
        grad_normed = lax.psum_scatter(part, "expert", scatter_dimension=0, tiled=True)
        input_grad = input_back(s, grad_normed, grad_middle[s], hidden_in, attn_gain[None], input_grad)
        first = adapter_index[s] * RANK
        down_pieces.append(lax.dynamic_slice_in_dim(mm(grad_low, normed_low[s], TN), first, RANK, 0))
        up_piece = jnp.concatenate([mm(low_rank[s], dk, TN), mm(low_rank[s], dv, TN)], axis=1)
        up_pieces.append(lax.dynamic_slice_in_dim(up_piece, first, RANK, 0))
    final = final + mm(own_collect_m[locals_ - 1], held)
    layer_out = final.astype(BF16).reshape(seqs, row_count, width)

    down_part = width // (groups * ranks)
    pieces = jnp.concatenate(
        [
            jnp.stack(down_pieces).reshape(seqs * RANK, groups, ranks, down_part),
            jnp.stack(up_pieces).reshape(seqs * RANK, groups, ranks, 2 * down_part),
        ],
        axis=-1,
    )
    pieces = pieces.transpose(1, 0, 2, 3).reshape(groups, seqs * RANK, 3 * ranks * down_part)
    pieces = lax.all_to_all(pieces, "dp", split_axis=0, concat_axis=0, tiled=True)
    pieces = pieces.reshape(groups * seqs, RANK, 3 * ranks * down_part)
    belongs = (adapters[:, None] == jnp.arange(NADAPT, dtype=jnp.int32)[None, :]).astype(F32)
    sums = jnp.einsum("qkf,qa->akf", pieces, belongs, precision=PRECISE)
    sums = sums.reshape(NADAPT * RANK, ranks, 3 * down_part).transpose(1, 0, 2)
    sums = jnp.sum(send(sums), axis=0).T
    return (layer_out, input_grad, sums[:down_part], sums[down_part:])


def solution(mesh):
    return jax.shard_map(
        per_device,
        mesh=mesh,
        in_specs=(
            P("dp", "expert", None),
            P("dp", "expert", None),
            P("dp", None),
            P("dp", "expert", None),
            P("dp", "expert", None),
            P("dp"),
            P(),
            P(),
            P(),
            P(),
            P("dp", None),
            P("expert", "dp", None),
            P("expert", "dp", None),
            P("expert", "dp", None),
            P("expert", "dp", None),
            P(),
            P(),
        ),
        out_specs=(
            P("dp", "expert", None),
            P("dp", "expert", None),
            P(("dp", "expert"), None),
            P(("dp", "expert"), None),
        ),
        check_vma=False,
    )
```

```python
import functools
import math

import jax
import jax.numpy as jnp
import numpy as np
from jax import lax
from jax.experimental import pallas as pl
from jax.experimental.pallas import tpu as pltpu
from jax.sharding import PartitionSpec as P

HEADS = 16
HDIM = 128
FF = 5632
EXPERTS = 8
TOP = 2
RANK = 16
NADAPT = 8

PRECISE = lax.Precision.HIGHEST
EPSILON = 1e-06
ROPE_BASE = 10000.0
MASKED_SCORE = -1e30
SCALE_QK = 1.0 / math.sqrt(HDIM)
BF16 = jnp.bfloat16
F32 = jnp.float32
VMEM_LIMIT = 58 * 1024 * 1024

NN = (((1,), (0,)), ((), ()))
NT = (((1,), (1,)), ((), ()))
TN = (((0,), (0,)), ((), ()))


def mm(left, right, dims=NN):
    return lax.dot_general(left, right, dims, preferred_element_type=F32)


def params(*semantics):
    return pltpu.CompilerParams(dimension_semantics=semantics, vmem_limit_bytes=VMEM_LIMIT)


def once(shape, index_map):
    return pl.BlockSpec(shape, index_map, pipeline_mode=pl.Buffered(1))


def rms_scale(values):
    return lax.rsqrt(jnp.mean(values * values, axis=-1, keepdims=True) + EPSILON)


def norm_back(values, scale_rows, norm_gain, grad_rows):
    scaled_grad = norm_gain * grad_rows
    return scale_rows * (
        scaled_grad
        - values * scale_rows * scale_rows * jnp.mean(scaled_grad * values, axis=-1, keepdims=True)
    )


def angle_tables(positions):
    half_dim = HDIM // 2
    frequency = ROPE_BASE ** (-(jnp.arange(half_dim, dtype=F32) * (2.0 / HDIM)))
    frequency = jnp.concatenate([frequency, frequency])
    sign = jnp.concatenate([-jnp.ones((half_dim,), F32), jnp.ones((half_dim,), F32)])
    angles = positions.astype(F32)[..., None] * frequency
    return (jnp.cos(angles), jnp.sin(angles) * sign)


def three_parts(values):
    first = values.astype(BF16)
    rest = values - first.astype(F32)
    second = rest.astype(BF16)
    third = (rest - second.astype(F32)).astype(BF16)
    return first, second, third


def gather_line(block, axis, size, put, start):
    here = lax.axis_index(axis)
    rightward = [(i, i + 1) for i in range(size - 1)]
    leftward = [(i + 1, i) for i in range(size - 1)]
    from_left, from_right = [block], [block]
    for _ in range(size - 1):
        from_left.append(lax.ppermute(from_left[-1], axis, rightward))
        from_right.append(lax.ppermute(from_right[-1], axis, leftward))
    total = put(start, block, here)
    for step in range(1, size):
        piece = jnp.where(here >= step, from_left[step], from_right[size - step])
        total = put(total, piece, lax.rem(here - step + size, size))
    return total


def exchange(total, axis, size, bit):
    other = lax.ppermute(total, axis, [(i, i ^ bit) for i in range(size)])
    low = jnp.bitwise_and(lax.axis_index(axis), bit) == 0
    return jnp.stack([jnp.where(low, total, other), jnp.where(low, other, total)])


def halves_bits(size):
    bits = [1 << k for k in range(1, size.bit_length() - 1)]
    return [bits + [1], bits[::-1] + [1]]


def in_order(halves, orders, size):
    made = []
    for total, bits in zip(halves, orders):
        count = len(bits)
        order = sorted(range(count), key=lambda d: -bits[count - 1 - d])
        total = total.transpose(*order, *range(count, total.ndim))
        made.append(total.reshape(size, *total.shape[count:]))
    whole = jnp.stack(made, axis=1)
    return whole.reshape(-1, whole.shape[-1])


def send(buffer):
    return lax.all_to_all(buffer, "expert", split_axis=0, concat_axis=0, tiled=True)


def kv_body(seqs, seq_len, key_tiles, x_ref, low_ref, w_ref, up_ref, cos_ref, sin_ref, out_ref):
    is_key = pl.program_id(0) < key_tiles
    for s in range(seqs):
        rows = pl.ds(s * seq_len, seq_len)
        made = mm(x_ref[rows, :], w_ref[...]) + mm(low_ref[rows, :], up_ref[...], NT)

        @pl.when(is_key)
        def _(made=made, rows=rows):
            for h in range(made.shape[1] // HDIM):
                cols = slice(h * HDIM, (h + 1) * HDIM)
                part = made[:, cols]
                turned = part * cos_ref[...] + pltpu.roll(part, HDIM // 2, 1) * sin_ref[...]
                out_ref[rows, cols] = turned.astype(BF16)

        @pl.when(jnp.logical_not(is_key))
        def _(made=made, rows=rows):
            out_ref[rows, :] = made.astype(BF16)


def make_key_value(normed_low, low_rank, weights, adapt_up, cos_k, sin_k, seqs):
    rows, width = normed_low.shape
    seq_len = rows // seqs
    tile = 512
    return pl.pallas_call(
        functools.partial(kv_body, seqs, seq_len, width // tile),
        grid=(2 * width // tile,),
        in_specs=[
            once((rows, width), lambda i: (0, 0)),
            once((rows, low_rank.shape[1]), lambda i: (0, 0)),
            pl.BlockSpec((width, tile), lambda i: (0, i)),
            pl.BlockSpec((tile, low_rank.shape[1]), lambda i: (i, 0)),
            once((seq_len, HDIM), lambda i: (0, 0)),
            once((seq_len, HDIM), lambda i: (0, 0)),
        ],
        out_specs=pl.BlockSpec((rows, tile), lambda i: (0, i)),
        out_shape=jax.ShapeDtypeStruct((rows, 2 * width), BF16),
        compiler_params=params("arbitrary"),
        name="key_value",
    )(normed_low, low_rank, weights, adapt_up, cos_k, sin_k)


def project_body(x_ref, w_ref, *refs):
    made = mm(x_ref[...], w_ref[...])
    if len(refs) == 1:
        refs[0][...] = made.astype(BF16)
    else:
        gate_ref, out_ref, gated_ref = refs
        out_ref[...] = made.astype(BF16)
        gated_ref[...] = (made * gate_ref[...]).astype(BF16)


def project(values, weights, from_column, gate=None):
    locals_, rows, width = values.shape
    tile = 512
    first, step = from_column // tile, width // tile
    out_spec = pl.BlockSpec((None, rows, tile), lambda l, i: (l, 0, i))
    out_shape = jax.ShapeDtypeStruct(values.shape, BF16)
    in_specs = [
        pl.BlockSpec((None, rows, width), lambda l, i: (l, 0, 0)),
        pl.BlockSpec((width, tile), lambda l, i: (0, first + step * l + i)),
    ]
    more = []
    if gate is not None:
        in_specs.append(pl.BlockSpec((None, rows, 1), lambda l, i: (l, 0, 0)))
        more = [gate]
    return pl.pallas_call(
        project_body,
        grid=(locals_, step),
        in_specs=in_specs,
        out_specs=out_spec if gate is None else [out_spec] * 2,
        out_shape=out_shape if gate is None else [out_shape] * 2,
        compiler_params=params("arbitrary", "arbitrary"),
        name="project",
    )(values, weights, *more)


def attend_body(q_ref, k_ref, v_ref, cos_ref, sin_ref, qb_ref, kb_ref, rot_ref, out_ref, probs_ref):
    locals_, _, slots, _ = q_ref.shape
    rows = locals_ * slots
    q = q_ref[...].reshape(rows, HDIM).astype(F32)
    cos, sin = cos_ref[...].reshape(rows, HDIM), sin_ref[...].reshape(rows, HDIM)
    rot = (q * cos + pltpu.roll(q, HDIM // 2, 1) * sin).astype(BF16)
    rot_ref[...] = rot.reshape(rot_ref.shape)
    k, v = k_ref[0], v_ref[0]
    kb = kb_ref[0]
    for l in range(locals_):
        part = rot[l * slots : (l + 1) * slots]
        visible = kb <= qb_ref[l, 0]
        masked = jnp.where(visible, mm(part, k, NT), MASKED_SCORE)
        top = jnp.max(masked, axis=-1, keepdims=True)
        terms = jnp.exp((masked - top) * SCALE_QK)
        total = jnp.sum(terms, axis=-1, keepdims=True)
        probs = (terms * (1.0 / total)).astype(BF16)
        probs_ref[l, 0, 0] = probs
        out_ref[l, 0] = mm(probs, v).astype(BF16)


def attend(queries, key_value, cos_q, sin_q, query_blocks, key_blocks):
    locals_, seqs, slots, width = queries.shape
    seq_len = key_value.shape[1]
    q_spec = pl.BlockSpec((locals_, 1, slots, HDIM), lambda s, h: (0, s, 0, h))
    tab_spec = pl.BlockSpec((locals_, 1, slots, HDIM), lambda s, h: (0, s, 0, 0))
    return pl.pallas_call(
        attend_body,
        grid=(seqs, HEADS),
        in_specs=[
            q_spec,
            pl.BlockSpec((1, seq_len, HDIM), lambda s, h: (s, 0, h)),
            pl.BlockSpec((1, seq_len, HDIM), lambda s, h: (s, 0, HEADS + h)),
            tab_spec,
            tab_spec,
            pl.BlockSpec((locals_, 1, slots, 1), lambda s, h: (0, s, 0, 0)),
            pl.BlockSpec((1, 1, seq_len), lambda s, h: (s, 0, 0)),
        ],
        out_specs=[
            q_spec,
            q_spec,
            pl.BlockSpec((locals_, 1, 1, slots, seq_len), lambda s, h: (0, s, h, 0, 0)),
        ],
        out_shape=[
            jax.ShapeDtypeStruct(queries.shape, BF16),
            jax.ShapeDtypeStruct(queries.shape, BF16),
            jax.ShapeDtypeStruct((locals_, seqs, HEADS, slots, seq_len), BF16),
        ],
        compiler_params=params("arbitrary", "arbitrary"),
        name="attend",
    )(queries, key_value, key_value, cos_q, sin_q, query_blocks, key_blocks)


def attend_back_body(q_ref, k_ref, v_ref, g_ref, p_ref, cos_ref, sin_ref, ck_ref, sk_ref, dq_ref, dk_ref, dv_ref):
    locals_, _, slots, _ = q_ref.shape
    rows = locals_ * slots
    k, v = k_ref[0], v_ref[0]
    q = q_ref[...].reshape(rows, HDIM)
    grad = g_ref[...].reshape(rows, HDIM)
    probs = p_ref[...].reshape(rows, k.shape[0])
    weighed = probs.astype(F32) * mm(grad, v, NT)
    delta = jnp.sum(weighed, axis=-1, keepdims=True)
    grad_scores = (weighed - probs.astype(F32) * delta).astype(BF16)
    dq = mm(grad_scores, k) * SCALE_QK
    cos, sin = cos_ref[...].reshape(rows, HDIM), sin_ref[...].reshape(rows, HDIM)
    dq = dq * cos - pltpu.roll(dq, HDIM // 2, 1) * sin
    dq_ref[...] = dq.astype(BF16).reshape(dq_ref.shape)
    dk = mm(grad_scores, q, TN) * SCALE_QK
    dk_ref[...] = (dk * ck_ref[...] - pltpu.roll(dk, HDIM // 2, 1) * sk_ref[...]).astype(BF16)
    dv_ref[...] = mm(probs, grad, TN).astype(BF16)


def attend_back(s, query_rot, key_value, grad, probs, cos_q, sin_q, cos_k, sin_k):
    locals_, _, slots, width = query_rot.shape
    seq_len = key_value.shape[1]
    tab_spec = pl.BlockSpec((locals_, 1, slots, HDIM), lambda h: (0, s, 0, 0))
    key_tab = pl.BlockSpec((seq_len, HDIM), lambda h: (0, 0))
    grad_spec = pl.BlockSpec((locals_, slots, HDIM), lambda h: (0, 0, h))
    key_spec = pl.BlockSpec((seq_len, HDIM), lambda h: (0, h))
    return pl.pallas_call(
        attend_back_body,
        grid=(HEADS,),
        in_specs=[
            pl.BlockSpec((locals_, 1, slots, HDIM), lambda h: (0, s, 0, h)),
            pl.BlockSpec((1, seq_len, HDIM), lambda h: (s, 0, h)),
            pl.BlockSpec((1, seq_len, HDIM), lambda h: (s, 0, HEADS + h)),
            grad_spec,
            pl.BlockSpec((locals_, 1, 1, slots, seq_len), lambda h: (0, s, h, 0, 0)),
            tab_spec,
            tab_spec,
            key_tab,
            key_tab,
        ],
        out_specs=[grad_spec, key_spec, key_spec],
        out_shape=[
            jax.ShapeDtypeStruct((locals_, slots, width), BF16),
            jax.ShapeDtypeStruct((seq_len, width), BF16),
            jax.ShapeDtypeStruct((seq_len, width), BF16),
        ],
        compiler_params=params("arbitrary"),
        name="attend_back",
    )(query_rot, key_value, key_value, grad, probs, cos_q, sin_q, cos_k, sin_k)


def expert_body(has_start, is_last, x_ref, c_ref, wg_ref, wu_ref, wd_ref, *refs):
    refs = list(refs)
    start = [refs.pop(0), refs.pop(0)] if has_start else []
    if is_last:
        cot_ref, gate_ref, pick_ref, router_ref, low_ref, back_ref, out_ref, gs_ref = refs[:8]
        late = start + [cot_ref]
    else:
        out_ref, gs_ref = refs[:2]
        late = start
    count = len(late)
    held, sem = (refs[-count - 1 : -1], refs[-1]) if count else ([], None)
    copies = [pltpu.make_async_copy(late[i], held[i], sem.at[i]) for i in range(count)]

    @pl.when(pl.program_id(0) == 0)
    def _():
        for copy in copies:
            copy.start()
        out_ref[...] = jnp.zeros_like(out_ref)
        gs_ref[...] = jnp.zeros_like(gs_ref)

    x, c = x_ref[...], c_ref[...]
    wg, wu, wd = wg_ref[...], wu_ref[...], wd_ref[...]
    gate, up = mm(x, wg), mm(x, wu)
    sig = jax.nn.sigmoid(gate)
    silu = gate * sig
    out_ref[...] += mm((silu * up).astype(BF16), wd)
    grad = mm(c, wd, NT)
    grad_gate = (grad * up * sig * (1.0 + gate * (1.0 - sig))).astype(BF16)
    grad_up = (grad * silu).astype(BF16)
    gs_ref[...] += mm(grad_gate, wg, NT) + mm(grad_up, wu, NT)

    @pl.when(pl.program_id(0) == pl.num_programs(0) - 1)
    def _():
        for copy in copies:
            copy.wait()
        made, back = out_ref[...], gs_ref[...]
        if has_start:
            made, back = made + held[0][...], back + held[1][...]
        if has_start and not is_last:
            out_ref[...] = made
            gs_ref[...] = back
        if is_last:
            share = gate_ref[...]
            dots = jnp.sum(held[-1][...].astype(F32) * made, axis=-1, keepdims=True)
            weigh = pick_ref[...] * (dots * share * (1.0 - share))
            high = weigh.astype(BF16)
            low = (weigh - high.astype(F32)).astype(BF16)
            router = router_ref[...]
            back_ref[...] = (back + mm(high, router, NT) + mm(low, router, NT)).astype(BF16)
            low_ref[...] = (share * made).astype(BF16)


def expert_pass(rows_in, grad_in, inner, down, l, down_from, start=None, last=None):
    rows, width = rows_in.shape
    units = inner.shape[1] // 2
    tile = 512 if units % 512 == 0 and down_from % 512 == 0 else 256
    first = down_from // tile

    def whole(array):
        return once(array.shape, lambda i: (0,) * array.ndim)

    more = ([] if start is None else list(start)) + ([] if last is None else list(last))
    kind = F32 if last is None else BF16
    late = ([] if start is None else [F32, F32]) + ([] if last is None else [BF16])
    away = len(late)
    scratch = [] if last is None else [pltpu.VMEM((rows, width), F32)] * 2
    if away:
        scratch += [pltpu.VMEM((rows, width), t) for t in late] + [pltpu.SemaphoreType.DMA((away,))]
    return pl.pallas_call(
        functools.partial(expert_body, start is not None, last is not None),
        grid=(units // tile,),
        in_specs=[
            whole(rows_in),
            whole(grad_in),
            pl.BlockSpec((width, tile), lambda i: (0, i)),
            pl.BlockSpec((width, tile), lambda i: (0, units // tile + i)),
            pl.BlockSpec((None, tile, width), lambda i: (l, first + i, 0)),
        ]
        + [pl.BlockSpec(memory_space=pl.ANY) if i < away else whole(m) for i, m in enumerate(more)],
        out_specs=[pl.BlockSpec((rows, width), lambda i: (0, 0))] * 2,
        out_shape=[jax.ShapeDtypeStruct((rows, width), kind)] * 2,
        scratch_shapes=scratch,
        compiler_params=params("arbitrary"),
        name="expert",
    )(rows_in, grad_in, inner, inner, down, *more)


def out_back_body(locals_, arrived_ref, order_ref, gate_ref, projected_ref, *refs):
    w_refs, (out_ref, dots_ref, rows_ref) = refs[:locals_], refs[locals_:]
    slots = projected_ref.shape[1]

    @pl.when(pl.program_id(0) == 0)
    def _():
        for l in range(locals_):
            rows = mm(order_ref[pl.ds(l * slots, slots), :], arrived_ref[...])
            dots_ref[l] = jnp.sum(rows * projected_ref[l].astype(F32), axis=-1, keepdims=True)
            rows_ref[l] = (rows * gate_ref[l]).astype(BF16)

    for l in range(locals_):
        out_ref[l] = mm(rows_ref[l], w_refs[l][...], NT).astype(BF16)


def out_back(s, arrived, order, gate, projected, weights, from_column):
    locals_, slots = gate.shape[0], gate.shape[2]
    rows, width = arrived.shape
    tile = 512
    return pl.pallas_call(
        functools.partial(out_back_body, locals_),
        grid=(width // tile,),
        in_specs=[
            once((rows, width), lambda i: (0, 0)),
            once((rows, rows), lambda i: (0, 0)),
            once((locals_, None, slots, 1), lambda i: (0, s, 0, 0)),
            once((locals_, None, slots, width), lambda i: (0, s, 0, 0)),
        ]
        + [
            pl.BlockSpec((tile, width), lambda i, l=l: (i, from_column // width + l))
            for l in range(locals_)
        ],
        out_specs=[
            pl.BlockSpec((locals_, slots, tile), lambda i: (0, 0, i)),
            pl.BlockSpec((locals_, slots, 1), lambda i: (0, 0, 0)),
        ],
        out_shape=[
            jax.ShapeDtypeStruct((locals_, slots, width), BF16),
            jax.ShapeDtypeStruct((locals_, slots, 1), F32),
        ],
        scratch_shapes=[pltpu.VMEM((locals_, slots, width), BF16)],
        compiler_params=params("arbitrary"),
        name="out_back",
    )(arrived, order, gate, projected, *([weights] * locals_))


def last_body(
    locals_, seq_len, dk_ref, dv_ref, dq_ref, table_ref, dots_ref, weigh_ref, mask_ref, up_ref, router_ref, down_ref, w_ref, *refs
):
    wq_refs, (out_ref, low_ref, source_ref, weigh_low_ref) = refs[:locals_], refs[locals_:]
    width = dk_ref.shape[1]
    slots = dq_ref.shape[1]

    @pl.when(pl.program_id(0) == 0)
    def _():
        low = mm(dk_ref[...], up_ref[:width, :]) + mm(dv_ref[...], up_ref[width:, :])
        low_ref[...] = (low * mask_ref[...]).astype(BF16)
        for l in range(locals_):
            weigh = weigh_ref[l] * dots_ref[l]
            high = weigh.astype(BF16)
            weigh_low_ref[l, :, :EXPERTS] = high
            weigh_low_ref[l, :, EXPERTS:] = (weigh - high.astype(F32)).astype(BF16)

    router = jnp.concatenate([router_ref[...]] * 2, axis=1)
    for l in range(locals_):
        source = mm(dq_ref[l], wq_refs[l][...], NT) + mm(weigh_low_ref[l], router, NT)
        source_ref[pl.ds(l * slots, slots), :] = source.astype(BF16)
    total = mm(dk_ref[...], w_ref[:, :width], NT) + mm(dv_ref[...], w_ref[:, width:], NT)
    total += mm(low_ref[...], down_ref[...], NT)
    total += mm(table_ref[0], source_ref[...])
    out_ref[...] = total.astype(BF16)


def last_grad(s, dk, dv, dq, table, dots, weigh, mask, adapt_up, router, adapt_down, weights, query_column):
    seq_len, width = dk.shape
    locals_, slots, _ = dq.shape
    tile = 256
    ranks = adapt_up.shape[1]
    return pl.pallas_call(
        functools.partial(last_body, locals_, seq_len),
        grid=(width // tile,),
        in_specs=[
            once((seq_len, width), lambda i: (0, 0)),
            once((seq_len, width), lambda i: (0, 0)),
            once((locals_, slots, width), lambda i: (0, 0, 0)),
            once((1, seq_len, locals_ * slots), lambda i: (s, 0, 0)),
            once((locals_, slots, 1), lambda i: (0, 0, 0)),
            once((locals_, None, slots, EXPERTS), lambda i: (0, s, 0, 0)),
            once((None, 1, ranks), lambda i: (s, 0, 0)),
            once((2 * width, ranks), lambda i: (0, 0)),
            pl.BlockSpec((tile, EXPERTS), lambda i: (i, 0)),
            pl.BlockSpec((tile, ranks), lambda i: (i, 0)),
            pl.BlockSpec((tile, 2 * width), lambda i: (i, 0)),
        ]
        + [
            pl.BlockSpec((tile, width), lambda i, l=l: (i, query_column // width + l))
            for l in range(locals_)
        ],
        out_specs=[
            pl.BlockSpec((seq_len, tile), lambda i: (0, i)),
            pl.BlockSpec((seq_len, ranks), lambda i: (0, 0)),
        ],
        out_shape=[
            jax.ShapeDtypeStruct((seq_len, width), BF16),
            jax.ShapeDtypeStruct((seq_len, ranks), BF16),
        ],
        scratch_shapes=[
            pltpu.VMEM((locals_ * slots, tile), BF16),
            pltpu.VMEM((locals_, slots, 2 * EXPERTS), BF16),
        ],
        compiler_params=params("arbitrary"),
        name="last_grad",
    )(dk, dv, dq, table, dots, weigh, mask, adapt_up, router, adapt_down, weights, *([weights] * locals_))


def middle_back_body(back_ref, table_ref, part_ref, middle_ref, cot_ref, gain_ref, spread_ref, out_ref, rows_ref):
    middle = middle_ref[...]
    scale = rms_scale(middle)
    grad = part_ref[...] + mm(table_ref[...], back_ref[...])
    out = cot_ref[...].astype(F32) + norm_back(middle, scale, gain_ref[...], grad)
    out_ref[...] = out
    rows_ref[...] = mm(spread_ref[...], out.astype(BF16)).astype(BF16)


def middle_back(s, back, table, part, middle, cotangent, gain, spread):
    _, rows, width = middle.shape
    slots = spread.shape[1]

    def one(array):
        return once((None, *array.shape[1:]), lambda i: (s, 0, 0))

    return pl.pallas_call(
        middle_back_body,
        grid=(1,),
        in_specs=[
            once(back.shape, lambda i: (0, 0)),
            one(table),
            one(part),
            one(middle),
            one(cotangent),
            once(gain.shape, lambda i: (0, 0)),
            one(spread),
        ],
        out_specs=[once((rows, width), lambda i: (0, 0)), once((slots, width), lambda i: (0, 0))],
        out_shape=[
            jax.ShapeDtypeStruct((rows, width), F32),
            jax.ShapeDtypeStruct((slots, width), BF16),
        ],
        compiler_params=params("arbitrary"),
        name="middle_back",
    )(back, table, part, middle, cotangent, gain, spread)


def input_back_body(grad_ref, middle_ref, tokens_ref, gain_ref, *refs):
    tokens = tokens_ref[...].astype(F32)
    refs[-1][...] = middle_ref[...] + norm_back(
        tokens, rms_scale(tokens), gain_ref[...], grad_ref[...].astype(F32)
    )


def input_back(s, grad, grad_middle, tokens, gain, total):
    seqs, rows, width = tokens.shape
    tile = 128
    flat = pl.BlockSpec((tile, width), lambda i: (i, 0))
    one = pl.BlockSpec((None, tile, width), lambda i: (s, i, 0))
    return pl.pallas_call(
        input_back_body,
        grid=(rows // tile,),
        in_specs=[flat, flat, one, pl.BlockSpec((1, width), lambda i: (0, 0))]
        + ([] if total is None else [pl.BlockSpec(memory_space=pl.ANY)]),
        out_specs=one,
        out_shape=jax.ShapeDtypeStruct(tokens.shape, F32),
        input_output_aliases={} if total is None else {4: 0},
        compiler_params=params("arbitrary"),
        name="input_back",
    )(grad, grad_middle, tokens, gain, *([] if total is None else [total]))


def per_device(
    hidden_in,
    cotangent,
    block_ids,
    attn_routes,
    mlp_routes,
    adapter_index,
    attn_gain,
    mlp_gain,
    attn_router,
    mlp_router,
    kv_weight,
    query_weight,
    output_weight,
    inner_weight,
    down_weight,
    adapt_down,
    adapt_up,
):
    seqs, row_count, width = hidden_in.shape
    seq_len = block_ids.shape[1]
    ranks = seq_len // row_count
    locals_ = query_weight.shape[0]
    capacity = (17 * row_count * TOP + 16 * EXPERTS - 1) // (16 * EXPERTS)
    slots = ranks * capacity
    here = lax.axis_index("expert")

    query_column = 2 * width
    output_column = query_column + locals_ * width
    near = jnp.concatenate(
        [kv_weight]
        + [query_weight[l] for l in range(locals_)]
        + [output_weight[l] for l in range(locals_)],
        axis=1,
    )
    near_full = lax.all_gather(near, "dp", axis=0, tiled=True)
    down_full = lax.all_gather(down_weight, "dp", axis=1, tiled=True)
    groups = width // kv_weight.shape[0]

    def stretch(array, l, low, high):
        return jnp.concatenate([array[l, :, low:high], array[l, :, FF + low : FF + high]], axis=1)

    inner_full, beside = [], []
    for l in range(locals_):
        pieces = []
        cut = 3 * 512 if l + 1 < locals_ else FF * 3 // 4 // 512 * 512
        if l + 1 < locals_:
            pieces.append((0, None))
            beside.append(stretch(inner_weight, l, 0, cut))
        else:
            pieces.append((0, lax.all_gather(stretch(inner_weight, l, 0, cut), "dp", axis=0, tiled=True)))
        pieces.append((cut, lax.all_gather(stretch(inner_weight, l, cut, FF), "dp", axis=0, tiled=True)))
        inner_full.append(pieces)

    routes = lax.all_gather(
        jnp.concatenate([attn_routes, mlp_routes], axis=-1), "expert", axis=1, tiled=True
    ).reshape(seqs, ranks, row_count, 2, TOP)
    adapters = lax.all_gather(adapter_index, "dp", axis=0, tiled=True)
    expert_ids = jnp.arange(EXPERTS, dtype=jnp.int32)
    onehot = (routes[..., None] == expert_ids).astype(F32)
    hits = jnp.sum(onehot, axis=4)
    earlier = (
        jnp.arange(row_count)[:, None] > jnp.arange(row_count)[None, :]
    ).astype(BF16)
    before = jnp.einsum("ut,sptke->spuke", earlier, hits.astype(BF16), preferred_element_type=F32)
    place = jnp.sum(onehot * before[..., None, :], axis=-1).astype(jnp.int32)
    attn_all, mlp_all = routes[:, :, :, 0], routes[:, :, :, 1]
    attn_place, mlp_place = place[:, :, :, 0], place[:, :, :, 1]
    source = jnp.arange(ranks, dtype=jnp.int32)[None, :, None, None]
    which = jnp.arange(seqs, dtype=jnp.int32)[:, None, None, None]

    local_a = attn_all - here * locals_
    is_local = (local_a >= 0) & (local_a < locals_)
    slot_a = jnp.where(is_local, local_a * slots + source * capacity + attn_place, -1)
    slot_a = slot_a.reshape(seqs, seq_len, TOP)
    slot_iota = jnp.arange(locals_ * slots, dtype=jnp.int32)
    spread_a = (
        (slot_iota[None, :, None] == slot_a[:, None, :, 0])
        | (slot_iota[None, :, None] == slot_a[:, None, :, 1])
    ).astype(BF16)
    collect_a = (
        (slot_iota[None, None, :] == slot_a[:, :, 0, None])
        | (slot_iota[None, None, :] == slot_a[:, :, 1, None])
    ).astype(BF16)

    def own(array):
        return lax.dynamic_index_in_dim(array, here, 1, keepdims=False)

    attn_own, attn_own_place = own(attn_all), own(attn_place)
    mlp_own, mlp_own_place = own(mlp_all), own(mlp_place)
    own_slot = attn_own * capacity + attn_own_place
    own_iota = jnp.arange(EXPERTS * capacity, dtype=jnp.int32)
    own_spread_a = (
        (own_iota[None, :, None] == own_slot[:, None, :, 0])
        | (own_iota[None, :, None] == own_slot[:, None, :, 1])
    ).astype(BF16)
    own_collect_a = (
        (own_iota[None, None, :] == own_slot[:, :, 0, None])
        | (own_iota[None, None, :] == own_slot[:, :, 1, None])
    ).astype(BF16)
    mlp_rows = ranks * seqs * capacity
    mlp_iota = jnp.arange(mlp_rows, dtype=jnp.int32)
    own_spread_m, own_collect_m, other_sum = [], [], []
    for l in range(locals_):
        ids = jnp.where(
            mlp_own % locals_ == l,
            (mlp_own // locals_) * (seqs * capacity) + which[:, 0] * capacity + mlp_own_place,
            -1,
        ).reshape(seqs * row_count, TOP)
        own_spread_m.append(
            ((mlp_iota[:, None] == ids[None, :, 0]) | (mlp_iota[:, None] == ids[None, :, 1])).astype(BF16)
        )
        own_collect_m.append(
            ((mlp_iota[None, :] == ids[:, 0, None]) | (mlp_iota[None, :] == ids[:, 1, None])).astype(BF16)
        )
        ids = jnp.where(
            mlp_all == here * locals_ + l,
            source * (seqs * capacity) + which * capacity + mlp_place,
            -1,
        ).reshape(seqs * seq_len, TOP)
        table = (
            (mlp_iota[:, None] == ids[None, :, 0]) | (mlp_iota[:, None] == ids[None, :, 1])
        ).astype(BF16)
        both = jnp.sum(mlp_all, axis=-1).reshape(seqs * seq_len, 1).astype(BF16)
        sums = mm(table, jnp.concatenate([both, jnp.ones_like(both)], axis=1))
        other_sum.append((sums[:, :1], sums[:, 1:]))

    hidden_first, routes, adapters = lax.optimization_barrier((hidden_in, routes, adapters))
    everyone = gather_line(
        hidden_first,
        "expert",
        ranks,
        lambda total, piece, at: lax.dynamic_update_slice(total, piece[:, None], (0, at, 0, 0)),
        jnp.zeros((seqs, ranks, row_count, width), BF16),
    ).reshape(seqs, seq_len, width)

    flat_cot, everyone = lax.optimization_barrier((cotangent, everyone))
    orders = halves_bits(groups)
    beside = [[block[: block.shape[0] // 2], block[block.shape[0] // 2 :]] for block in beside]

    def exchange_all(step):
        return [
            [exchange(half, "dp", groups, bits[step]) for half, bits in zip(halves, orders)]
            for halves in beside
        ]

    flat_cot = flat_cot.reshape(seqs * row_count, width)
    cot_rows = [send(mm(own_spread_m[l], flat_cot).astype(BF16)) for l in range(locals_)]

    tokens_all = everyone.astype(F32)
    scale_all = rms_scale(tokens_all)
    normed_low = (tokens_all * scale_all * attn_gain).astype(BF16)
    router_parts = jnp.concatenate(three_parts(attn_gain[:, None] * attn_router.astype(F32)), axis=1)
    parts = mm(everyone.reshape(seqs * seq_len, width), router_parts).reshape(seqs, seq_len, 3, EXPERTS)
    logits = scale_all * (parts[:, :, 0] + (parts[:, :, 1] + parts[:, :, 2]))
    onehot_a = onehot[:, :, :, 0].reshape(seqs, seq_len, TOP, EXPERTS)
    gap = jnp.sum((onehot_a[:, :, 0] - onehot_a[:, :, 1]) * logits, axis=-1)

    flat_routes = attn_all.reshape(seqs, seq_len, TOP)
    places = jnp.arange(seq_len, dtype=jnp.int32)
    columns = [
        block_ids,
        jnp.broadcast_to(places // 128, block_ids.shape),
        jnp.broadcast_to(places % 128, block_ids.shape),
        jnp.sum(flat_routes, axis=-1),
        flat_routes[..., 0],
    ]
    known = jnp.stack([c.astype(BF16) for c in columns] + list(three_parts(gap)), axis=-1)
    known = jnp.einsum("srt,stc->src", spread_a, known, preferred_element_type=F32)
    known = known.reshape(seqs, locals_, slots, known.shape[-1]).transpose(1, 0, 2, 3)
    self_id = (here * locals_ + jnp.arange(locals_)).astype(F32)[:, None, None]
    slot_blocks = known[..., 0].astype(jnp.int32)
    slot_place = known[..., 1] * 128.0 + known[..., 2]
    slot_other = known[..., 3] - self_id
    slot_gap = known[..., 5] + (known[..., 6] + known[..., 7])
    slot_gap = jnp.where(known[..., 4] == self_id, slot_gap, -slot_gap)
    gate_a = jax.nn.sigmoid(slot_gap)
    expert_f = expert_ids.astype(F32)
    pick_a = (expert_f == self_id[..., None]).astype(F32) - (expert_f == slot_other[..., None]).astype(F32)
    weigh_a = pick_a * (gate_a * jax.nn.sigmoid(-slot_gap))[..., None]
    cos_q, sin_q = angle_tables(slot_place)
    cos_k, sin_k = angle_tables(places)
    query_blocks = slot_blocks[..., None]
    key_blocks = block_ids[:, None, :]

    flat_low = normed_low.reshape(seqs * seq_len, width)
    own_adapter = (
        jnp.arange(NADAPT * RANK, dtype=jnp.int32)[None, :] // RANK == adapter_index[:, None]
    )
    low_rank = mm(flat_low, adapt_down).reshape(seqs, seq_len, NADAPT * RANK)
    low_rank = jnp.where(own_adapter[:, None, :], low_rank, 0.0).astype(BF16)
    key_value = make_key_value(
        flat_low, low_rank.reshape(seqs * seq_len, -1), near_full, adapt_up, cos_k, sin_k, seqs
    ).reshape(seqs, seq_len, 2 * width)

    picked = jnp.einsum(
        "slrt,std->lsrd",
        spread_a.reshape(seqs, locals_, slots, seq_len),
        normed_low,
        preferred_element_type=F32,
    ).astype(BF16)
    beside, picked = lax.optimization_barrier((beside, picked))
    beside = exchange_all(0)
    queries = project(picked.reshape(locals_, seqs * slots, width), near_full, query_column)
    query_rot, attended, probs = attend(
        queries.reshape(locals_, seqs, slots, width), key_value, cos_q, sin_q, query_blocks, key_blocks
    )
    gate_rows = gate_a[..., None]
    projected, gated = project(
        attended.reshape(locals_, seqs * slots, width),
        near_full,
        output_column,
        gate_rows.reshape(locals_, seqs * slots, 1),
    )
    beside, projected = lax.optimization_barrier((beside, projected))
    for step in range(1, len(orders[0])):
        beside = exchange_all(step)
    for l, halves in enumerate(beside):
        inner_full[l][0] = (0, in_order(halves, orders, groups))
    projected = projected.reshape(locals_, seqs, slots, width)
    gated = gated.reshape(locals_, seqs, slots, width)
    order = np.arange(locals_ * slots).reshape(locals_, ranks, capacity).transpose(1, 0, 2).reshape(-1)
    to_send = jnp.asarray(np.eye(locals_ * slots)[order], BF16)
    to_slots = jnp.asarray(np.eye(locals_ * slots)[order].T, BF16)
    tokens = hidden_in.astype(F32)
    middles = []
    for s in range(seqs):
        back = send(mm(to_send, gated[:, s].reshape(locals_ * slots, width)).astype(BF16))
        middles.append(tokens[s] + mm(own_collect_a[s], back))
    middle = jnp.stack(middles)
    scale_two = rms_scale(middle)
    normed_two_low = (middle * scale_two * mlp_gain).astype(BF16).reshape(seqs * row_count, width)

    final = middle.reshape(seqs * row_count, width)
    grad_normed_two = jnp.zeros((seqs * row_count, width), F32)
    held = None
    for l in range(locals_):
        rows_in = send(mm(own_spread_m[l], normed_two_low).astype(BF16))
        slot_logits = mm(rows_in, mlp_router)
        me = (here * locals_ + l).astype(F32)
        pick_m = (expert_f[None, :] == me).astype(F32) - (
            expert_f[None, :] == other_sum[l][0] - me
        ).astype(F32)
        gate_m = jax.nn.sigmoid(jnp.sum(pick_m * slot_logits, axis=-1, keepdims=True))
        grad_rows = (gate_m * cot_rows[l].astype(F32)).astype(BF16)
        made = None
        for at, (low, inner) in enumerate(inner_full[l]):
            if held is not None and at + 1 == len(inner_full[l]):
                held, made = lax.optimization_barrier((held, made))
                final = final + mm(own_collect_m[l - 1], held)
            ends = (cot_rows[l], gate_m, pick_m, mlp_router) if at + 1 == len(inner_full[l]) else None
            made = expert_pass(rows_in, grad_rows, inner, down_full, l, low, made, ends)
        gated_out, grad_source = made
        grad_back = send(grad_source)
        if l + 1 < locals_:
            grad_normed_two = grad_normed_two + mm(own_collect_m[l], grad_back)
        held = send(gated_out) if l + 1 < locals_ else gated_out
    grad_normed_two = grad_normed_two.reshape(seqs, row_count, width)
    late = (collect_a, own_adapter.astype(F32)[:, None, :], weigh_a, attn_router, to_slots)
    (collect_a, mask, weigh_a, router_near, to_slots), grad_normed_two = lax.optimization_barrier(
        (late, grad_normed_two)
    )
    back_table = own_collect_m[locals_ - 1].reshape(seqs, row_count, mlp_rows)
    grad_middle, leaving = [], []
    for s in range(seqs):
        grad, rows = middle_back(
            s, grad_back, back_table, grad_normed_two, middle, cotangent, mlp_gain[None], own_spread_a
        )
        grad_middle.append(grad)
        leaving.append(rows)

    arrived = [send(leaving[0])]
    arrived[0], held, leaving[1:] = lax.optimization_barrier((arrived[0], held, leaving[1:]))
    held = send(held)
    down_pieces, up_pieces = [], []
    input_grad = None
    for s in range(seqs):
        grad_attended, dots = out_back(
            s, arrived[s], to_slots, gate_rows, projected, near_full, output_column
        )
        dq, dk, dv = attend_back(s, query_rot, key_value, grad_attended, probs, cos_q, sin_q, cos_k, sin_k)
        if s + 1 < seqs:
            leaving[s + 1], held, dk = lax.optimization_barrier((leaving[s + 1], held, dk))
            arrived.append(send(leaving[s + 1]))
        part, grad_low = last_grad(
            s, dk, dv, dq, collect_a, dots, weigh_a, mask, adapt_up, router_near, adapt_down, near_full,
            query_column,
        )
        if s + 1 < seqs:
            arrived[s + 1], part = lax.optimization_barrier((arrived[s + 1], part))
        grad_normed = lax.psum_scatter(part, "expert", scatter_dimension=0, tiled=True)
        input_grad = input_back(s, grad_normed, grad_middle[s], hidden_in, attn_gain[None], input_grad)
        first = adapter_index[s] * RANK
        down_pieces.append(lax.dynamic_slice_in_dim(mm(grad_low, normed_low[s], TN), first, RANK, 0))
        up_piece = jnp.concatenate([mm(low_rank[s], dk, TN), mm(low_rank[s], dv, TN)], axis=1)
        up_pieces.append(lax.dynamic_slice_in_dim(up_piece, first, RANK, 0))
    final = final + mm(own_collect_m[locals_ - 1], held)
    layer_out = final.astype(BF16).reshape(seqs, row_count, width)

    down_part = width // (groups * ranks)
    pieces = jnp.concatenate(
        [
            jnp.stack(down_pieces).reshape(seqs * RANK, groups, ranks, down_part),
            jnp.stack(up_pieces).reshape(seqs * RANK, groups, ranks, 2 * down_part),
        ],
        axis=-1,
    )
    pieces = pieces.transpose(1, 0, 2, 3).reshape(groups, seqs * RANK, 3 * ranks * down_part)
    pieces = lax.all_to_all(pieces, "dp", split_axis=0, concat_axis=0, tiled=True)
    pieces = pieces.reshape(groups * seqs, RANK, 3 * ranks * down_part)
    belongs = (adapters[:, None] == jnp.arange(NADAPT, dtype=jnp.int32)[None, :]).astype(F32)
    sums = jnp.einsum("qkf,qa->akf", pieces, belongs, precision=PRECISE)
    sums = sums.reshape(NADAPT * RANK, ranks, 3 * down_part).transpose(1, 0, 2)
    sums = jnp.sum(send(sums), axis=0).T
    return (layer_out, input_grad, sums[:down_part], sums[down_part:])


def solution(mesh):
    return jax.shard_map(
        per_device,
        mesh=mesh,
        in_specs=(
            P("dp", "expert", None),
            P("dp", "expert", None),
            P("dp", None),
            P("dp", "expert", None),
            P("dp", "expert", None),
            P("dp"),
            P(),
            P(),
            P(),
            P(),
            P("dp", None),
            P("expert", "dp", None),
            P("expert", "dp", None),
            P("expert", "dp", None),
            P("expert", "dp", None),
            P(),
            P(),
        ),
        out_specs=(
            P("dp", "expert", None),
            P("dp", "expert", None),
            P(("dp", "expert"), None),
            P(("dp", "expert"), None),
        ),
        check_vma=False,
    )
```

```python
import functools
import math

import jax
import jax.numpy as jnp
import numpy as np
from jax import lax
from jax.experimental import pallas as pl
from jax.experimental.pallas import tpu as pltpu
from jax.sharding import PartitionSpec as P

HEADS = 16
HDIM = 128
FF = 5632
EXPERTS = 8
TOP = 2
RANK = 16
NADAPT = 8

PRECISE = lax.Precision.HIGHEST
EPSILON = 1e-06
ROPE_BASE = 10000.0
MASKED_SCORE = -1e30
SCALE_QK = 1.0 / math.sqrt(HDIM)
BF16 = jnp.bfloat16
F32 = jnp.float32
VMEM_LIMIT = 58 * 1024 * 1024

NN = (((1,), (0,)), ((), ()))
NT = (((1,), (1,)), ((), ()))
TN = (((0,), (0,)), ((), ()))


def mm(left, right, dims=NN):
    return lax.dot_general(left, right, dims, preferred_element_type=F32)


def params(*semantics):
    return pltpu.CompilerParams(dimension_semantics=semantics, vmem_limit_bytes=VMEM_LIMIT)


def once(shape, index_map):
    return pl.BlockSpec(shape, index_map, pipeline_mode=pl.Buffered(1))


def rms_scale(values):
    return lax.rsqrt(jnp.mean(values * values, axis=-1, keepdims=True) + EPSILON)


def norm_back(values, scale_rows, norm_gain, grad_rows):
    scaled_grad = norm_gain * grad_rows
    return scale_rows * (
        scaled_grad
        - values * scale_rows * scale_rows * jnp.mean(scaled_grad * values, axis=-1, keepdims=True)
    )


def angle_tables(positions):
    half_dim = HDIM // 2
    frequency = ROPE_BASE ** (-(jnp.arange(half_dim, dtype=F32) * (2.0 / HDIM)))
    frequency = jnp.concatenate([frequency, frequency])
    sign = jnp.concatenate([-jnp.ones((half_dim,), F32), jnp.ones((half_dim,), F32)])
    angles = positions.astype(F32)[..., None] * frequency
    return (jnp.cos(angles), jnp.sin(angles) * sign)


def three_parts(values):
    first = values.astype(BF16)
    rest = values - first.astype(F32)
    second = rest.astype(BF16)
    third = (rest - second.astype(F32)).astype(BF16)
    return first, second, third


def gather_line(block, axis, size, put, start):
    here = lax.axis_index(axis)
    rightward = [(i, i + 1) for i in range(size - 1)]
    leftward = [(i + 1, i) for i in range(size - 1)]
    from_left, from_right = [block], [block]
    for _ in range(size - 1):
        from_left.append(lax.ppermute(from_left[-1], axis, rightward))
        from_right.append(lax.ppermute(from_right[-1], axis, leftward))
    total = put(start, block, here)
    for step in range(1, size):
        piece = jnp.where(here >= step, from_left[step], from_right[size - step])
        total = put(total, piece, lax.rem(here - step + size, size))
    return total


def exchange(total, axis, size, bit):
    other = lax.ppermute(total, axis, [(i, i ^ bit) for i in range(size)])
    low = jnp.bitwise_and(lax.axis_index(axis), bit) == 0
    return jnp.stack([jnp.where(low, total, other), jnp.where(low, other, total)])


def halves_bits(size):
    bits = [1 << k for k in range(1, size.bit_length() - 1)]
    return [bits + [1], bits[::-1] + [1]]


def in_order(halves, orders, size):
    made = []
    for total, bits in zip(halves, orders):
        count = len(bits)
        order = sorted(range(count), key=lambda d: -bits[count - 1 - d])
        total = total.transpose(*order, *range(count, total.ndim))
        made.append(total.reshape(size, *total.shape[count:]))
    whole = jnp.stack(made, axis=1)
    return whole.reshape(-1, whole.shape[-1])


def send(buffer):
    return lax.all_to_all(buffer, "expert", split_axis=0, concat_axis=0, tiled=True)


def kv_body(seqs, seq_len, key_tiles, x_ref, low_ref, w_ref, up_ref, cos_ref, sin_ref, out_ref):
    is_key = pl.program_id(0) < key_tiles
    for s in range(seqs):
        rows = pl.ds(s * seq_len, seq_len)
        made = mm(x_ref[rows, :], w_ref[...]) + mm(low_ref[rows, :], up_ref[...], NT)

        @pl.when(is_key)
        def _(made=made, rows=rows):
            for h in range(made.shape[1] // HDIM):
                cols = slice(h * HDIM, (h + 1) * HDIM)
                part = made[:, cols]
                turned = part * cos_ref[...] + pltpu.roll(part, HDIM // 2, 1) * sin_ref[...]
                out_ref[rows, cols] = turned.astype(BF16)

        @pl.when(jnp.logical_not(is_key))
        def _(made=made, rows=rows):
            out_ref[rows, :] = made.astype(BF16)


def make_key_value(normed_low, low_rank, weights, adapt_up, cos_k, sin_k, seqs):
    rows, width = normed_low.shape
    seq_len = rows // seqs
    tile = 512
    return pl.pallas_call(
        functools.partial(kv_body, seqs, seq_len, width // tile),
        grid=(2 * width // tile,),
        in_specs=[
            once((rows, width), lambda i: (0, 0)),
            once((rows, low_rank.shape[1]), lambda i: (0, 0)),
            pl.BlockSpec((width, tile), lambda i: (0, i)),
            pl.BlockSpec((tile, low_rank.shape[1]), lambda i: (i, 0)),
            once((seq_len, HDIM), lambda i: (0, 0)),
            once((seq_len, HDIM), lambda i: (0, 0)),
        ],
        out_specs=pl.BlockSpec((rows, tile), lambda i: (0, i)),
        out_shape=jax.ShapeDtypeStruct((rows, 2 * width), BF16),
        compiler_params=params("arbitrary"),
        name="key_value",
    )(normed_low, low_rank, weights, adapt_up, cos_k, sin_k)


def project_body(x_ref, w_ref, *refs):
    made = mm(x_ref[...], w_ref[...])
    if len(refs) == 1:
        refs[0][...] = made.astype(BF16)
    else:
        gate_ref, out_ref, gated_ref = refs
        out_ref[...] = made.astype(BF16)
        gated_ref[...] = (made * gate_ref[...]).astype(BF16)


def project(values, weights, from_column, gate=None):
    locals_, rows, width = values.shape
    tile = 512
    first, step = from_column // tile, width // tile
    out_spec = pl.BlockSpec((None, rows, tile), lambda l, i: (l, 0, i))
    out_shape = jax.ShapeDtypeStruct(values.shape, BF16)
    in_specs = [
        pl.BlockSpec((None, rows, width), lambda l, i: (l, 0, 0)),
        pl.BlockSpec((width, tile), lambda l, i: (0, first + step * l + i)),
    ]
    more = []
    if gate is not None:
        in_specs.append(pl.BlockSpec((None, rows, 1), lambda l, i: (l, 0, 0)))
        more = [gate]
    return pl.pallas_call(
        project_body,
        grid=(locals_, step),
        in_specs=in_specs,
        out_specs=out_spec if gate is None else [out_spec] * 2,
        out_shape=out_shape if gate is None else [out_shape] * 2,
        compiler_params=params("arbitrary", "arbitrary"),
        name="project",
    )(values, weights, *more)


def attend_body(q_ref, k_ref, v_ref, cos_ref, sin_ref, qb_ref, kb_ref, rot_ref, out_ref, probs_ref):
    locals_, _, slots, _ = q_ref.shape
    rows = locals_ * slots
    q = q_ref[...].reshape(rows, HDIM).astype(F32)
    cos, sin = cos_ref[...].reshape(rows, HDIM), sin_ref[...].reshape(rows, HDIM)
    rot = (q * cos + pltpu.roll(q, HDIM // 2, 1) * sin).astype(BF16)
    rot_ref[...] = rot.reshape(rot_ref.shape)
    k, v = k_ref[0], v_ref[0]
    kb = kb_ref[0]
    for l in range(locals_):
        part = rot[l * slots : (l + 1) * slots]
        visible = kb <= qb_ref[l, 0]
        masked = jnp.where(visible, mm(part, k, NT), MASKED_SCORE)
        top = jnp.max(masked, axis=-1, keepdims=True)
        terms = jnp.exp((masked - top) * SCALE_QK)
        total = jnp.sum(terms, axis=-1, keepdims=True)
        probs = (terms * (1.0 / total)).astype(BF16)
        probs_ref[l, 0, 0] = probs
        out_ref[l, 0] = mm(probs, v).astype(BF16)


def attend(queries, key_value, cos_q, sin_q, query_blocks, key_blocks):
    locals_, seqs, slots, width = queries.shape
    seq_len = key_value.shape[1]
    q_spec = pl.BlockSpec((locals_, 1, slots, HDIM), lambda s, h: (0, s, 0, h))
    tab_spec = pl.BlockSpec((locals_, 1, slots, HDIM), lambda s, h: (0, s, 0, 0))
    return pl.pallas_call(
        attend_body,
        grid=(seqs, HEADS),
        in_specs=[
            q_spec,
            pl.BlockSpec((1, seq_len, HDIM), lambda s, h: (s, 0, h)),
            pl.BlockSpec((1, seq_len, HDIM), lambda s, h: (s, 0, HEADS + h)),
            tab_spec,
            tab_spec,
            pl.BlockSpec((locals_, 1, slots, 1), lambda s, h: (0, s, 0, 0)),
            pl.BlockSpec((1, 1, seq_len), lambda s, h: (s, 0, 0)),
        ],
        out_specs=[
            q_spec,
            q_spec,
            pl.BlockSpec((locals_, 1, 1, slots, seq_len), lambda s, h: (0, s, h, 0, 0)),
        ],
        out_shape=[
            jax.ShapeDtypeStruct(queries.shape, BF16),
            jax.ShapeDtypeStruct(queries.shape, BF16),
            jax.ShapeDtypeStruct((locals_, seqs, HEADS, slots, seq_len), BF16),
        ],
        compiler_params=params("arbitrary", "arbitrary"),
        name="attend",
    )(queries, key_value, key_value, cos_q, sin_q, query_blocks, key_blocks)


def attend_back_body(q_ref, k_ref, v_ref, g_ref, p_ref, cos_ref, sin_ref, ck_ref, sk_ref, dq_ref, dk_ref, dv_ref):
    locals_, _, slots, _ = q_ref.shape
    rows = locals_ * slots
    k, v = k_ref[0], v_ref[0]
    q = q_ref[...].reshape(rows, HDIM)
    grad = g_ref[...].reshape(rows, HDIM)
    probs = p_ref[...].reshape(rows, k.shape[0])
    weighed = probs.astype(F32) * mm(grad, v, NT)
    delta = jnp.sum(weighed, axis=-1, keepdims=True)
    grad_scores = (weighed - probs.astype(F32) * delta).astype(BF16)
    dq = mm(grad_scores, k) * SCALE_QK
    cos, sin = cos_ref[...].reshape(rows, HDIM), sin_ref[...].reshape(rows, HDIM)
    dq = dq * cos - pltpu.roll(dq, HDIM // 2, 1) * sin
    dq_ref[...] = dq.astype(BF16).reshape(dq_ref.shape)
    dk = mm(grad_scores, q, TN) * SCALE_QK
    dk_ref[...] = (dk * ck_ref[...] - pltpu.roll(dk, HDIM // 2, 1) * sk_ref[...]).astype(BF16)
    dv_ref[...] = mm(probs, grad, TN).astype(BF16)


def attend_back(s, query_rot, key_value, grad, probs, cos_q, sin_q, cos_k, sin_k):
    locals_, _, slots, width = query_rot.shape
    seq_len = key_value.shape[1]
    tab_spec = pl.BlockSpec((locals_, 1, slots, HDIM), lambda h: (0, s, 0, 0))
    key_tab = pl.BlockSpec((seq_len, HDIM), lambda h: (0, 0))
    grad_spec = pl.BlockSpec((locals_, slots, HDIM), lambda h: (0, 0, h))
    key_spec = pl.BlockSpec((seq_len, HDIM), lambda h: (0, h))
    return pl.pallas_call(
        attend_back_body,
        grid=(HEADS,),
        in_specs=[
            pl.BlockSpec((locals_, 1, slots, HDIM), lambda h: (0, s, 0, h)),
            pl.BlockSpec((1, seq_len, HDIM), lambda h: (s, 0, h)),
            pl.BlockSpec((1, seq_len, HDIM), lambda h: (s, 0, HEADS + h)),
            grad_spec,
            pl.BlockSpec((locals_, 1, 1, slots, seq_len), lambda h: (0, s, h, 0, 0)),
            tab_spec,
            tab_spec,
            key_tab,
            key_tab,
        ],
        out_specs=[grad_spec, key_spec, key_spec],
        out_shape=[
            jax.ShapeDtypeStruct((locals_, slots, width), BF16),
            jax.ShapeDtypeStruct((seq_len, width), BF16),
            jax.ShapeDtypeStruct((seq_len, width), BF16),
        ],
        compiler_params=params("arbitrary"),
        name="attend_back",
    )(query_rot, key_value, key_value, grad, probs, cos_q, sin_q, cos_k, sin_k)


def expert_body(has_start, is_last, x_ref, c_ref, wg_ref, wu_ref, wd_ref, *refs):
    refs = list(refs)
    start = [refs.pop(0), refs.pop(0)] if has_start else []
    if is_last:
        cot_ref, gate_ref, pick_ref, router_ref, low_ref, back_ref, out_ref, gs_ref = refs[:8]
        late = start + [cot_ref]
    else:
        out_ref, gs_ref = refs[:2]
        late = start
    count = len(late)
    held, sem = (refs[-count - 1 : -1], refs[-1]) if count else ([], None)
    copies = [pltpu.make_async_copy(late[i], held[i], sem.at[i]) for i in range(count)]

    @pl.when(pl.program_id(0) == 0)
    def _():
        for copy in copies:
            copy.start()
        out_ref[...] = jnp.zeros_like(out_ref)
        gs_ref[...] = jnp.zeros_like(gs_ref)

    x, c = x_ref[...], c_ref[...]
    wg, wu, wd = wg_ref[...], wu_ref[...], wd_ref[...]
    gate, up = mm(x, wg), mm(x, wu)
    sig = jax.nn.sigmoid(gate)
    silu = gate * sig
    out_ref[...] += mm((silu * up).astype(BF16), wd)
    grad = mm(c, wd, NT)
    grad_gate = (grad * up * sig * (1.0 + gate * (1.0 - sig))).astype(BF16)
    grad_up = (grad * silu).astype(BF16)
    gs_ref[...] += mm(grad_gate, wg, NT) + mm(grad_up, wu, NT)

    @pl.when(pl.program_id(0) == pl.num_programs(0) - 1)
    def _():
        for copy in copies:
            copy.wait()
        made, back = out_ref[...], gs_ref[...]
        if has_start:
            made, back = made + held[0][...], back + held[1][...]
        if has_start and not is_last:
            out_ref[...] = made
            gs_ref[...] = back
        if is_last:
            share = gate_ref[...]
            dots = jnp.sum(held[-1][...].astype(F32) * made, axis=-1, keepdims=True)
            weigh = pick_ref[...] * (dots * share * (1.0 - share))
            high = weigh.astype(BF16)
            low = (weigh - high.astype(F32)).astype(BF16)
            router = router_ref[...]
            back_ref[...] = (back + mm(high, router, NT) + mm(low, router, NT)).astype(BF16)
            low_ref[...] = (share * made).astype(BF16)


def expert_pass(rows_in, grad_in, inner, down, l, down_from, start=None, last=None):
    rows, width = rows_in.shape
    units = inner.shape[1] // 2
    tile = 512 if units % 512 == 0 and down_from % 512 == 0 else 256
    first = down_from // tile

    def whole(array):
        return once(array.shape, lambda i: (0,) * array.ndim)

    more = ([] if start is None else list(start)) + ([] if last is None else list(last))
    kind = F32 if last is None else BF16
    late = ([] if start is None else [F32, F32]) + ([] if last is None else [BF16])
    away = len(late)
    scratch = [] if last is None else [pltpu.VMEM((rows, width), F32)] * 2
    if away:
        scratch += [pltpu.VMEM((rows, width), t) for t in late] + [pltpu.SemaphoreType.DMA((away,))]
    return pl.pallas_call(
        functools.partial(expert_body, start is not None, last is not None),
        grid=(units // tile,),
        in_specs=[
            whole(rows_in),
            whole(grad_in),
            pl.BlockSpec((width, tile), lambda i: (0, i)),
            pl.BlockSpec((width, tile), lambda i: (0, units // tile + i)),
            pl.BlockSpec((None, tile, width), lambda i: (l, first + i, 0)),
        ]
        + [pl.BlockSpec(memory_space=pl.ANY) if i < away else whole(m) for i, m in enumerate(more)],
        out_specs=[pl.BlockSpec((rows, width), lambda i: (0, 0))] * 2,
        out_shape=[jax.ShapeDtypeStruct((rows, width), kind)] * 2,
        scratch_shapes=scratch,
        compiler_params=params("arbitrary"),
        name="expert",
    )(rows_in, grad_in, inner, inner, down, *more)


def out_back_body(locals_, arrived_ref, order_ref, gate_ref, projected_ref, *refs):
    w_refs, (out_ref, dots_ref, rows_ref) = refs[:locals_], refs[locals_:]
    slots = projected_ref.shape[1]

    @pl.when(pl.program_id(0) == 0)
    def _():
        for l in range(locals_):
            rows = mm(order_ref[pl.ds(l * slots, slots), :], arrived_ref[...])
            dots_ref[l] = jnp.sum(rows * projected_ref[l].astype(F32), axis=-1, keepdims=True)
            rows_ref[l] = (rows * gate_ref[l]).astype(BF16)

    for l in range(locals_):
        out_ref[l] = mm(rows_ref[l], w_refs[l][...], NT).astype(BF16)


def out_back(s, arrived, order, gate, projected, weights, from_column):
    locals_, slots = gate.shape[0], gate.shape[2]
    rows, width = arrived.shape
    tile = 512
    return pl.pallas_call(
        functools.partial(out_back_body, locals_),
        grid=(width // tile,),
        in_specs=[
            once((rows, width), lambda i: (0, 0)),
            once((rows, rows), lambda i: (0, 0)),
            once((locals_, None, slots, 1), lambda i: (0, s, 0, 0)),
            once((locals_, None, slots, width), lambda i: (0, s, 0, 0)),
        ]
        + [
            pl.BlockSpec((tile, width), lambda i, l=l: (i, from_column // width + l))
            for l in range(locals_)
        ],
        out_specs=[
            pl.BlockSpec((locals_, slots, tile), lambda i: (0, 0, i)),
            pl.BlockSpec((locals_, slots, 1), lambda i: (0, 0, 0)),
        ],
        out_shape=[
            jax.ShapeDtypeStruct((locals_, slots, width), BF16),
            jax.ShapeDtypeStruct((locals_, slots, 1), F32),
        ],
        scratch_shapes=[pltpu.VMEM((locals_, slots, width), BF16)],
        compiler_params=params("arbitrary"),
        name="out_back",
    )(arrived, order, gate, projected, *([weights] * locals_))


def last_body(
    locals_, seq_len, dk_ref, dv_ref, dq_ref, table_ref, dots_ref, weigh_ref, mask_ref, up_ref, router_ref, down_ref, w_ref, *refs
):
    wq_refs, (out_ref, low_ref, source_ref, weigh_low_ref) = refs[:locals_], refs[locals_:]
    width = dk_ref.shape[1]
    slots = dq_ref.shape[1]

    @pl.when(pl.program_id(0) == 0)
    def _():
        low = mm(dk_ref[...], up_ref[:width, :]) + mm(dv_ref[...], up_ref[width:, :])
        low_ref[...] = (low * mask_ref[...]).astype(BF16)
        for l in range(locals_):
            weigh = weigh_ref[l] * dots_ref[l]
            high = weigh.astype(BF16)
            weigh_low_ref[l, :, :EXPERTS] = high
            weigh_low_ref[l, :, EXPERTS:] = (weigh - high.astype(F32)).astype(BF16)

    router = jnp.concatenate([router_ref[...]] * 2, axis=1)
    for l in range(locals_):
        source = mm(dq_ref[l], wq_refs[l][...], NT) + mm(weigh_low_ref[l], router, NT)
        source_ref[pl.ds(l * slots, slots), :] = source.astype(BF16)
    total = mm(dk_ref[...], w_ref[:, :width], NT) + mm(dv_ref[...], w_ref[:, width:], NT)
    total += mm(low_ref[...], down_ref[...], NT)
    total += mm(table_ref[0], source_ref[...])
    out_ref[...] = total.astype(BF16)


def last_grad(s, dk, dv, dq, table, dots, weigh, mask, adapt_up, router, adapt_down, weights, query_column):
    seq_len, width = dk.shape
    locals_, slots, _ = dq.shape
    tile = 256
    ranks = adapt_up.shape[1]
    return pl.pallas_call(
        functools.partial(last_body, locals_, seq_len),
        grid=(width // tile,),
        in_specs=[
            once((seq_len, width), lambda i: (0, 0)),
            once((seq_len, width), lambda i: (0, 0)),
            once((locals_, slots, width), lambda i: (0, 0, 0)),
            once((1, seq_len, locals_ * slots), lambda i: (s, 0, 0)),
            once((locals_, slots, 1), lambda i: (0, 0, 0)),
            once((locals_, None, slots, EXPERTS), lambda i: (0, s, 0, 0)),
            once((None, 1, ranks), lambda i: (s, 0, 0)),
            once((2 * width, ranks), lambda i: (0, 0)),
            pl.BlockSpec((tile, EXPERTS), lambda i: (i, 0)),
            pl.BlockSpec((tile, ranks), lambda i: (i, 0)),
            pl.BlockSpec((tile, 2 * width), lambda i: (i, 0)),
        ]
        + [
            pl.BlockSpec((tile, width), lambda i, l=l: (i, query_column // width + l))
            for l in range(locals_)
        ],
        out_specs=[
            pl.BlockSpec((seq_len, tile), lambda i: (0, i)),
            pl.BlockSpec((seq_len, ranks), lambda i: (0, 0)),
        ],
        out_shape=[
            jax.ShapeDtypeStruct((seq_len, width), BF16),
            jax.ShapeDtypeStruct((seq_len, ranks), BF16),
        ],
        scratch_shapes=[
            pltpu.VMEM((locals_ * slots, tile), BF16),
            pltpu.VMEM((locals_, slots, 2 * EXPERTS), BF16),
        ],
        compiler_params=params("arbitrary"),
        name="last_grad",
    )(dk, dv, dq, table, dots, weigh, mask, adapt_up, router, adapt_down, weights, *([weights] * locals_))


def middle_back_body(back_ref, table_ref, part_ref, middle_ref, cot_ref, gain_ref, spread_ref, out_ref, rows_ref):
    middle = middle_ref[...]
    scale = rms_scale(middle)
    grad = part_ref[...] + mm(table_ref[...], back_ref[...])
    out = cot_ref[...].astype(F32) + norm_back(middle, scale, gain_ref[...], grad)
    out_ref[...] = out
    rows_ref[...] = mm(spread_ref[...], out.astype(BF16)).astype(BF16)


def middle_back(s, back, table, part, middle, cotangent, gain, spread):
    _, rows, width = middle.shape
    slots = spread.shape[1]

    def one(array):
        return once((None, *array.shape[1:]), lambda i: (s, 0, 0))

    return pl.pallas_call(
        middle_back_body,
        grid=(1,),
        in_specs=[
            once(back.shape, lambda i: (0, 0)),
            one(table),
            one(part),
            one(middle),
            one(cotangent),
            once(gain.shape, lambda i: (0, 0)),
            one(spread),
        ],
        out_specs=[once((rows, width), lambda i: (0, 0)), once((slots, width), lambda i: (0, 0))],
        out_shape=[
            jax.ShapeDtypeStruct((rows, width), F32),
            jax.ShapeDtypeStruct((slots, width), BF16),
        ],
        compiler_params=params("arbitrary"),
        name="middle_back",
    )(back, table, part, middle, cotangent, gain, spread)


def input_back_body(grad_ref, middle_ref, tokens_ref, gain_ref, *refs):
    tokens = tokens_ref[...].astype(F32)
    refs[-1][...] = middle_ref[...] + norm_back(
        tokens, rms_scale(tokens), gain_ref[...], grad_ref[...].astype(F32)
    )


def input_back(s, grad, grad_middle, tokens, gain, total):
    seqs, rows, width = tokens.shape
    tile = 128
    flat = pl.BlockSpec((tile, width), lambda i: (i, 0))
    one = pl.BlockSpec((None, tile, width), lambda i: (s, i, 0))
    return pl.pallas_call(
        input_back_body,
        grid=(rows // tile,),
        in_specs=[flat, flat, one, pl.BlockSpec((1, width), lambda i: (0, 0))]
        + ([] if total is None else [pl.BlockSpec(memory_space=pl.ANY)]),
        out_specs=one,
        out_shape=jax.ShapeDtypeStruct(tokens.shape, F32),
        input_output_aliases={} if total is None else {4: 0},
        compiler_params=params("arbitrary"),
        name="input_back",
    )(grad, grad_middle, tokens, gain, *([] if total is None else [total]))


def per_device(
    hidden_in,
    cotangent,
    block_ids,
    attn_routes,
    mlp_routes,
    adapter_index,
    attn_gain,
    mlp_gain,
    attn_router,
    mlp_router,
    kv_weight,
    query_weight,
    output_weight,
    inner_weight,
    down_weight,
    adapt_down,
    adapt_up,
):
    seqs, row_count, width = hidden_in.shape
    seq_len = block_ids.shape[1]
    ranks = seq_len // row_count
    locals_ = query_weight.shape[0]
    capacity = (17 * row_count * TOP + 16 * EXPERTS - 1) // (16 * EXPERTS)
    slots = ranks * capacity
    here = lax.axis_index("expert")

    query_column = 2 * width
    output_column = query_column + locals_ * width
    near = jnp.concatenate(
        [kv_weight]
        + [query_weight[l] for l in range(locals_)]
        + [output_weight[l] for l in range(locals_)],
        axis=1,
    )
    near_full = lax.all_gather(near, "dp", axis=0, tiled=True)
    down_full = lax.all_gather(down_weight, "dp", axis=1, tiled=True)
    groups = width // kv_weight.shape[0]

    def stretch(array, l, low, high):
        return jnp.concatenate([array[l, :, low:high], array[l, :, FF + low : FF + high]], axis=1)

    inner_full, beside = [], []
    for l in range(locals_):
        pieces = []
        cut = 3 * 512 if l + 1 < locals_ else FF * 3 // 4 // 512 * 512
        if l + 1 < locals_:
            pieces.append((0, None))
            beside.append(stretch(inner_weight, l, 0, cut))
        else:
            pieces.append((0, lax.all_gather(stretch(inner_weight, l, 0, cut), "dp", axis=0, tiled=True)))
        pieces.append((cut, lax.all_gather(stretch(inner_weight, l, cut, FF), "dp", axis=0, tiled=True)))
        inner_full.append(pieces)

    routes = lax.all_gather(
        jnp.concatenate([attn_routes, mlp_routes], axis=-1), "expert", axis=1, tiled=True
    ).reshape(seqs, ranks, row_count, 2, TOP)
    adapters = lax.all_gather(adapter_index, "dp", axis=0, tiled=True)
    expert_ids = jnp.arange(EXPERTS, dtype=jnp.int32)
    onehot = (routes[..., None] == expert_ids).astype(F32)
    hits = jnp.sum(onehot, axis=4)
    earlier = (
        jnp.arange(row_count)[:, None] > jnp.arange(row_count)[None, :]
    ).astype(BF16)
    before = jnp.einsum("ut,sptke->spuke", earlier, hits.astype(BF16), preferred_element_type=F32)
    place = jnp.sum(onehot * before[..., None, :], axis=-1).astype(jnp.int32)
    attn_all, mlp_all = routes[:, :, :, 0], routes[:, :, :, 1]
    attn_place, mlp_place = place[:, :, :, 0], place[:, :, :, 1]
    source = jnp.arange(ranks, dtype=jnp.int32)[None, :, None, None]
    which = jnp.arange(seqs, dtype=jnp.int32)[:, None, None, None]

    local_a = attn_all - here * locals_
    is_local = (local_a >= 0) & (local_a < locals_)
    slot_a = jnp.where(is_local, local_a * slots + source * capacity + attn_place, -1)
    slot_a = slot_a.reshape(seqs, seq_len, TOP)
    slot_iota = jnp.arange(locals_ * slots, dtype=jnp.int32)
    spread_a = (
        (slot_iota[None, :, None] == slot_a[:, None, :, 0])
        | (slot_iota[None, :, None] == slot_a[:, None, :, 1])
    ).astype(BF16)
    collect_a = (
        (slot_iota[None, None, :] == slot_a[:, :, 0, None])
        | (slot_iota[None, None, :] == slot_a[:, :, 1, None])
    ).astype(BF16)

    def own(array):
        return lax.dynamic_index_in_dim(array, here, 1, keepdims=False)

    attn_own, attn_own_place = own(attn_all), own(attn_place)
    mlp_own, mlp_own_place = own(mlp_all), own(mlp_place)
    own_slot = attn_own * capacity + attn_own_place
    own_iota = jnp.arange(EXPERTS * capacity, dtype=jnp.int32)
    own_spread_a = (
        (own_iota[None, :, None] == own_slot[:, None, :, 0])
        | (own_iota[None, :, None] == own_slot[:, None, :, 1])
    ).astype(BF16)
    own_collect_a = (
        (own_iota[None, None, :] == own_slot[:, :, 0, None])
        | (own_iota[None, None, :] == own_slot[:, :, 1, None])
    ).astype(BF16)
    mlp_rows = ranks * seqs * capacity
    mlp_iota = jnp.arange(mlp_rows, dtype=jnp.int32)
    own_spread_m, own_collect_m, other_sum = [], [], []
    for l in range(locals_):
        ids = jnp.where(
            mlp_own % locals_ == l,
            (mlp_own // locals_) * (seqs * capacity) + which[:, 0] * capacity + mlp_own_place,
            -1,
        ).reshape(seqs * row_count, TOP)
        own_spread_m.append(
            ((mlp_iota[:, None] == ids[None, :, 0]) | (mlp_iota[:, None] == ids[None, :, 1])).astype(BF16)
        )
        own_collect_m.append(
            ((mlp_iota[None, :] == ids[:, 0, None]) | (mlp_iota[None, :] == ids[:, 1, None])).astype(BF16)
        )
        ids = jnp.where(
            mlp_all == here * locals_ + l,
            source * (seqs * capacity) + which * capacity + mlp_place,
            -1,
        ).reshape(seqs * seq_len, TOP)
        table = (
            (mlp_iota[:, None] == ids[None, :, 0]) | (mlp_iota[:, None] == ids[None, :, 1])
        ).astype(BF16)
        both = jnp.sum(mlp_all, axis=-1).reshape(seqs * seq_len, 1).astype(BF16)
        sums = mm(table, jnp.concatenate([both, jnp.ones_like(both)], axis=1))
        other_sum.append((sums[:, :1], sums[:, 1:]))

    hidden_first, routes, adapters = lax.optimization_barrier((hidden_in, routes, adapters))
    everyone = gather_line(
        hidden_first,
        "expert",
        ranks,
        lambda total, piece, at: lax.dynamic_update_slice(total, piece[:, None], (0, at, 0, 0)),
        jnp.zeros((seqs, ranks, row_count, width), BF16),
    ).reshape(seqs, seq_len, width)

    flat_cot, everyone = lax.optimization_barrier((cotangent, everyone))
    orders = halves_bits(groups)
    beside = [[block[: block.shape[0] // 2], block[block.shape[0] // 2 :]] for block in beside]

    def exchange_all(step):
        return [
            [exchange(half, "dp", groups, bits[step]) for half, bits in zip(halves, orders)]
            for halves in beside
        ]

    flat_cot = flat_cot.reshape(seqs * row_count, width)
    cot_rows = [send(mm(own_spread_m[l], flat_cot).astype(BF16)) for l in range(locals_)]

    tokens_all = everyone.astype(F32)
    scale_all = rms_scale(tokens_all)
    normed_low = (tokens_all * scale_all * attn_gain).astype(BF16)
    router_parts = jnp.concatenate(three_parts(attn_gain[:, None] * attn_router.astype(F32)), axis=1)
    parts = mm(everyone.reshape(seqs * seq_len, width), router_parts).reshape(seqs, seq_len, 3, EXPERTS)
    logits = scale_all * (parts[:, :, 0] + (parts[:, :, 1] + parts[:, :, 2]))
    onehot_a = onehot[:, :, :, 0].reshape(seqs, seq_len, TOP, EXPERTS)
    gap = jnp.sum((onehot_a[:, :, 0] - onehot_a[:, :, 1]) * logits, axis=-1)

    flat_routes = attn_all.reshape(seqs, seq_len, TOP)
    places = jnp.arange(seq_len, dtype=jnp.int32)
    columns = [
        block_ids,
        jnp.broadcast_to(places // 128, block_ids.shape),
        jnp.broadcast_to(places % 128, block_ids.shape),
        jnp.sum(flat_routes, axis=-1),
        flat_routes[..., 0],
    ]
    known = jnp.stack([c.astype(BF16) for c in columns] + list(three_parts(gap)), axis=-1)
    known = jnp.einsum("srt,stc->src", spread_a, known, preferred_element_type=F32)
    known = known.reshape(seqs, locals_, slots, known.shape[-1]).transpose(1, 0, 2, 3)
    self_id = (here * locals_ + jnp.arange(locals_)).astype(F32)[:, None, None]
    slot_blocks = known[..., 0].astype(jnp.int32)
    slot_place = known[..., 1] * 128.0 + known[..., 2]
    slot_other = known[..., 3] - self_id
    slot_gap = known[..., 5] + (known[..., 6] + known[..., 7])
    slot_gap = jnp.where(known[..., 4] == self_id, slot_gap, -slot_gap)
    gate_a = jax.nn.sigmoid(slot_gap)
    expert_f = expert_ids.astype(F32)
    pick_a = (expert_f == self_id[..., None]).astype(F32) - (expert_f == slot_other[..., None]).astype(F32)
    weigh_a = pick_a * (gate_a * jax.nn.sigmoid(-slot_gap))[..., None]
    cos_q, sin_q = angle_tables(slot_place)
    cos_k, sin_k = angle_tables(places)
    query_blocks = slot_blocks[..., None]
    key_blocks = block_ids[:, None, :]

    flat_low = normed_low.reshape(seqs * seq_len, width)
    own_adapter = (
        jnp.arange(NADAPT * RANK, dtype=jnp.int32)[None, :] // RANK == adapter_index[:, None]
    )
    low_rank = mm(flat_low, adapt_down).reshape(seqs, seq_len, NADAPT * RANK)
    low_rank = jnp.where(own_adapter[:, None, :], low_rank, 0.0).astype(BF16)
    key_value = make_key_value(
        flat_low, low_rank.reshape(seqs * seq_len, -1), near_full, adapt_up, cos_k, sin_k, seqs
    ).reshape(seqs, seq_len, 2 * width)

    picked = jnp.einsum(
        "slrt,std->lsrd",
        spread_a.reshape(seqs, locals_, slots, seq_len),
        normed_low,
        preferred_element_type=F32,
    ).astype(BF16)
    beside, picked = lax.optimization_barrier((beside, picked))
    beside = exchange_all(0)
    queries = project(picked.reshape(locals_, seqs * slots, width), near_full, query_column)
    query_rot, attended, probs = attend(
        queries.reshape(locals_, seqs, slots, width), key_value, cos_q, sin_q, query_blocks, key_blocks
    )
    gate_rows = gate_a[..., None]
    projected, gated = project(
        attended.reshape(locals_, seqs * slots, width),
        near_full,
        output_column,
        gate_rows.reshape(locals_, seqs * slots, 1),
    )
    beside, projected = lax.optimization_barrier((beside, projected))
    for step in range(1, len(orders[0])):
        beside = exchange_all(step)
    for l, halves in enumerate(beside):
        inner_full[l][0] = (0, in_order(halves, orders, groups))
    projected = projected.reshape(locals_, seqs, slots, width)
    gated = gated.reshape(locals_, seqs, slots, width)
    order = np.arange(locals_ * slots).reshape(locals_, ranks, capacity).transpose(1, 0, 2).reshape(-1)
    to_send = jnp.asarray(np.eye(locals_ * slots)[order], BF16)
    to_slots = jnp.asarray(np.eye(locals_ * slots)[order].T, BF16)
    tokens = hidden_in.astype(F32)
    middles = []
    for s in range(seqs):
        back = send(mm(to_send, gated[:, s].reshape(locals_ * slots, width)).astype(BF16))
        middles.append(tokens[s] + mm(own_collect_a[s], back))
    middle = jnp.stack(middles)
    scale_two = rms_scale(middle)
    normed_two_low = (middle * scale_two * mlp_gain).astype(BF16).reshape(seqs * row_count, width)

    final = middle.reshape(seqs * row_count, width)
    grad_normed_two = jnp.zeros((seqs * row_count, width), F32)
    held = None
    for l in range(locals_):
        rows_in = send(mm(own_spread_m[l], normed_two_low).astype(BF16))
        slot_logits = mm(rows_in, mlp_router)
        me = (here * locals_ + l).astype(F32)
        pick_m = (expert_f[None, :] == me).astype(F32) - (
            expert_f[None, :] == other_sum[l][0] - me
        ).astype(F32)
        gate_m = jax.nn.sigmoid(jnp.sum(pick_m * slot_logits, axis=-1, keepdims=True))
        grad_rows = (gate_m * cot_rows[l].astype(F32)).astype(BF16)
        made = None
        for at, (low, inner) in enumerate(inner_full[l]):
            if held is not None and at + 1 == len(inner_full[l]):
                held, made = lax.optimization_barrier((held, made))
                final = final + mm(own_collect_m[l - 1], held)
            ends = (cot_rows[l], gate_m, pick_m, mlp_router) if at + 1 == len(inner_full[l]) else None
            made = expert_pass(rows_in, grad_rows, inner, down_full, l, low, made, ends)
        gated_out, grad_source = made
        grad_back = send(grad_source)
        if l + 1 < locals_:
            grad_normed_two = grad_normed_two + mm(own_collect_m[l], grad_back)
        held = send(gated_out) if l + 1 < locals_ else gated_out
    grad_normed_two = grad_normed_two.reshape(seqs, row_count, width)
    late = (collect_a, own_adapter.astype(F32)[:, None, :], weigh_a, attn_router, to_slots)
    (collect_a, mask, weigh_a, router_near, to_slots), grad_normed_two = lax.optimization_barrier(
        (late, grad_normed_two)
    )
    back_table = own_collect_m[locals_ - 1].reshape(seqs, row_count, mlp_rows)
    grad_middle, leaving = [], []
    for s in range(seqs):
        grad, rows = middle_back(
            s, grad_back, back_table, grad_normed_two, middle, cotangent, mlp_gain[None], own_spread_a
        )
        grad_middle.append(grad)
        leaving.append(rows)

    arrived = [send(leaving[0])]
    arrived[0], leaving[1:] = lax.optimization_barrier((arrived[0], leaving[1:]))
    arrived += [send(rows) for rows in leaving[1:]]
    down_pieces, up_pieces = [], []
    input_grad = None
    for s in range(seqs):
        grad_attended, dots = out_back(
            s, arrived[s], to_slots, gate_rows, projected, near_full, output_column
        )
        dq, dk, dv = attend_back(s, query_rot, key_value, grad_attended, probs, cos_q, sin_q, cos_k, sin_k)
        if s == 0:
            arrived[1:], held, dk = lax.optimization_barrier((arrived[1:], held, dk))
            held = send(held)
        part, grad_low = last_grad(
            s, dk, dv, dq, collect_a, dots, weigh_a, mask, adapt_up, router_near, adapt_down, near_full,
            query_column,
        )
        if s + 1 < seqs:
            arrived[s + 1], held, part = lax.optimization_barrier((arrived[s + 1], held, part))
        grad_normed = lax.psum_scatter(part, "expert", scatter_dimension=0, tiled=True)
        input_grad = input_back(s, grad_normed, grad_middle[s], hidden_in, attn_gain[None], input_grad)
        first = adapter_index[s] * RANK
        down_pieces.append(lax.dynamic_slice_in_dim(mm(grad_low, normed_low[s], TN), first, RANK, 0))
        up_piece = jnp.concatenate([mm(low_rank[s], dk, TN), mm(low_rank[s], dv, TN)], axis=1)
        up_pieces.append(lax.dynamic_slice_in_dim(up_piece, first, RANK, 0))
    final = final + mm(own_collect_m[locals_ - 1], held)
    layer_out = final.astype(BF16).reshape(seqs, row_count, width)

    down_part = width // (groups * ranks)
    pieces = jnp.concatenate(
        [
            jnp.stack(down_pieces).reshape(seqs * RANK, groups, ranks, down_part),
            jnp.stack(up_pieces).reshape(seqs * RANK, groups, ranks, 2 * down_part),
        ],
        axis=-1,
    )
    pieces = pieces.transpose(1, 0, 2, 3).reshape(groups, seqs * RANK, 3 * ranks * down_part)
    pieces = lax.all_to_all(pieces, "dp", split_axis=0, concat_axis=0, tiled=True)
    pieces = pieces.reshape(groups * seqs, RANK, 3 * ranks * down_part)
    belongs = (adapters[:, None] == jnp.arange(NADAPT, dtype=jnp.int32)[None, :]).astype(F32)
    sums = jnp.einsum("qkf,qa->akf", pieces, belongs, precision=PRECISE)
    sums = sums.reshape(NADAPT * RANK, ranks, 3 * down_part).transpose(1, 0, 2)
    sums = jnp.sum(send(sums), axis=0).T
    return (layer_out, input_grad, sums[:down_part], sums[down_part:])


def solution(mesh):
    return jax.shard_map(
        per_device,
        mesh=mesh,
        in_specs=(
            P("dp", "expert", None),
            P("dp", "expert", None),
            P("dp", None),
            P("dp", "expert", None),
            P("dp", "expert", None),
            P("dp"),
            P(),
            P(),
            P(),
            P(),
            P("dp", None),
            P("expert", "dp", None),
            P("expert", "dp", None),
            P("expert", "dp", None),
            P("expert", "dp", None),
            P(),
            P(),
        ),
        out_specs=(
            P("dp", "expert", None),
            P("dp", "expert", None),
            P(("dp", "expert"), None),
            P(("dp", "expert"), None),
        ),
        check_vma=False,
    )
```

```python
import functools
import math

import jax
import jax.numpy as jnp
import numpy as np
from jax import lax
from jax.experimental import pallas as pl
from jax.experimental.pallas import tpu as pltpu
from jax.sharding import PartitionSpec as P

HEADS = 16
HDIM = 128
FF = 5632
EXPERTS = 8
TOP = 2
RANK = 16
NADAPT = 8

PRECISE = lax.Precision.HIGHEST
EPSILON = 1e-06
ROPE_BASE = 10000.0
MASKED_SCORE = -1e30
SCALE_QK = 1.0 / math.sqrt(HDIM)
BF16 = jnp.bfloat16
F32 = jnp.float32
VMEM_LIMIT = 58 * 1024 * 1024

NN = (((1,), (0,)), ((), ()))
NT = (((1,), (1,)), ((), ()))
TN = (((0,), (0,)), ((), ()))


def mm(left, right, dims=NN):
    return lax.dot_general(left, right, dims, preferred_element_type=F32)


def params(*semantics):
    return pltpu.CompilerParams(dimension_semantics=semantics, vmem_limit_bytes=VMEM_LIMIT)


def once(shape, index_map):
    return pl.BlockSpec(shape, index_map, pipeline_mode=pl.Buffered(1))


def rms_scale(values):
    return lax.rsqrt(jnp.mean(values * values, axis=-1, keepdims=True) + EPSILON)


def norm_back(values, scale_rows, norm_gain, grad_rows):
    scaled_grad = norm_gain * grad_rows
    return scale_rows * (
        scaled_grad
        - values * scale_rows * scale_rows * jnp.mean(scaled_grad * values, axis=-1, keepdims=True)
    )


def angle_tables(positions):
    half_dim = HDIM // 2
    frequency = ROPE_BASE ** (-(jnp.arange(half_dim, dtype=F32) * (2.0 / HDIM)))
    frequency = jnp.concatenate([frequency, frequency])
    sign = jnp.concatenate([-jnp.ones((half_dim,), F32), jnp.ones((half_dim,), F32)])
    angles = positions.astype(F32)[..., None] * frequency
    return (jnp.cos(angles), jnp.sin(angles) * sign)


def three_parts(values):
    first = values.astype(BF16)
    rest = values - first.astype(F32)
    second = rest.astype(BF16)
    third = (rest - second.astype(F32)).astype(BF16)
    return first, second, third


def hop(from_left, from_right, axis, size):
    rightward = [(i, i + 1) for i in range(size - 1)]
    leftward = [(i + 1, i) for i in range(size - 1)]
    return lax.ppermute(from_left, axis, rightward), lax.ppermute(from_right, axis, leftward)


def put_line(hops, axis, put, start):
    size = len(hops)
    here = lax.axis_index(axis)
    total = put(start, hops[0][0], here)
    for step in range(1, size):
        piece = jnp.where(here >= step, hops[step][0], hops[size - step][1])
        total = put(total, piece, lax.rem(here - step + size, size))
    return total


def exchange(total, axis, size, bit):
    other = lax.ppermute(total, axis, [(i, i ^ bit) for i in range(size)])
    low = jnp.bitwise_and(lax.axis_index(axis), bit) == 0
    return jnp.stack([jnp.where(low, total, other), jnp.where(low, other, total)])


def halves_bits(size):
    bits = [1 << k for k in range(1, size.bit_length() - 1)]
    return [bits, bits[::-1]]


def in_order(halves, orders, size):
    made = []
    for total, bits in zip(halves, orders):
        count = len(bits)
        order = sorted(range(count), key=lambda d: -bits[count - 1 - d])
        total = total.transpose(*order, *range(count, total.ndim))
        made.append(total.reshape(size, *total.shape[count:]))
    whole = jnp.stack(made, axis=1)
    return whole.reshape(-1, whole.shape[-1])


def send(buffer):
    return lax.all_to_all(buffer, "expert", split_axis=0, concat_axis=0, tiled=True)


def merge_body(core_ref, mine_ref, other_ref, out_ref):
    rows = mine_ref.shape[0]
    low = core_ref[0] == 0
    mine, other = mine_ref[...], other_ref[...]
    out_ref[:rows, :] = jnp.where(low, mine, other)
    out_ref[rows:, :] = jnp.where(low, other, mine)


def merge_halves(mine, other, core, block_rows):
    parts, rows, part = mine.shape
    half = pl.BlockSpec((None, block_rows, part), lambda q, g: (q, g, 0))
    return pl.pallas_call(
        merge_body,
        grid=(parts, rows // block_rows),
        in_specs=[pl.BlockSpec(memory_space=pltpu.SMEM), half, half],
        out_specs=pl.BlockSpec((2 * block_rows, part), lambda q, g: (g, q)),
        out_shape=jax.ShapeDtypeStruct((2 * rows, parts * part), BF16),
        compiler_params=params("arbitrary", "arbitrary"),
        name="merge_halves",
    )(core, mine, other)


def kv_body(seqs, seq_len, key_tiles, x_ref, low_ref, wk_ref, wv_ref, up_ref, cos_ref, sin_ref, out_ref):
    is_key = pl.program_id(0) < key_tiles

    @pl.when(is_key)
    def _():
        for s in range(seqs):
            rows = pl.ds(s * seq_len, seq_len)
            made = mm(x_ref[rows, :], wk_ref[...]) + mm(low_ref[rows, :], up_ref[...], NT)
            for h in range(made.shape[1] // HDIM):
                cols = slice(h * HDIM, (h + 1) * HDIM)
                part = made[:, cols]
                turned = part * cos_ref[...] + pltpu.roll(part, HDIM // 2, 1) * sin_ref[...]
                out_ref[rows, cols] = turned.astype(BF16)

    @pl.when(jnp.logical_not(is_key))
    def _():
        for s in range(seqs):
            rows = pl.ds(s * seq_len, seq_len)
            made = mm(x_ref[rows, :], wv_ref[...]) + mm(low_ref[rows, :], up_ref[...], NT)
            out_ref[rows, :] = made.astype(BF16)


def make_key_value(normed_low, low_rank, weights, value_weights, adapt_up, cos_k, sin_k, seqs):
    rows, width = normed_low.shape
    seq_len = rows // seqs
    tile = 512
    count = width // tile
    return pl.pallas_call(
        functools.partial(kv_body, seqs, seq_len, count),
        grid=(2 * count,),
        in_specs=[
            once((rows, width), lambda i: (0, 0)),
            once((rows, low_rank.shape[1]), lambda i: (0, 0)),
            pl.BlockSpec((width, tile), lambda i: (0, jnp.minimum(i, count - 1))),
            pl.BlockSpec((width, tile), lambda i: (0, jnp.maximum(i - count, 0))),
            pl.BlockSpec((tile, low_rank.shape[1]), lambda i: (i, 0)),
            once((seq_len, HDIM), lambda i: (0, 0)),
            once((seq_len, HDIM), lambda i: (0, 0)),
        ],
        out_specs=pl.BlockSpec((rows, tile), lambda i: (0, i)),
        out_shape=jax.ShapeDtypeStruct((rows, 2 * width), BF16),
        compiler_params=params("arbitrary"),
        name="key_value",
    )(normed_low, low_rank, weights, value_weights, adapt_up, cos_k, sin_k)


def project_body(x_ref, w_ref, *refs):
    made = mm(x_ref[...], w_ref[...])
    if len(refs) == 1:
        refs[0][...] = made.astype(BF16)
    else:
        gate_ref, out_ref, gated_ref = refs
        out_ref[...] = made.astype(BF16)
        gated_ref[...] = (made * gate_ref[...]).astype(BF16)


def project(values, weights, from_column, gate=None):
    locals_, rows, width = values.shape
    tile = 512
    first, step = from_column // tile, width // tile
    out_spec = pl.BlockSpec((None, rows, tile), lambda l, i: (l, 0, i))
    out_shape = jax.ShapeDtypeStruct(values.shape, BF16)
    in_specs = [
        pl.BlockSpec((None, rows, width), lambda l, i: (l, 0, 0)),
        pl.BlockSpec((width, tile), lambda l, i: (0, first + step * l + i)),
    ]
    more = []
    if gate is not None:
        in_specs.append(pl.BlockSpec((None, rows, 1), lambda l, i: (l, 0, 0)))
        more = [gate]
    return pl.pallas_call(
        project_body,
        grid=(locals_, step),
        in_specs=in_specs,
        out_specs=out_spec if gate is None else [out_spec] * 2,
        out_shape=out_shape if gate is None else [out_shape] * 2,
        compiler_params=params("arbitrary", "arbitrary"),
        name="project",
    )(values, weights, *more)


def attend_body(q_ref, k_ref, v_ref, cos_ref, sin_ref, qb_ref, kb_ref, rot_ref, out_ref, probs_ref):
    locals_, _, slots, _ = q_ref.shape
    rows = locals_ * slots
    q = q_ref[...].reshape(rows, HDIM).astype(F32)
    cos, sin = cos_ref[...].reshape(rows, HDIM), sin_ref[...].reshape(rows, HDIM)
    rot = (q * cos + pltpu.roll(q, HDIM // 2, 1) * sin).astype(BF16)
    rot_ref[...] = rot.reshape(rot_ref.shape)
    k, v = k_ref[0], v_ref[0]
    kb = kb_ref[0]
    for l in range(locals_):
        part = rot[l * slots : (l + 1) * slots]
        visible = kb <= qb_ref[l, 0]
        masked = jnp.where(visible, mm(part, k, NT), MASKED_SCORE)
        top = jnp.max(masked, axis=-1, keepdims=True)
        terms = jnp.exp((masked - top) * SCALE_QK)
        total = jnp.sum(terms, axis=-1, keepdims=True)
        probs = (terms * (1.0 / total)).astype(BF16)
        probs_ref[l, 0, 0] = probs
        out_ref[l, 0] = mm(probs, v).astype(BF16)


def attend(queries, key_value, cos_q, sin_q, query_blocks, key_blocks):
    locals_, seqs, slots, width = queries.shape
    seq_len = key_value.shape[1]
    q_spec = pl.BlockSpec((locals_, 1, slots, HDIM), lambda s, h: (0, s, 0, h))
    tab_spec = pl.BlockSpec((locals_, 1, slots, HDIM), lambda s, h: (0, s, 0, 0))
    return pl.pallas_call(
        attend_body,
        grid=(seqs, HEADS),
        in_specs=[
            q_spec,
            pl.BlockSpec((1, seq_len, HDIM), lambda s, h: (s, 0, h)),
            pl.BlockSpec((1, seq_len, HDIM), lambda s, h: (s, 0, HEADS + h)),
            tab_spec,
            tab_spec,
            pl.BlockSpec((locals_, 1, slots, 1), lambda s, h: (0, s, 0, 0)),
            pl.BlockSpec((1, 1, seq_len), lambda s, h: (s, 0, 0)),
        ],
        out_specs=[
            q_spec,
            q_spec,
            pl.BlockSpec((locals_, 1, 1, slots, seq_len), lambda s, h: (0, s, h, 0, 0)),
        ],
        out_shape=[
            jax.ShapeDtypeStruct(queries.shape, BF16),
            jax.ShapeDtypeStruct(queries.shape, BF16),
            jax.ShapeDtypeStruct((locals_, seqs, HEADS, slots, seq_len), BF16),
        ],
        compiler_params=params("arbitrary", "arbitrary"),
        name="attend",
    )(queries, key_value, key_value, cos_q, sin_q, query_blocks, key_blocks)


def attend_back_body(q_ref, k_ref, v_ref, g_ref, p_ref, cos_ref, sin_ref, ck_ref, sk_ref, dq_ref, dk_ref, dv_ref):
    locals_, _, slots, _ = q_ref.shape
    rows = locals_ * slots
    k, v = k_ref[0], v_ref[0]
    q = q_ref[...].reshape(rows, HDIM)
    grad = g_ref[...].reshape(rows, HDIM)
    probs = p_ref[...].reshape(rows, k.shape[0])
    weighed = probs.astype(F32) * mm(grad, v, NT)
    delta = jnp.sum(weighed, axis=-1, keepdims=True)
    grad_scores = (weighed - probs.astype(F32) * delta).astype(BF16)
    dq = mm(grad_scores, k) * SCALE_QK
    cos, sin = cos_ref[...].reshape(rows, HDIM), sin_ref[...].reshape(rows, HDIM)
    dq = dq * cos - pltpu.roll(dq, HDIM // 2, 1) * sin
    dq_ref[...] = dq.astype(BF16).reshape(dq_ref.shape)
    dk = mm(grad_scores, q, TN) * SCALE_QK
    dk_ref[...] = (dk * ck_ref[...] - pltpu.roll(dk, HDIM // 2, 1) * sk_ref[...]).astype(BF16)
    dv_ref[...] = mm(probs, grad, TN).astype(BF16)


def attend_back(s, query_rot, key_value, grad, probs, cos_q, sin_q, cos_k, sin_k):
    locals_, _, slots, width = query_rot.shape
    seq_len = key_value.shape[1]
    tab_spec = pl.BlockSpec((locals_, 1, slots, HDIM), lambda h: (0, s, 0, 0))
    key_tab = pl.BlockSpec((seq_len, HDIM), lambda h: (0, 0))
    grad_spec = pl.BlockSpec((locals_, slots, HDIM), lambda h: (0, 0, h))
    key_spec = pl.BlockSpec((seq_len, HDIM), lambda h: (0, h))
    return pl.pallas_call(
        attend_back_body,
        grid=(HEADS,),
        in_specs=[
            pl.BlockSpec((locals_, 1, slots, HDIM), lambda h: (0, s, 0, h)),
            pl.BlockSpec((1, seq_len, HDIM), lambda h: (s, 0, h)),
            pl.BlockSpec((1, seq_len, HDIM), lambda h: (s, 0, HEADS + h)),
            grad_spec,
            pl.BlockSpec((locals_, 1, 1, slots, seq_len), lambda h: (0, s, h, 0, 0)),
            tab_spec,
            tab_spec,
            key_tab,
            key_tab,
        ],
        out_specs=[grad_spec, key_spec, key_spec],
        out_shape=[
            jax.ShapeDtypeStruct((locals_, slots, width), BF16),
            jax.ShapeDtypeStruct((seq_len, width), BF16),
            jax.ShapeDtypeStruct((seq_len, width), BF16),
        ],
        compiler_params=params("arbitrary"),
        name="attend_back",
    )(query_rot, key_value, key_value, grad, probs, cos_q, sin_q, cos_k, sin_k)


def expert_body(has_start, is_last, joint, x_ref, c_ref, wg_ref, wu_ref, wd_ref, *refs):
    refs = list(refs)
    start = [refs.pop(0), refs.pop(0)] if has_start else []
    if is_last:
        cot_ref, gate_ref, pick_ref, router_ref = refs[:4]
        made_refs, (out_ref, gs_ref) = (refs[4:5], refs[5:7]) if joint else (refs[4:6], refs[6:8])
        late = start + [cot_ref]
    else:
        out_ref, gs_ref = refs[:2]
        late = start
    count = len(late)
    held, sem = (refs[-count - 1 : -1], refs[-1]) if count else ([], None)
    copies = [pltpu.make_async_copy(late[i], held[i], sem.at[i]) for i in range(count)]

    @pl.when(pl.program_id(0) == 0)
    def _():
        for copy in copies:
            copy.start()
        out_ref[...] = jnp.zeros_like(out_ref)
        gs_ref[...] = jnp.zeros_like(gs_ref)

    x, c = x_ref[...], c_ref[...]
    wg, wu, wd = wg_ref[...], wu_ref[...], wd_ref[...]
    gate, up = mm(x, wg), mm(x, wu)
    sig = jax.nn.sigmoid(gate)
    silu = gate * sig
    out_ref[...] += mm((silu * up).astype(BF16), wd)
    grad = mm(c, wd, NT)
    grad_gate = (grad * up * sig * (1.0 + gate * (1.0 - sig))).astype(BF16)
    grad_up = (grad * silu).astype(BF16)
    gs_ref[...] += mm(grad_gate, wg, NT) + mm(grad_up, wu, NT)

    @pl.when(pl.program_id(0) == pl.num_programs(0) - 1)
    def _():
        for copy in copies:
            copy.wait()
        made, back = out_ref[...], gs_ref[...]
        if has_start:
            made, back = made + held[0][...], back + held[1][...]
        if has_start and not is_last:
            out_ref[...] = made
            gs_ref[...] = back
        if is_last:
            share = gate_ref[...]
            dots = jnp.sum(held[-1][...].astype(F32) * made, axis=-1, keepdims=True)
            weigh = pick_ref[...] * (dots * share * (1.0 - share))
            high = weigh.astype(BF16)
            low = (weigh - high.astype(F32)).astype(BF16)
            router = router_ref[...]
            width = x_ref.shape[1]
            made_refs[0][:, :width] = (back + mm(high, router, NT) + mm(low, router, NT)).astype(BF16)
            if joint:
                made_refs[0][:, width:] = (share * made).astype(BF16)
            else:
                made_refs[1][...] = (share * made).astype(BF16)


def expert_pass(rows_in, grad_in, inner, down, l, down_from, start=None, last=None, joint=False):
    rows, width = rows_in.shape
    units = inner.shape[1] // 2
    tile = 512 if units % 512 == 0 and down_from % 512 == 0 else 256
    first = down_from // tile

    def whole(array):
        return once(array.shape, lambda i: (0,) * array.ndim)

    more = ([] if start is None else list(start)) + ([] if last is None else list(last))
    outs = [(2 * width, BF16)] if joint else [(width, F32 if last is None else BF16)] * 2
    late = ([] if start is None else [F32, F32]) + ([] if last is None else [BF16])
    away = len(late)
    scratch = [] if last is None else [pltpu.VMEM((rows, width), F32)] * 2
    if away:
        scratch += [pltpu.VMEM((rows, width), t) for t in late] + [pltpu.SemaphoreType.DMA((away,))]
    return pl.pallas_call(
        functools.partial(expert_body, start is not None, last is not None, joint),
        grid=(units // tile,),
        in_specs=[
            whole(rows_in),
            whole(grad_in),
            pl.BlockSpec((width, tile), lambda i: (0, i)),
            pl.BlockSpec((width, tile), lambda i: (0, units // tile + i)),
            pl.BlockSpec((None, tile, width), lambda i: (l, first + i, 0)),
        ]
        + [pl.BlockSpec(memory_space=pl.ANY) if i < away else whole(m) for i, m in enumerate(more)],
        out_specs=[once((rows, columns), lambda i: (0, 0)) for columns, _ in outs],
        out_shape=[jax.ShapeDtypeStruct((rows, columns), kind) for columns, kind in outs],
        scratch_shapes=scratch,
        compiler_params=params("arbitrary"),
        name="expert",
    )(rows_in, grad_in, inner, inner, down, *more)


def out_back_body(locals_, arrived_ref, order_ref, gate_ref, projected_ref, *refs):
    w_refs, (out_ref, dots_ref, rows_ref) = refs[:locals_], refs[locals_:]
    slots = projected_ref.shape[1]

    @pl.when(pl.program_id(0) == 0)
    def _():
        for l in range(locals_):
            rows = mm(order_ref[pl.ds(l * slots, slots), :], arrived_ref[...])
            dots_ref[l] = jnp.sum(rows * projected_ref[l].astype(F32), axis=-1, keepdims=True)
            rows_ref[l] = (rows * gate_ref[l]).astype(BF16)

    for l in range(locals_):
        out_ref[l] = mm(rows_ref[l], w_refs[l][...], NT).astype(BF16)


def out_back(s, arrived, order, gate, projected, weights, from_column):
    locals_, slots = gate.shape[0], gate.shape[2]
    rows, width = arrived.shape
    tile = 512
    return pl.pallas_call(
        functools.partial(out_back_body, locals_),
        grid=(width // tile,),
        in_specs=[
            once((rows, width), lambda i: (0, 0)),
            once((rows, rows), lambda i: (0, 0)),
            once((locals_, None, slots, 1), lambda i: (0, s, 0, 0)),
            once((locals_, None, slots, width), lambda i: (0, s, 0, 0)),
        ]
        + [
            pl.BlockSpec((tile, width), lambda i, l=l: (i, from_column // width + l))
            for l in range(locals_)
        ],
        out_specs=[
            pl.BlockSpec((locals_, slots, tile), lambda i: (0, 0, i)),
            pl.BlockSpec((locals_, slots, 1), lambda i: (0, 0, 0)),
        ],
        out_shape=[
            jax.ShapeDtypeStruct((locals_, slots, width), BF16),
            jax.ShapeDtypeStruct((locals_, slots, 1), F32),
        ],
        scratch_shapes=[pltpu.VMEM((locals_, slots, width), BF16)],
        compiler_params=params("arbitrary"),
        name="out_back",
    )(arrived, order, gate, projected, *([weights] * locals_))


def last_body(
    locals_, seq_len, dk_ref, dv_ref, dq_ref, table_ref, dots_ref, weigh_ref, mask_ref, up_ref, router_ref, down_ref, wk_ref, wv_ref, *refs
):
    wq_refs, (out_ref, low_ref, source_ref, weigh_low_ref) = refs[:locals_], refs[locals_:]
    width = dk_ref.shape[1]
    slots = dq_ref.shape[1]

    @pl.when(pl.program_id(0) == 0)
    def _():
        low = mm(dk_ref[...], up_ref[:width, :]) + mm(dv_ref[...], up_ref[width:, :])
        low_ref[...] = (low * mask_ref[...]).astype(BF16)
        for l in range(locals_):
            weigh = weigh_ref[l] * dots_ref[l]
            high = weigh.astype(BF16)
            weigh_low_ref[l, :, :EXPERTS] = high
            weigh_low_ref[l, :, EXPERTS:] = (weigh - high.astype(F32)).astype(BF16)

    router = jnp.concatenate([router_ref[...]] * 2, axis=1)
    for l in range(locals_):
        source = mm(dq_ref[l], wq_refs[l][...], NT) + mm(weigh_low_ref[l], router, NT)
        source_ref[pl.ds(l * slots, slots), :] = source.astype(BF16)
    total = mm(dk_ref[...], wk_ref[...], NT) + mm(dv_ref[...], wv_ref[...], NT)
    total += mm(low_ref[...], down_ref[...], NT)
    total += mm(table_ref[0], source_ref[...])
    out_ref[...] = total.astype(BF16)


def last_grad(
    s, dk, dv, dq, table, dots, weigh, mask, adapt_up, router, adapt_down, weights, value_weights, query_column
):
    seq_len, width = dk.shape
    locals_, slots, _ = dq.shape
    tile = 256
    ranks = adapt_up.shape[1]
    return pl.pallas_call(
        functools.partial(last_body, locals_, seq_len),
        grid=(width // tile,),
        in_specs=[
            once((seq_len, width), lambda i: (0, 0)),
            once((seq_len, width), lambda i: (0, 0)),
            once((locals_, slots, width), lambda i: (0, 0, 0)),
            once((1, seq_len, locals_ * slots), lambda i: (s, 0, 0)),
            once((locals_, slots, 1), lambda i: (0, 0, 0)),
            once((locals_, None, slots, EXPERTS), lambda i: (0, s, 0, 0)),
            once((None, 1, ranks), lambda i: (s, 0, 0)),
            once((2 * width, ranks), lambda i: (0, 0)),
            pl.BlockSpec((tile, EXPERTS), lambda i: (i, 0)),
            pl.BlockSpec((tile, ranks), lambda i: (i, 0)),
            pl.BlockSpec((tile, width), lambda i: (i, 0)),
            pl.BlockSpec((tile, width), lambda i: (i, 0)),
        ]
        + [
            pl.BlockSpec((tile, width), lambda i, l=l: (i, query_column // width + l))
            for l in range(locals_)
        ],
        out_specs=[
            pl.BlockSpec((seq_len, tile), lambda i: (0, i)),
            pl.BlockSpec((seq_len, ranks), lambda i: (0, 0)),
        ],
        out_shape=[
            jax.ShapeDtypeStruct((seq_len, width), BF16),
            jax.ShapeDtypeStruct((seq_len, ranks), BF16),
        ],
        scratch_shapes=[
            pltpu.VMEM((locals_ * slots, tile), BF16),
            pltpu.VMEM((locals_, slots, 2 * EXPERTS), BF16),
        ],
        compiler_params=params("arbitrary"),
        name="last_grad",
    )(dk, dv, dq, table, dots, weigh, mask, adapt_up, router, adapt_down, weights, value_weights, *([weights] * locals_))


def middle_back_body(back_ref, table_ref, part_ref, middle_ref, cot_ref, gain_ref, spread_ref, out_ref, rows_ref):
    middle = middle_ref[...]
    scale = rms_scale(middle)
    grad = part_ref[...] + mm(table_ref[...], back_ref[...])
    out = cot_ref[...].astype(F32) + norm_back(middle, scale, gain_ref[...], grad)
    out_ref[...] = out
    rows_ref[...] = mm(spread_ref[...], out.astype(BF16)).astype(BF16)


def middle_back(s, back, table, part, middle, cotangent, gain, spread):
    _, rows, width = middle.shape
    slots = spread.shape[1]

    def one(array):
        return once((None, *array.shape[1:]), lambda i: (s, 0, 0))

    return pl.pallas_call(
        middle_back_body,
        grid=(1,),
        in_specs=[
            once(back.shape, lambda i: (0, 0)),
            one(table),
            one(part),
            one(middle),
            one(cotangent),
            once(gain.shape, lambda i: (0, 0)),
            one(spread),
        ],
        out_specs=[once((rows, width), lambda i: (0, 0)), once((slots, width), lambda i: (0, 0))],
        out_shape=[
            jax.ShapeDtypeStruct((rows, width), F32),
            jax.ShapeDtypeStruct((slots, width), BF16),
        ],
        compiler_params=params("arbitrary"),
        name="middle_back",
    )(back, table, part, middle, cotangent, gain, spread)


def input_back_body(grad_ref, middle_ref, tokens_ref, gain_ref, *refs):
    tokens = tokens_ref[...].astype(F32)
    refs[-1][...] = middle_ref[...] + norm_back(
        tokens, rms_scale(tokens), gain_ref[...], grad_ref[...].astype(F32)
    )


def input_back(s, grad, grad_middle, tokens, gain, total):
    seqs, rows, width = tokens.shape
    tile = 128
    flat = pl.BlockSpec((tile, width), lambda i: (i, 0))
    one = pl.BlockSpec((None, tile, width), lambda i: (s, i, 0))
    return pl.pallas_call(
        input_back_body,
        grid=(rows // tile,),
        in_specs=[flat, flat, one, pl.BlockSpec((1, width), lambda i: (0, 0))]
        + ([] if total is None else [pl.BlockSpec(memory_space=pl.ANY)]),
        out_specs=one,
        out_shape=jax.ShapeDtypeStruct(tokens.shape, F32),
        input_output_aliases={} if total is None else {4: 0},
        compiler_params=params("arbitrary"),
        name="input_back",
    )(grad, grad_middle, tokens, gain, *([] if total is None else [total]))


def per_device(
    hidden_in,
    cotangent,
    block_ids,
    attn_routes,
    mlp_routes,
    adapter_index,
    attn_gain,
    mlp_gain,
    attn_router,
    mlp_router,
    kv_weight,
    query_weight,
    output_weight,
    inner_weight,
    down_weight,
    adapt_down,
    adapt_up,
):
    seqs, row_count, width = hidden_in.shape
    seq_len = block_ids.shape[1]
    ranks = seq_len // row_count
    locals_ = query_weight.shape[0]
    capacity = (17 * row_count * TOP + 16 * EXPERTS - 1) // (16 * EXPERTS)
    slots = ranks * capacity
    here = lax.axis_index("expert")

    query_column = width
    output_column = query_column + locals_ * width
    near = jnp.concatenate(
        [kv_weight[:, :width]]
        + [query_weight[l] for l in range(locals_)]
        + [output_weight[l] for l in range(locals_)],
        axis=1,
    )
    near_full = lax.all_gather(near, "dp", axis=0, tiled=True)
    down_full = lax.all_gather(down_weight, "dp", axis=1, tiled=True)
    groups = width // kv_weight.shape[0]

    def stretch(array, l, low, high):
        return jnp.concatenate([array[l, :, low:high], array[l, :, FF + low : FF + high]], axis=1)

    inner_full, beside = [], []
    for l in range(locals_):
        pieces = []
        cut = 3 * 512 if l + 1 < locals_ else FF * 3 // 4 // 512 * 512
        if l + 1 < locals_:
            pieces.append((0, None))
            beside.append(stretch(inner_weight, l, 0, cut))
        else:
            pieces.append((0, lax.all_gather(stretch(inner_weight, l, 0, cut), "dp", axis=0, tiled=True)))
        pieces.append((cut, lax.all_gather(stretch(inner_weight, l, cut, FF), "dp", axis=0, tiled=True)))
        inner_full.append(pieces)

    routes = lax.all_gather(
        jnp.concatenate([attn_routes, mlp_routes], axis=-1), "expert", axis=1, tiled=True
    ).reshape(seqs, ranks, row_count, 2, TOP)
    adapters = lax.all_gather(adapter_index, "dp", axis=0, tiled=True)
    expert_ids = jnp.arange(EXPERTS, dtype=jnp.int32)
    onehot = (routes[..., None] == expert_ids).astype(F32)
    hits = jnp.sum(onehot, axis=4)
    earlier = (
        jnp.arange(row_count)[:, None] > jnp.arange(row_count)[None, :]
    ).astype(BF16)
    before = jnp.einsum("ut,sptke->spuke", earlier, hits.astype(BF16), preferred_element_type=F32)
    place = jnp.sum(onehot * before[..., None, :], axis=-1).astype(jnp.int32)
    attn_all, mlp_all = routes[:, :, :, 0], routes[:, :, :, 1]
    attn_place, mlp_place = place[:, :, :, 0], place[:, :, :, 1]
    source = jnp.arange(ranks, dtype=jnp.int32)[None, :, None, None]
    which = jnp.arange(seqs, dtype=jnp.int32)[:, None, None, None]

    local_a = attn_all - here * locals_
    is_local = (local_a >= 0) & (local_a < locals_)
    slot_a = jnp.where(is_local, local_a * slots + source * capacity + attn_place, -1)
    slot_a = slot_a.reshape(seqs, seq_len, TOP)
    slot_iota = jnp.arange(locals_ * slots, dtype=jnp.int32)
    spread_a = (
        (slot_iota[None, :, None] == slot_a[:, None, :, 0])
        | (slot_iota[None, :, None] == slot_a[:, None, :, 1])
    ).astype(BF16)
    collect_a = (
        (slot_iota[None, None, :] == slot_a[:, :, 0, None])
        | (slot_iota[None, None, :] == slot_a[:, :, 1, None])
    ).astype(BF16)

    def own(array):
        return lax.dynamic_index_in_dim(array, here, 1, keepdims=False)

    attn_own, attn_own_place = own(attn_all), own(attn_place)
    mlp_own, mlp_own_place = own(mlp_all), own(mlp_place)
    own_slot = attn_own * capacity + attn_own_place
    own_iota = jnp.arange(EXPERTS * capacity, dtype=jnp.int32)
    own_spread_a = (
        (own_iota[None, :, None] == own_slot[:, None, :, 0])
        | (own_iota[None, :, None] == own_slot[:, None, :, 1])
    ).astype(BF16)
    own_collect_a = (
        (own_iota[None, None, :] == own_slot[:, :, 0, None])
        | (own_iota[None, None, :] == own_slot[:, :, 1, None])
    ).astype(BF16)
    mlp_rows = ranks * seqs * capacity
    mlp_iota = jnp.arange(mlp_rows, dtype=jnp.int32)
    own_spread_m, own_collect_m, other_sum = [], [], []
    for l in range(locals_):
        ids = jnp.where(
            mlp_own % locals_ == l,
            (mlp_own // locals_) * (seqs * capacity) + which[:, 0] * capacity + mlp_own_place,
            -1,
        ).reshape(seqs * row_count, TOP)
        own_spread_m.append(
            ((mlp_iota[:, None] == ids[None, :, 0]) | (mlp_iota[:, None] == ids[None, :, 1])).astype(BF16)
        )
        own_collect_m.append(
            ((mlp_iota[None, :] == ids[:, 0, None]) | (mlp_iota[None, :] == ids[:, 1, None])).astype(BF16)
        )
        ids = jnp.where(
            mlp_all == here * locals_ + l,
            source * (seqs * capacity) + which * capacity + mlp_place,
            -1,
        ).reshape(seqs * seq_len, TOP)
        table = (
            (mlp_iota[:, None] == ids[None, :, 0]) | (mlp_iota[:, None] == ids[None, :, 1])
        ).astype(BF16)
        both = jnp.sum(mlp_all, axis=-1).reshape(seqs * seq_len, 1).astype(BF16)
        sums = mm(table, jnp.concatenate([both, jnp.ones_like(both)], axis=1))
        other_sum.append((sums[:, :1], sums[:, 1:]))

    hidden_first, routes = lax.optimization_barrier((hidden_in, routes))
    hops = [(hidden_first, hidden_first)]
    hops.append(hop(*hops[-1], "expert", ranks))

    orders = halves_bits(groups)

    def halves_of(block):
        return [block[: block.shape[0] // 2], block[block.shape[0] // 2 :]]

    def exchange_halves(halves, step):
        return [exchange(half, "dp", groups, bits[step]) for half, bits in zip(halves, orders)]

    part = width // ranks
    value_half = halves_of(lax.dynamic_slice_in_dim(kv_weight, width + here * part, part, 1))
    for step in range(len(orders[0])):
        value_half = exchange_halves(value_half, step)
    value_half = in_order(value_half, orders, groups // 2)
    while len(hops) < ranks:
        hops.append(hop(*hops[-1], "expert", ranks))
    value_half, hops[-1] = lax.optimization_barrier((value_half, hops[-1]))
    value_hops = [(value_half, value_half)]
    while len(value_hops) < 3:
        value_hops.append(hop(*value_hops[-1], "expert", ranks))
    everyone = put_line(
        hops,
        "expert",
        lambda total, piece, at: lax.dynamic_update_slice(total, piece[:, None], (0, at, 0, 0)),
        jnp.zeros((seqs, ranks, row_count, width), BF16),
    ).reshape(seqs, seq_len, width)
    tokens_all = everyone.astype(F32)
    scale_all = rms_scale(tokens_all)
    normed_low = lax.optimization_barrier((tokens_all * scale_all * attn_gain).astype(BF16))
    router_parts = jnp.concatenate(three_parts(attn_gain[:, None] * attn_router.astype(F32)), axis=1)
    parts = mm(everyone.reshape(seqs * seq_len, width), router_parts).reshape(seqs, seq_len, 3, EXPERTS)
    logits = scale_all * (parts[:, :, 0] + (parts[:, :, 1] + parts[:, :, 2]))
    onehot_a = onehot[:, :, :, 0].reshape(seqs, seq_len, TOP, EXPERTS)
    gap = jnp.sum((onehot_a[:, :, 0] - onehot_a[:, :, 1]) * logits, axis=-1)

    flat_routes = attn_all.reshape(seqs, seq_len, TOP)
    places = jnp.arange(seq_len, dtype=jnp.int32)
    columns = [
        block_ids,
        jnp.broadcast_to(places // 128, block_ids.shape),
        jnp.broadcast_to(places % 128, block_ids.shape),
        jnp.sum(flat_routes, axis=-1),
        flat_routes[..., 0],
    ]
    known = jnp.stack([c.astype(BF16) for c in columns] + list(three_parts(gap)), axis=-1)
    known = jnp.einsum("srt,stc->src", spread_a, known, preferred_element_type=F32)
    known = known.reshape(seqs, locals_, slots, known.shape[-1]).transpose(1, 0, 2, 3)
    self_id = (here * locals_ + jnp.arange(locals_)).astype(F32)[:, None, None]
    slot_blocks = known[..., 0].astype(jnp.int32)
    slot_place = known[..., 1] * 128.0 + known[..., 2]
    slot_other = known[..., 3] - self_id
    slot_gap = known[..., 5] + (known[..., 6] + known[..., 7])
    slot_gap = jnp.where(known[..., 4] == self_id, slot_gap, -slot_gap)
    gate_a = jax.nn.sigmoid(slot_gap)
    expert_f = expert_ids.astype(F32)
    pick_a = (expert_f == self_id[..., None]).astype(F32) - (expert_f == slot_other[..., None]).astype(F32)
    weigh_a = pick_a * (gate_a * jax.nn.sigmoid(-slot_gap))[..., None]
    cos_q, sin_q = angle_tables(slot_place)
    cos_k, sin_k = angle_tables(places)
    query_blocks = slot_blocks[..., None]
    key_blocks = block_ids[:, None, :]

    flat_low = normed_low.reshape(seqs * seq_len, width)
    own_adapter = (
        jnp.arange(NADAPT * RANK, dtype=jnp.int32)[None, :] // RANK == adapter_index[:, None]
    )
    low_rank = mm(flat_low, adapt_down).reshape(seqs, seq_len, NADAPT * RANK)
    low_rank = jnp.where(own_adapter[:, None, :], low_rank, 0.0).astype(BF16)
    picked = jnp.einsum(
        "slrt,std->lsrd",
        spread_a.reshape(seqs, locals_, slots, seq_len),
        normed_low,
        preferred_element_type=F32,
    ).astype(BF16)
    beside, picked = lax.optimization_barrier((beside, picked))
    beside = [exchange_halves(halves_of(block), 0) for block in beside]
    queries = project(picked.reshape(locals_, seqs * slots, width), near_full, query_column)
    value_hops[2], normed_low = lax.optimization_barrier((value_hops[2], normed_low))
    while len(value_hops) < ranks:
        value_hops.append(hop(*value_hops[-1], "expert", ranks))
    value_line = put_line(
        value_hops,
        "expert",
        lambda total, piece, at: lax.dynamic_update_slice(total, piece[None], (at, 0, 0)),
        jnp.zeros((ranks, *value_half.shape), BF16),
    )
    value_line, queries, low_rank = lax.optimization_barrier((value_line, queries, low_rank))
    value_full = merge_halves(
        value_line,
        lax.ppermute(value_line, "dp", [(i, i ^ 1) for i in range(groups)]),
        jnp.bitwise_and(lax.axis_index("dp"), 1).astype(jnp.int32).reshape(1),
        kv_weight.shape[0],
    )

    flat_cot, value_full = lax.optimization_barrier((cotangent, value_full))
    flat_cot = flat_cot.reshape(seqs * row_count, width)
    cot_rows = [send(mm(own_spread_m[l], flat_cot).astype(BF16)) for l in range(locals_)]

    key_value = make_key_value(
        flat_low, low_rank.reshape(seqs * seq_len, -1), near_full, value_full, adapt_up, cos_k, sin_k, seqs
    ).reshape(seqs, seq_len, 2 * width)

    query_rot, attended, probs = attend(
        queries.reshape(locals_, seqs, slots, width), key_value, cos_q, sin_q, query_blocks, key_blocks
    )
    cot_rows[0], attended = lax.optimization_barrier((cot_rows[0], attended))
    gate_rows = gate_a[..., None]
    projected, gated = project(
        attended.reshape(locals_, seqs * slots, width),
        near_full,
        output_column,
        gate_rows.reshape(locals_, seqs * slots, 1),
    )
    beside, projected = lax.optimization_barrier((beside, projected))
    for l, halves in enumerate(beside):
        for step in range(1, len(orders[0])):
            halves = exchange_halves(halves, step)
        halves = [exchange(half, "dp", groups, 1) for half in halves]
        inner_full[l][0] = (0, in_order(halves, [bits + [1] for bits in orders], groups))
    projected = projected.reshape(locals_, seqs, slots, width)
    gated = gated.reshape(locals_, seqs, slots, width)
    order = np.arange(locals_ * slots).reshape(locals_, ranks, capacity).transpose(1, 0, 2).reshape(-1)
    to_send = jnp.asarray(np.eye(locals_ * slots)[order], BF16)
    to_slots = jnp.asarray(np.eye(locals_ * slots)[order].T, BF16)
    tokens = hidden_in.astype(F32)
    middles = []
    for s in range(seqs):
        back = send(mm(to_send, gated[:, s].reshape(locals_ * slots, width)).astype(BF16))
        middles.append(tokens[s] + mm(own_collect_a[s], back))
    middle = jnp.stack(middles)
    scale_two = rms_scale(middle)
    normed_two_low = (middle * scale_two * mlp_gain).astype(BF16).reshape(seqs * row_count, width)

    final = middle.reshape(seqs * row_count, width)
    grad_normed_two = jnp.zeros((seqs * row_count, width), F32)
    held = None
    for l in range(locals_):
        rows_in = send(mm(own_spread_m[l], normed_two_low).astype(BF16))
        slot_logits = mm(rows_in, mlp_router)
        me = (here * locals_ + l).astype(F32)
        pick_m = (expert_f[None, :] == me).astype(F32) - (
            expert_f[None, :] == other_sum[l][0] - me
        ).astype(F32)
        gate_m = jax.nn.sigmoid(jnp.sum(pick_m * slot_logits, axis=-1, keepdims=True))
        grad_rows = (gate_m * cot_rows[l].astype(F32)).astype(BF16)
        made = None
        for at, (low, inner) in enumerate(inner_full[l]):
            ends = (cot_rows[l], gate_m, pick_m, mlp_router) if at + 1 == len(inner_full[l]) else None
            joint = ends is not None and l + 1 < locals_
            made = expert_pass(rows_in, grad_rows, inner, down_full, l, low, made, ends, joint)
        if l + 1 < locals_:
            both_back = send(made[0])
            grad_normed_two = grad_normed_two + mm(own_collect_m[l], both_back[:, :width])
            final = final + mm(own_collect_m[l], both_back[:, width:])
        else:
            grad_back, held = send(made[0]), made[1]
    grad_normed_two = grad_normed_two.reshape(seqs, row_count, width)
    late = (collect_a, own_adapter.astype(F32)[:, None, :], weigh_a, attn_router, to_slots)
    (collect_a, mask, weigh_a, router_near, to_slots), grad_normed_two = lax.optimization_barrier(
        (late, grad_normed_two)
    )
    back_table = own_collect_m[locals_ - 1].reshape(seqs, row_count, mlp_rows)
    grad_middle, leaving = [], []
    for s in range(seqs):
        grad, rows = middle_back(
            s, grad_back, back_table, grad_normed_two, middle, cotangent, mlp_gain[None], own_spread_a
        )
        grad_middle.append(grad)
        leaving.append(rows)

    arrived = [send(leaving[0])]
    arrived[0], leaving[1:] = lax.optimization_barrier((arrived[0], leaving[1:]))
    arrived += [send(rows) for rows in leaving[1:]]
    down_pieces, up_pieces = [], []
    input_grad = None
    for s in range(seqs):
        grad_attended, dots = out_back(
            s, arrived[s], to_slots, gate_rows, projected, near_full, output_column
        )
        dq, dk, dv = attend_back(s, query_rot, key_value, grad_attended, probs, cos_q, sin_q, cos_k, sin_k)
        if s == 0:
            arrived[1:], held, dk = lax.optimization_barrier((arrived[1:], held, dk))
            held = send(held)
        part, grad_low = last_grad(
            s, dk, dv, dq, collect_a, dots, weigh_a, mask, adapt_up, router_near, adapt_down, near_full,
            value_full, query_column,
        )
        if s + 1 < seqs:
            arrived[s + 1], held, part = lax.optimization_barrier((arrived[s + 1], held, part))
        grad_normed = lax.psum_scatter(part, "expert", scatter_dimension=0, tiled=True)
        input_grad = input_back(s, grad_normed, grad_middle[s], hidden_in, attn_gain[None], input_grad)
        first = adapter_index[s] * RANK
        down_pieces.append(lax.dynamic_slice_in_dim(mm(grad_low, normed_low[s], TN), first, RANK, 0))
        up_piece = jnp.concatenate([mm(low_rank[s], dk, TN), mm(low_rank[s], dv, TN)], axis=1)
        up_pieces.append(lax.dynamic_slice_in_dim(up_piece, first, RANK, 0))
    final = final + mm(own_collect_m[locals_ - 1], held)
    layer_out = final.astype(BF16).reshape(seqs, row_count, width)

    down_part = width // (groups * ranks)
    pieces = jnp.concatenate(
        [
            jnp.stack(down_pieces).reshape(seqs * RANK, groups, ranks, down_part),
            jnp.stack(up_pieces).reshape(seqs * RANK, groups, ranks, 2 * down_part),
        ],
        axis=-1,
    )
    pieces = pieces.transpose(1, 0, 2, 3).reshape(groups, seqs * RANK, 3 * ranks * down_part)
    pieces = lax.all_to_all(pieces, "dp", split_axis=0, concat_axis=0, tiled=True)
    pieces = pieces.reshape(groups * seqs, RANK, 3 * ranks * down_part)
    belongs = (adapters[:, None] == jnp.arange(NADAPT, dtype=jnp.int32)[None, :]).astype(F32)
    sums = jnp.einsum("qkf,qa->akf", pieces, belongs, precision=PRECISE)
    sums = sums.reshape(NADAPT * RANK, ranks, 3 * down_part).transpose(1, 0, 2)
    sums = jnp.sum(send(sums), axis=0).T
    return (layer_out, input_grad, sums[:down_part], sums[down_part:])


def solution(mesh):
    return jax.shard_map(
        per_device,
        mesh=mesh,
        in_specs=(
            P("dp", "expert", None),
            P("dp", "expert", None),
            P("dp", None),
            P("dp", "expert", None),
            P("dp", "expert", None),
            P("dp"),
            P(),
            P(),
            P(),
            P(),
            P("dp", None),
            P("expert", "dp", None),
            P("expert", "dp", None),
            P("expert", "dp", None),
            P("expert", "dp", None),
            P(),
            P(),
        ),
        out_specs=(
            P("dp", "expert", None),
            P("dp", "expert", None),
            P(("dp", "expert"), None),
            P(("dp", "expert"), None),
        ),
        check_vma=False,
    )
```

```python
import functools
import math

import jax
import jax.numpy as jnp
import numpy as np
from jax import lax
from jax.experimental import pallas as pl
from jax.experimental.pallas import tpu as pltpu
from jax.sharding import PartitionSpec as P

HEADS = 16
HDIM = 128
FF = 5632
EXPERTS = 8
TOP = 2
RANK = 16
NADAPT = 8

PRECISE = lax.Precision.HIGHEST
EPSILON = 1e-06
ROPE_BASE = 10000.0
MASKED_SCORE = -1e30
SCALE_QK = 1.0 / math.sqrt(HDIM)
BF16 = jnp.bfloat16
F32 = jnp.float32
VMEM_LIMIT = 58 * 1024 * 1024

NN = (((1,), (0,)), ((), ()))
NT = (((1,), (1,)), ((), ()))
TN = (((0,), (0,)), ((), ()))


def mm(left, right, dims=NN):
    return lax.dot_general(left, right, dims, preferred_element_type=F32)


def params(*semantics):
    return pltpu.CompilerParams(dimension_semantics=semantics, vmem_limit_bytes=VMEM_LIMIT)


def once(shape, index_map):
    return pl.BlockSpec(shape, index_map, pipeline_mode=pl.Buffered(1))


def rms_scale(values):
    return lax.rsqrt(jnp.mean(values * values, axis=-1, keepdims=True) + EPSILON)


def norm_back(values, scale_rows, norm_gain, grad_rows):
    scaled_grad = norm_gain * grad_rows
    return scale_rows * (
        scaled_grad
        - values * scale_rows * scale_rows * jnp.mean(scaled_grad * values, axis=-1, keepdims=True)
    )


def angle_tables(positions):
    half_dim = HDIM // 2
    frequency = ROPE_BASE ** (-(jnp.arange(half_dim, dtype=F32) * (2.0 / HDIM)))
    frequency = jnp.concatenate([frequency, frequency])
    sign = jnp.concatenate([-jnp.ones((half_dim,), F32), jnp.ones((half_dim,), F32)])
    angles = positions.astype(F32)[..., None] * frequency
    return (jnp.cos(angles), jnp.sin(angles) * sign)


def three_parts(values):
    first = values.astype(BF16)
    rest = values - first.astype(F32)
    second = rest.astype(BF16)
    third = (rest - second.astype(F32)).astype(BF16)
    return first, second, third


def hop(from_left, from_right, axis, size):
    rightward = [(i, i + 1) for i in range(size - 1)]
    leftward = [(i + 1, i) for i in range(size - 1)]
    return lax.ppermute(from_left, axis, rightward), lax.ppermute(from_right, axis, leftward)


def put_line(hops, axis, put, start):
    size = len(hops)
    here = lax.axis_index(axis)
    total = put(start, hops[0][0], here)
    for step in range(1, size):
        piece = jnp.where(here >= step, hops[step][0], hops[size - step][1])
        total = put(total, piece, lax.rem(here - step + size, size))
    return total


def exchange(total, axis, size, bit):
    other = lax.ppermute(total, axis, [(i, i ^ bit) for i in range(size)])
    low = jnp.bitwise_and(lax.axis_index(axis), bit) == 0
    return jnp.stack([jnp.where(low, total, other), jnp.where(low, other, total)])


def halves_bits(size):
    bits = [1 << k for k in range(1, size.bit_length() - 1)]
    return [bits, bits[::-1]]


def in_order(halves, orders, size):
    made = []
    for total, bits in zip(halves, orders):
        count = len(bits)
        order = sorted(range(count), key=lambda d: -bits[count - 1 - d])
        total = total.transpose(*order, *range(count, total.ndim))
        made.append(total.reshape(size, *total.shape[count:]))
    whole = jnp.stack(made, axis=1)
    return whole.reshape(-1, whole.shape[-1])


def send(buffer):
    return lax.all_to_all(buffer, "expert", split_axis=0, concat_axis=0, tiled=True)


def merge_body(core_ref, mine_ref, other_ref, out_ref):
    rows = mine_ref.shape[0]
    low = core_ref[0] == 0
    mine, other = mine_ref[...], other_ref[...]
    out_ref[:rows, :] = jnp.where(low, mine, other)
    out_ref[rows:, :] = jnp.where(low, other, mine)


def merge_halves(mine, other, core, block_rows):
    parts, rows, part = mine.shape
    half = pl.BlockSpec((None, block_rows, part), lambda q, g: (q, g, 0))
    return pl.pallas_call(
        merge_body,
        grid=(parts, rows // block_rows),
        in_specs=[pl.BlockSpec(memory_space=pltpu.SMEM), half, half],
        out_specs=pl.BlockSpec((2 * block_rows, part), lambda q, g: (g, q)),
        out_shape=jax.ShapeDtypeStruct((2 * rows, parts * part), BF16),
        compiler_params=params("arbitrary", "arbitrary"),
        name="merge_halves",
    )(core, mine, other)


def kv_body(seqs, seq_len, key_tiles, x_ref, low_ref, wk_ref, wv_ref, up_ref, cos_ref, sin_ref, out_ref):
    is_key = pl.program_id(0) < key_tiles

    @pl.when(is_key)
    def _():
        for s in range(seqs):
            rows = pl.ds(s * seq_len, seq_len)
            made = mm(x_ref[rows, :], wk_ref[...]) + mm(low_ref[rows, :], up_ref[...], NT)
            for h in range(made.shape[1] // HDIM):
                cols = slice(h * HDIM, (h + 1) * HDIM)
                part = made[:, cols]
                turned = part * cos_ref[...] + pltpu.roll(part, HDIM // 2, 1) * sin_ref[...]
                out_ref[rows, cols] = turned.astype(BF16)

    @pl.when(jnp.logical_not(is_key))
    def _():
        for s in range(seqs):
            rows = pl.ds(s * seq_len, seq_len)
            made = mm(x_ref[rows, :], wv_ref[...]) + mm(low_ref[rows, :], up_ref[...], NT)
            out_ref[rows, :] = made.astype(BF16)


def make_key_value(normed_low, low_rank, weights, value_weights, adapt_up, cos_k, sin_k, seqs):
    rows, width = normed_low.shape
    seq_len = rows // seqs
    tile = 512
    count = width // tile
    return pl.pallas_call(
        functools.partial(kv_body, seqs, seq_len, count),
        grid=(2 * count,),
        in_specs=[
            once((rows, width), lambda i: (0, 0)),
            once((rows, low_rank.shape[1]), lambda i: (0, 0)),
            pl.BlockSpec((width, tile), lambda i: (0, jnp.minimum(i, count - 1))),
            pl.BlockSpec((width, tile), lambda i: (0, jnp.maximum(i - count, 0))),
            pl.BlockSpec((tile, low_rank.shape[1]), lambda i: (i, 0)),
            once((seq_len, HDIM), lambda i: (0, 0)),
            once((seq_len, HDIM), lambda i: (0, 0)),
        ],
        out_specs=pl.BlockSpec((rows, tile), lambda i: (0, i)),
        out_shape=jax.ShapeDtypeStruct((rows, 2 * width), BF16),
        compiler_params=params("arbitrary"),
        name="key_value",
    )(normed_low, low_rank, weights, value_weights, adapt_up, cos_k, sin_k)


def project_body(x_ref, w_ref, *refs):
    made = mm(x_ref[...], w_ref[...])
    if len(refs) == 1:
        refs[0][...] = made.astype(BF16)
    else:
        gate_ref, out_ref, gated_ref = refs
        out_ref[...] = made.astype(BF16)
        gated_ref[...] = (made * gate_ref[...]).astype(BF16)


def project(values, weights, from_column, gate=None):
    locals_, rows, width = values.shape
    tile = 512
    first, step = from_column // tile, width // tile
    out_spec = pl.BlockSpec((None, rows, tile), lambda l, i: (l, 0, i))
    out_shape = jax.ShapeDtypeStruct(values.shape, BF16)
    in_specs = [
        pl.BlockSpec((None, rows, width), lambda l, i: (l, 0, 0)),
        pl.BlockSpec((width, tile), lambda l, i: (0, first + step * l + i)),
    ]
    more = []
    if gate is not None:
        in_specs.append(pl.BlockSpec((None, rows, 1), lambda l, i: (l, 0, 0)))
        more = [gate]
    return pl.pallas_call(
        project_body,
        grid=(locals_, step),
        in_specs=in_specs,
        out_specs=out_spec if gate is None else [out_spec] * 2,
        out_shape=out_shape if gate is None else [out_shape] * 2,
        compiler_params=params("arbitrary", "arbitrary"),
        name="project",
    )(values, weights, *more)


def attend_body(q_ref, k_ref, v_ref, cos_ref, sin_ref, qb_ref, kb_ref, rot_ref, out_ref, probs_ref):
    locals_, _, slots, _ = q_ref.shape
    rows = locals_ * slots
    q = q_ref[...].reshape(rows, HDIM).astype(F32)
    cos, sin = cos_ref[...].reshape(rows, HDIM), sin_ref[...].reshape(rows, HDIM)
    rot = (q * cos + pltpu.roll(q, HDIM // 2, 1) * sin).astype(BF16)
    rot_ref[...] = rot.reshape(rot_ref.shape)
    k, v = k_ref[0], v_ref[0]
    kb = kb_ref[0]
    for l in range(locals_):
        part = rot[l * slots : (l + 1) * slots]
        visible = kb <= qb_ref[l, 0]
        masked = jnp.where(visible, mm(part, k, NT), MASKED_SCORE)
        top = jnp.max(masked, axis=-1, keepdims=True)
        terms = jnp.exp((masked - top) * SCALE_QK)
        total = jnp.sum(terms, axis=-1, keepdims=True)
        probs = (terms * (1.0 / total)).astype(BF16)
        probs_ref[l, 0, 0] = probs
        out_ref[l, 0] = mm(probs, v).astype(BF16)


def attend(queries, key_value, cos_q, sin_q, query_blocks, key_blocks):
    locals_, seqs, slots, width = queries.shape
    seq_len = key_value.shape[1]
    q_spec = pl.BlockSpec((locals_, 1, slots, HDIM), lambda s, h: (0, s, 0, h))
    tab_spec = pl.BlockSpec((locals_, 1, slots, HDIM), lambda s, h: (0, s, 0, 0))
    return pl.pallas_call(
        attend_body,
        grid=(seqs, HEADS),
        in_specs=[
            q_spec,
            pl.BlockSpec((1, seq_len, HDIM), lambda s, h: (s, 0, h)),
            pl.BlockSpec((1, seq_len, HDIM), lambda s, h: (s, 0, HEADS + h)),
            tab_spec,
            tab_spec,
            pl.BlockSpec((locals_, 1, slots, 1), lambda s, h: (0, s, 0, 0)),
            pl.BlockSpec((1, 1, seq_len), lambda s, h: (s, 0, 0)),
        ],
        out_specs=[
            q_spec,
            q_spec,
            pl.BlockSpec((locals_, 1, 1, slots, seq_len), lambda s, h: (0, s, h, 0, 0)),
        ],
        out_shape=[
            jax.ShapeDtypeStruct(queries.shape, BF16),
            jax.ShapeDtypeStruct(queries.shape, BF16),
            jax.ShapeDtypeStruct((locals_, seqs, HEADS, slots, seq_len), BF16),
        ],
        compiler_params=params("arbitrary", "arbitrary"),
        name="attend",
    )(queries, key_value, key_value, cos_q, sin_q, query_blocks, key_blocks)


def attend_back_body(q_ref, k_ref, v_ref, g_ref, p_ref, cos_ref, sin_ref, ck_ref, sk_ref, dq_ref, dk_ref, dv_ref):
    locals_, _, slots, _ = q_ref.shape
    rows = locals_ * slots
    k, v = k_ref[0], v_ref[0]
    q = q_ref[...].reshape(rows, HDIM)
    grad = g_ref[...].reshape(rows, HDIM)
    probs = p_ref[...].reshape(rows, k.shape[0])
    weighed = probs.astype(F32) * mm(grad, v, NT)
    delta = jnp.sum(weighed, axis=-1, keepdims=True)
    grad_scores = (weighed - probs.astype(F32) * delta).astype(BF16)
    dq = mm(grad_scores, k) * SCALE_QK
    cos, sin = cos_ref[...].reshape(rows, HDIM), sin_ref[...].reshape(rows, HDIM)
    dq = dq * cos - pltpu.roll(dq, HDIM // 2, 1) * sin
    dq_ref[...] = dq.astype(BF16).reshape(dq_ref.shape)
    dk = mm(grad_scores, q, TN) * SCALE_QK
    dk_ref[...] = (dk * ck_ref[...] - pltpu.roll(dk, HDIM // 2, 1) * sk_ref[...]).astype(BF16)
    dv_ref[...] = mm(probs, grad, TN).astype(BF16)


def attend_back(s, query_rot, key_value, grad, probs, cos_q, sin_q, cos_k, sin_k):
    locals_, _, slots, width = query_rot.shape
    seq_len = key_value.shape[1]
    tab_spec = pl.BlockSpec((locals_, 1, slots, HDIM), lambda h: (0, s, 0, 0))
    key_tab = pl.BlockSpec((seq_len, HDIM), lambda h: (0, 0))
    grad_spec = pl.BlockSpec((locals_, slots, HDIM), lambda h: (0, 0, h))
    key_spec = pl.BlockSpec((seq_len, HDIM), lambda h: (0, h))
    return pl.pallas_call(
        attend_back_body,
        grid=(HEADS,),
        in_specs=[
            pl.BlockSpec((locals_, 1, slots, HDIM), lambda h: (0, s, 0, h)),
            pl.BlockSpec((1, seq_len, HDIM), lambda h: (s, 0, h)),
            pl.BlockSpec((1, seq_len, HDIM), lambda h: (s, 0, HEADS + h)),
            grad_spec,
            pl.BlockSpec((locals_, 1, 1, slots, seq_len), lambda h: (0, s, h, 0, 0)),
            tab_spec,
            tab_spec,
            key_tab,
            key_tab,
        ],
        out_specs=[grad_spec, key_spec, key_spec],
        out_shape=[
            jax.ShapeDtypeStruct((locals_, slots, width), BF16),
            jax.ShapeDtypeStruct((seq_len, width), BF16),
            jax.ShapeDtypeStruct((seq_len, width), BF16),
        ],
        compiler_params=params("arbitrary"),
        name="attend_back",
    )(query_rot, key_value, key_value, grad, probs, cos_q, sin_q, cos_k, sin_k)


def expert_body(has_start, is_last, joint, x_ref, c_ref, wg_ref, wu_ref, wd_ref, *refs):
    refs = list(refs)
    start = [refs.pop(0), refs.pop(0)] if has_start else []
    if is_last:
        cot_ref, gate_ref, pick_ref, router_ref = refs[:4]
        made_refs, (out_ref, gs_ref) = (refs[4:5], refs[5:7]) if joint else (refs[4:6], refs[6:8])
        late = start + [cot_ref]
    else:
        out_ref, gs_ref = refs[:2]
        late = start
    count = len(late)
    held, sem = (refs[-count - 1 : -1], refs[-1]) if count else ([], None)
    copies = [pltpu.make_async_copy(late[i], held[i], sem.at[i]) for i in range(count)]

    @pl.when(pl.program_id(0) == 0)
    def _():
        for copy in copies:
            copy.start()
        out_ref[...] = jnp.zeros_like(out_ref)
        gs_ref[...] = jnp.zeros_like(gs_ref)

    x, c = x_ref[...], c_ref[...]
    wg, wu, wd = wg_ref[...], wu_ref[...], wd_ref[...]
    gate, up = mm(x, wg), mm(x, wu)
    sig = jax.nn.sigmoid(gate)
    silu = gate * sig
    out_ref[...] += mm((silu * up).astype(BF16), wd)
    grad = mm(c, wd, NT)
    grad_gate = (grad * up * sig * (1.0 + gate * (1.0 - sig))).astype(BF16)
    grad_up = (grad * silu).astype(BF16)
    gs_ref[...] += mm(grad_gate, wg, NT) + mm(grad_up, wu, NT)

    @pl.when(pl.program_id(0) == pl.num_programs(0) - 1)
    def _():
        for copy in copies:
            copy.wait()
        made, back = out_ref[...], gs_ref[...]
        if has_start:
            made, back = made + held[0][...], back + held[1][...]
        if has_start and not is_last:
            out_ref[...] = made
            gs_ref[...] = back
        if is_last:
            share = gate_ref[...]
            dots = jnp.sum(held[-1][...].astype(F32) * made, axis=-1, keepdims=True)
            weigh = pick_ref[...] * (dots * share * (1.0 - share))
            high = weigh.astype(BF16)
            low = (weigh - high.astype(F32)).astype(BF16)
            router = router_ref[...]
            width = x_ref.shape[1]
            made_refs[0][:, :width] = (back + mm(high, router, NT) + mm(low, router, NT)).astype(BF16)
            if joint:
                made_refs[0][:, width:] = (share * made).astype(BF16)
            else:
                made_refs[1][...] = (share * made).astype(BF16)


def expert_pass(rows_in, grad_in, inner, down, l, down_from, start=None, last=None, joint=False):
    rows, width = rows_in.shape
    units = inner.shape[1] // 2
    tile = 512 if units % 512 == 0 and down_from % 512 == 0 else 256
    first = down_from // tile

    def whole(array):
        return once(array.shape, lambda i: (0,) * array.ndim)

    more = ([] if start is None else list(start)) + ([] if last is None else list(last))
    outs = [(2 * width, BF16)] if joint else [(width, F32 if last is None else BF16)] * 2
    late = ([] if start is None else [F32, F32]) + ([] if last is None else [BF16])
    away = len(late)
    scratch = [] if last is None else [pltpu.VMEM((rows, width), F32)] * 2
    if away:
        scratch += [pltpu.VMEM((rows, width), t) for t in late] + [pltpu.SemaphoreType.DMA((away,))]
    return pl.pallas_call(
        functools.partial(expert_body, start is not None, last is not None, joint),
        grid=(units // tile,),
        in_specs=[
            whole(rows_in),
            whole(grad_in),
            pl.BlockSpec((width, tile), lambda i: (0, i)),
            pl.BlockSpec((width, tile), lambda i: (0, units // tile + i)),
            pl.BlockSpec((None, tile, width), lambda i: (l, first + i, 0)),
        ]
        + [pl.BlockSpec(memory_space=pl.ANY) if i < away else whole(m) for i, m in enumerate(more)],
        out_specs=[once((rows, columns), lambda i: (0, 0)) for columns, _ in outs],
        out_shape=[jax.ShapeDtypeStruct((rows, columns), kind) for columns, kind in outs],
        scratch_shapes=scratch,
        compiler_params=params("arbitrary"),
        name="expert",
    )(rows_in, grad_in, inner, inner, down, *more)


def out_back_body(locals_, arrived_ref, order_ref, gate_ref, projected_ref, *refs):
    w_refs, (out_ref, dots_ref, rows_ref) = refs[:locals_], refs[locals_:]
    slots = projected_ref.shape[1]

    @pl.when(pl.program_id(0) == 0)
    def _():
        for l in range(locals_):
            rows = mm(order_ref[pl.ds(l * slots, slots), :], arrived_ref[...])
            dots_ref[l] = jnp.sum(rows * projected_ref[l].astype(F32), axis=-1, keepdims=True)
            rows_ref[l] = (rows * gate_ref[l]).astype(BF16)

    for l in range(locals_):
        out_ref[l] = mm(rows_ref[l], w_refs[l][...], NT).astype(BF16)


def out_back(s, arrived, order, gate, projected, weights, from_column):
    locals_, slots = gate.shape[0], gate.shape[2]
    rows, width = arrived.shape
    tile = 512
    return pl.pallas_call(
        functools.partial(out_back_body, locals_),
        grid=(width // tile,),
        in_specs=[
            once((rows, width), lambda i: (0, 0)),
            once((rows, rows), lambda i: (0, 0)),
            once((locals_, None, slots, 1), lambda i: (0, s, 0, 0)),
            once((locals_, None, slots, width), lambda i: (0, s, 0, 0)),
        ]
        + [
            pl.BlockSpec((tile, width), lambda i, l=l: (i, from_column // width + l))
            for l in range(locals_)
        ],
        out_specs=[
            pl.BlockSpec((locals_, slots, tile), lambda i: (0, 0, i)),
            pl.BlockSpec((locals_, slots, 1), lambda i: (0, 0, 0)),
        ],
        out_shape=[
            jax.ShapeDtypeStruct((locals_, slots, width), BF16),
            jax.ShapeDtypeStruct((locals_, slots, 1), F32),
        ],
        scratch_shapes=[pltpu.VMEM((locals_, slots, width), BF16)],
        compiler_params=params("arbitrary"),
        name="out_back",
    )(arrived, order, gate, projected, *([weights] * locals_))


def last_body(
    locals_, seq_len, dk_ref, dv_ref, dq_ref, table_ref, dots_ref, weigh_ref, mask_ref, up_ref, router_ref, down_ref, wk_ref, wv_ref, *refs
):
    wq_refs, (out_ref, low_ref, source_ref, weigh_low_ref) = refs[:locals_], refs[locals_:]
    width = dk_ref.shape[1]
    slots = dq_ref.shape[1]

    @pl.when(pl.program_id(0) == 0)
    def _():
        low = mm(dk_ref[...], up_ref[:width, :]) + mm(dv_ref[...], up_ref[width:, :])
        low_ref[...] = (low * mask_ref[...]).astype(BF16)
        for l in range(locals_):
            weigh = weigh_ref[l] * dots_ref[l]
            high = weigh.astype(BF16)
            weigh_low_ref[l, :, :EXPERTS] = high
            weigh_low_ref[l, :, EXPERTS:] = (weigh - high.astype(F32)).astype(BF16)

    router = jnp.concatenate([router_ref[...]] * 2, axis=1)
    for l in range(locals_):
        source = mm(dq_ref[l], wq_refs[l][...], NT) + mm(weigh_low_ref[l], router, NT)
        source_ref[pl.ds(l * slots, slots), :] = source.astype(BF16)
    total = mm(dk_ref[...], wk_ref[...], NT) + mm(dv_ref[...], wv_ref[...], NT)
    total += mm(low_ref[...], down_ref[...], NT)
    total += mm(table_ref[0], source_ref[...])
    out_ref[...] = total.astype(BF16)


def last_grad(
    s, dk, dv, dq, table, dots, weigh, mask, adapt_up, router, adapt_down, weights, value_weights, query_column
):
    seq_len, width = dk.shape
    locals_, slots, _ = dq.shape
    tile = 256
    ranks = adapt_up.shape[1]
    return pl.pallas_call(
        functools.partial(last_body, locals_, seq_len),
        grid=(width // tile,),
        in_specs=[
            once((seq_len, width), lambda i: (0, 0)),
            once((seq_len, width), lambda i: (0, 0)),
            once((locals_, slots, width), lambda i: (0, 0, 0)),
            once((1, seq_len, locals_ * slots), lambda i: (s, 0, 0)),
            once((locals_, slots, 1), lambda i: (0, 0, 0)),
            once((locals_, None, slots, EXPERTS), lambda i: (0, s, 0, 0)),
            once((None, 1, ranks), lambda i: (s, 0, 0)),
            once((2 * width, ranks), lambda i: (0, 0)),
            pl.BlockSpec((tile, EXPERTS), lambda i: (i, 0)),
            pl.BlockSpec((tile, ranks), lambda i: (i, 0)),
            pl.BlockSpec((tile, width), lambda i: (i, 0)),
            pl.BlockSpec((tile, width), lambda i: (i, 0)),
        ]
        + [
            pl.BlockSpec((tile, width), lambda i, l=l: (i, query_column // width + l))
            for l in range(locals_)
        ],
        out_specs=[
            pl.BlockSpec((seq_len, tile), lambda i: (0, i)),
            pl.BlockSpec((seq_len, ranks), lambda i: (0, 0)),
        ],
        out_shape=[
            jax.ShapeDtypeStruct((seq_len, width), BF16),
            jax.ShapeDtypeStruct((seq_len, ranks), BF16),
        ],
        scratch_shapes=[
            pltpu.VMEM((locals_ * slots, tile), BF16),
            pltpu.VMEM((locals_, slots, 2 * EXPERTS), BF16),
        ],
        compiler_params=params("arbitrary"),
        name="last_grad",
    )(dk, dv, dq, table, dots, weigh, mask, adapt_up, router, adapt_down, weights, value_weights, *([weights] * locals_))


def middle_back_body(back_ref, table_ref, part_ref, middle_ref, cot_ref, gain_ref, spread_ref, out_ref, rows_ref):
    middle = middle_ref[...]
    scale = rms_scale(middle)
    grad = part_ref[...] + mm(table_ref[...], back_ref[...])
    out = cot_ref[...].astype(F32) + norm_back(middle, scale, gain_ref[...], grad)
    out_ref[...] = out
    rows_ref[...] = mm(spread_ref[...], out.astype(BF16)).astype(BF16)


def middle_back(s, back, table, part, middle, cotangent, gain, spread):
    _, rows, width = middle.shape
    slots = spread.shape[1]

    def one(array):
        return once((None, *array.shape[1:]), lambda i: (s, 0, 0))

    return pl.pallas_call(
        middle_back_body,
        grid=(1,),
        in_specs=[
            once(back.shape, lambda i: (0, 0)),
            one(table),
            one(part),
            one(middle),
            one(cotangent),
            once(gain.shape, lambda i: (0, 0)),
            one(spread),
        ],
        out_specs=[once((rows, width), lambda i: (0, 0)), once((slots, width), lambda i: (0, 0))],
        out_shape=[
            jax.ShapeDtypeStruct((rows, width), F32),
            jax.ShapeDtypeStruct((slots, width), BF16),
        ],
        compiler_params=params("arbitrary"),
        name="middle_back",
    )(back, table, part, middle, cotangent, gain, spread)


def input_back_body(grad_ref, middle_ref, tokens_ref, gain_ref, *refs):
    tokens = tokens_ref[...].astype(F32)
    refs[-1][...] = middle_ref[...] + norm_back(
        tokens, rms_scale(tokens), gain_ref[...], grad_ref[...].astype(F32)
    )


def input_back(s, grad, grad_middle, tokens, gain, total):
    seqs, rows, width = tokens.shape
    tile = 128
    flat = pl.BlockSpec((tile, width), lambda i: (i, 0))
    one = pl.BlockSpec((None, tile, width), lambda i: (s, i, 0))
    return pl.pallas_call(
        input_back_body,
        grid=(rows // tile,),
        in_specs=[flat, flat, one, pl.BlockSpec((1, width), lambda i: (0, 0))]
        + ([] if total is None else [pl.BlockSpec(memory_space=pl.ANY)]),
        out_specs=one,
        out_shape=jax.ShapeDtypeStruct(tokens.shape, F32),
        input_output_aliases={} if total is None else {4: 0},
        compiler_params=params("arbitrary"),
        name="input_back",
    )(grad, grad_middle, tokens, gain, *([] if total is None else [total]))


def per_device(
    hidden_in,
    cotangent,
    block_ids,
    attn_routes,
    mlp_routes,
    adapter_index,
    attn_gain,
    mlp_gain,
    attn_router,
    mlp_router,
    kv_weight,
    query_weight,
    output_weight,
    inner_weight,
    down_weight,
    adapt_down,
    adapt_up,
):
    seqs, row_count, width = hidden_in.shape
    seq_len = block_ids.shape[1]
    ranks = seq_len // row_count
    locals_ = query_weight.shape[0]
    capacity = (17 * row_count * TOP + 16 * EXPERTS - 1) // (16 * EXPERTS)
    slots = ranks * capacity
    here = lax.axis_index("expert")

    query_column = width
    output_column = query_column + locals_ * width
    near = jnp.concatenate(
        [kv_weight[:, :width]]
        + [query_weight[l] for l in range(locals_)]
        + [output_weight[l] for l in range(locals_)],
        axis=1,
    )
    near_full = lax.all_gather(near, "dp", axis=0, tiled=True)
    down_full = lax.all_gather(down_weight, "dp", axis=1, tiled=True)
    groups = width // kv_weight.shape[0]

    def stretch(array, l, low, high):
        return jnp.concatenate([array[l, :, low:high], array[l, :, FF + low : FF + high]], axis=1)

    inner_full, beside = [], []
    for l in range(locals_):
        pieces = []
        cut = 2 * 512 if l + 1 < locals_ else FF * 3 // 4 // 512 * 512
        if l + 1 < locals_:
            pieces.append((0, None))
            beside.append(stretch(inner_weight, l, 0, cut))
        else:
            pieces.append((0, lax.all_gather(stretch(inner_weight, l, 0, cut), "dp", axis=0, tiled=True)))
        pieces.append((cut, lax.all_gather(stretch(inner_weight, l, cut, FF), "dp", axis=0, tiled=True)))
        inner_full.append(pieces)

    routes = lax.all_gather(
        jnp.concatenate([attn_routes, mlp_routes], axis=-1), "expert", axis=1, tiled=True
    ).reshape(seqs, ranks, row_count, 2, TOP)
    adapters = lax.all_gather(adapter_index, "dp", axis=0, tiled=True)
    expert_ids = jnp.arange(EXPERTS, dtype=jnp.int32)
    onehot = (routes[..., None] == expert_ids).astype(F32)
    hits = jnp.sum(onehot, axis=4)
    earlier = (
        jnp.arange(row_count)[:, None] > jnp.arange(row_count)[None, :]
    ).astype(BF16)
    before = jnp.einsum("ut,sptke->spuke", earlier, hits.astype(BF16), preferred_element_type=F32)
    place = jnp.sum(onehot * before[..., None, :], axis=-1).astype(jnp.int32)
    attn_all, mlp_all = routes[:, :, :, 0], routes[:, :, :, 1]
    attn_place, mlp_place = place[:, :, :, 0], place[:, :, :, 1]
    source = jnp.arange(ranks, dtype=jnp.int32)[None, :, None, None]
    which = jnp.arange(seqs, dtype=jnp.int32)[:, None, None, None]

    local_a = attn_all - here * locals_
    is_local = (local_a >= 0) & (local_a < locals_)
    slot_a = jnp.where(is_local, local_a * slots + source * capacity + attn_place, -1)
    slot_a = slot_a.reshape(seqs, seq_len, TOP)
    slot_iota = jnp.arange(locals_ * slots, dtype=jnp.int32)
    spread_a = (
        (slot_iota[None, :, None] == slot_a[:, None, :, 0])
        | (slot_iota[None, :, None] == slot_a[:, None, :, 1])
    ).astype(BF16)
    collect_a = (
        (slot_iota[None, None, :] == slot_a[:, :, 0, None])
        | (slot_iota[None, None, :] == slot_a[:, :, 1, None])
    ).astype(BF16)

    def own(array):
        return lax.dynamic_index_in_dim(array, here, 1, keepdims=False)

    attn_own, attn_own_place = own(attn_all), own(attn_place)
    mlp_own, mlp_own_place = own(mlp_all), own(mlp_place)
    own_slot = attn_own * capacity + attn_own_place
    own_iota = jnp.arange(EXPERTS * capacity, dtype=jnp.int32)
    own_spread_a = (
        (own_iota[None, :, None] == own_slot[:, None, :, 0])
        | (own_iota[None, :, None] == own_slot[:, None, :, 1])
    ).astype(BF16)
    own_collect_a = (
        (own_iota[None, None, :] == own_slot[:, :, 0, None])
        | (own_iota[None, None, :] == own_slot[:, :, 1, None])
    ).astype(BF16)
    mlp_rows = ranks * seqs * capacity
    mlp_iota = jnp.arange(mlp_rows, dtype=jnp.int32)
    own_spread_m, own_collect_m, other_sum = [], [], []
    for l in range(locals_):
        ids = jnp.where(
            mlp_own % locals_ == l,
            (mlp_own // locals_) * (seqs * capacity) + which[:, 0] * capacity + mlp_own_place,
            -1,
        ).reshape(seqs * row_count, TOP)
        own_spread_m.append(
            ((mlp_iota[:, None] == ids[None, :, 0]) | (mlp_iota[:, None] == ids[None, :, 1])).astype(BF16)
        )
        own_collect_m.append(
            ((mlp_iota[None, :] == ids[:, 0, None]) | (mlp_iota[None, :] == ids[:, 1, None])).astype(BF16)
        )
        ids = jnp.where(
            mlp_all == here * locals_ + l,
            source * (seqs * capacity) + which * capacity + mlp_place,
            -1,
        ).reshape(seqs * seq_len, TOP)
        table = (
            (mlp_iota[:, None] == ids[None, :, 0]) | (mlp_iota[:, None] == ids[None, :, 1])
        ).astype(BF16)
        both = jnp.sum(mlp_all, axis=-1).reshape(seqs * seq_len, 1).astype(BF16)
        sums = mm(table, jnp.concatenate([both, jnp.ones_like(both)], axis=1))
        other_sum.append((sums[:, :1], sums[:, 1:]))

    hidden_first, routes = lax.optimization_barrier((hidden_in, routes))
    hops = [(hidden_first, hidden_first)]
    hops.append(hop(*hops[-1], "expert", ranks))

    orders = halves_bits(groups)

    def halves_of(block):
        return [block[: block.shape[0] // 2], block[block.shape[0] // 2 :]]

    def exchange_halves(halves, step):
        return [exchange(half, "dp", groups, bits[step]) for half, bits in zip(halves, orders)]

    part = width // ranks
    value_half = halves_of(lax.dynamic_slice_in_dim(kv_weight, width + here * part, part, 1))
    for step in range(len(orders[0])):
        value_half = exchange_halves(value_half, step)
    value_half = in_order(value_half, orders, groups // 2)
    while len(hops) < ranks:
        hops.append(hop(*hops[-1], "expert", ranks))
    value_half, hops[-1] = lax.optimization_barrier((value_half, hops[-1]))
    value_hops = [(value_half, value_half)]
    while len(value_hops) < 3:
        value_hops.append(hop(*value_hops[-1], "expert", ranks))
    everyone = put_line(
        hops,
        "expert",
        lambda total, piece, at: lax.dynamic_update_slice(total, piece[:, None], (0, at, 0, 0)),
        jnp.zeros((seqs, ranks, row_count, width), BF16),
    ).reshape(seqs, seq_len, width)
    tokens_all = everyone.astype(F32)
    scale_all = rms_scale(tokens_all)
    normed_low = lax.optimization_barrier((tokens_all * scale_all * attn_gain).astype(BF16))
    router_parts = jnp.concatenate(three_parts(attn_gain[:, None] * attn_router.astype(F32)), axis=1)
    parts = mm(everyone.reshape(seqs * seq_len, width), router_parts).reshape(seqs, seq_len, 3, EXPERTS)
    logits = scale_all * (parts[:, :, 0] + (parts[:, :, 1] + parts[:, :, 2]))
    onehot_a = onehot[:, :, :, 0].reshape(seqs, seq_len, TOP, EXPERTS)
    gap = jnp.sum((onehot_a[:, :, 0] - onehot_a[:, :, 1]) * logits, axis=-1)

    flat_routes = attn_all.reshape(seqs, seq_len, TOP)
    places = jnp.arange(seq_len, dtype=jnp.int32)
    columns = [
        block_ids,
        jnp.broadcast_to(places // 128, block_ids.shape),
        jnp.broadcast_to(places % 128, block_ids.shape),
        jnp.sum(flat_routes, axis=-1),
        flat_routes[..., 0],
    ]
    known = jnp.stack([c.astype(BF16) for c in columns] + list(three_parts(gap)), axis=-1)
    known = jnp.einsum("srt,stc->src", spread_a, known, preferred_element_type=F32)
    known = known.reshape(seqs, locals_, slots, known.shape[-1]).transpose(1, 0, 2, 3)
    self_id = (here * locals_ + jnp.arange(locals_)).astype(F32)[:, None, None]
    slot_blocks = known[..., 0].astype(jnp.int32)
    slot_place = known[..., 1] * 128.0 + known[..., 2]
    slot_other = known[..., 3] - self_id
    slot_gap = known[..., 5] + (known[..., 6] + known[..., 7])
    slot_gap = jnp.where(known[..., 4] == self_id, slot_gap, -slot_gap)
    gate_a = jax.nn.sigmoid(slot_gap)
    expert_f = expert_ids.astype(F32)
    pick_a = (expert_f == self_id[..., None]).astype(F32) - (expert_f == slot_other[..., None]).astype(F32)
    weigh_a = pick_a * (gate_a * jax.nn.sigmoid(-slot_gap))[..., None]
    cos_q, sin_q = angle_tables(slot_place)
    cos_k, sin_k = angle_tables(places)
    query_blocks = slot_blocks[..., None]
    key_blocks = block_ids[:, None, :]

    flat_low = normed_low.reshape(seqs * seq_len, width)
    own_adapter = (
        jnp.arange(NADAPT * RANK, dtype=jnp.int32)[None, :] // RANK == adapter_index[:, None]
    )
    low_rank = mm(flat_low, adapt_down).reshape(seqs, seq_len, NADAPT * RANK)
    low_rank = jnp.where(own_adapter[:, None, :], low_rank, 0.0).astype(BF16)
    picked = jnp.einsum(
        "slrt,std->lsrd",
        spread_a.reshape(seqs, locals_, slots, seq_len),
        normed_low,
        preferred_element_type=F32,
    ).astype(BF16)
    beside, picked = lax.optimization_barrier((beside, picked))
    beside = [exchange_halves(halves_of(block), 0) for block in beside]
    queries = project(picked.reshape(locals_, seqs * slots, width), near_full, query_column)
    value_hops[2], normed_low = lax.optimization_barrier((value_hops[2], normed_low))
    while len(value_hops) < ranks:
        value_hops.append(hop(*value_hops[-1], "expert", ranks))
    value_line = put_line(
        value_hops,
        "expert",
        lambda total, piece, at: lax.dynamic_update_slice(total, piece[None], (at, 0, 0)),
        jnp.zeros((ranks, *value_half.shape), BF16),
    )
    value_line, queries, low_rank = lax.optimization_barrier((value_line, queries, low_rank))
    value_full = merge_halves(
        value_line,
        lax.ppermute(value_line, "dp", [(i, i ^ 1) for i in range(groups)]),
        jnp.bitwise_and(lax.axis_index("dp"), 1).astype(jnp.int32).reshape(1),
        kv_weight.shape[0],
    )

    flat_cot, value_full = lax.optimization_barrier((cotangent, value_full))
    flat_cot = flat_cot.reshape(seqs * row_count, width)
    cot_rows = [send(mm(own_spread_m[l], flat_cot).astype(BF16)) for l in range(locals_)]

    key_value = make_key_value(
        flat_low, low_rank.reshape(seqs * seq_len, -1), near_full, value_full, adapt_up, cos_k, sin_k, seqs
    ).reshape(seqs, seq_len, 2 * width)

    query_rot, attended, probs = attend(
        queries.reshape(locals_, seqs, slots, width), key_value, cos_q, sin_q, query_blocks, key_blocks
    )
    cot_rows[0], attended = lax.optimization_barrier((cot_rows[0], attended))
    gate_rows = gate_a[..., None]
    projected, gated = project(
        attended.reshape(locals_, seqs * slots, width),
        near_full,
        output_column,
        gate_rows.reshape(locals_, seqs * slots, 1),
    )
    beside, projected = lax.optimization_barrier((beside, projected))
    for l, halves in enumerate(beside):
        for step in range(1, len(orders[0])):
            halves = exchange_halves(halves, step)
        halves = [exchange(half, "dp", groups, 1) for half in halves]
        inner_full[l][0] = (0, in_order(halves, [bits + [1] for bits in orders], groups))
    projected = projected.reshape(locals_, seqs, slots, width)
    gated = gated.reshape(locals_, seqs, slots, width)
    order = np.arange(locals_ * slots).reshape(locals_, ranks, capacity).transpose(1, 0, 2).reshape(-1)
    to_send = jnp.asarray(np.eye(locals_ * slots)[order], BF16)
    to_slots = jnp.asarray(np.eye(locals_ * slots)[order].T, BF16)
    tokens = hidden_in.astype(F32)
    middles = []
    for s in range(seqs):
        back = send(mm(to_send, gated[:, s].reshape(locals_ * slots, width)).astype(BF16))
        middles.append(tokens[s] + mm(own_collect_a[s], back))
    middle = jnp.stack(middles)
    scale_two = rms_scale(middle)
    normed_two_low = (middle * scale_two * mlp_gain).astype(BF16).reshape(seqs * row_count, width)

    final = middle.reshape(seqs * row_count, width)
    grad_normed_two = jnp.zeros((seqs * row_count, width), F32)
    held = None
    for l in range(locals_):
        rows_in = send(mm(own_spread_m[l], normed_two_low).astype(BF16))
        slot_logits = mm(rows_in, mlp_router)
        me = (here * locals_ + l).astype(F32)
        pick_m = (expert_f[None, :] == me).astype(F32) - (
            expert_f[None, :] == other_sum[l][0] - me
        ).astype(F32)
        gate_m = jax.nn.sigmoid(jnp.sum(pick_m * slot_logits, axis=-1, keepdims=True))
        grad_rows = (gate_m * cot_rows[l].astype(F32)).astype(BF16)
        made = None
        for at, (low, inner) in enumerate(inner_full[l]):
            ends = (cot_rows[l], gate_m, pick_m, mlp_router) if at + 1 == len(inner_full[l]) else None
            joint = ends is not None and l + 1 < locals_
            made = expert_pass(rows_in, grad_rows, inner, down_full, l, low, made, ends, joint)
        if l + 1 < locals_:
            both_back = send(made[0])
            grad_normed_two = grad_normed_two + mm(own_collect_m[l], both_back[:, :width])
            final = final + mm(own_collect_m[l], both_back[:, width:])
        else:
            grad_back, held = send(made[0]), made[1]
    grad_normed_two = grad_normed_two.reshape(seqs, row_count, width)
    late = (collect_a, own_adapter.astype(F32)[:, None, :], weigh_a, attn_router, to_slots)
    (collect_a, mask, weigh_a, router_near, to_slots), grad_normed_two = lax.optimization_barrier(
        (late, grad_normed_two)
    )
    back_table = own_collect_m[locals_ - 1].reshape(seqs, row_count, mlp_rows)
    grad_middle, leaving = [], []
    for s in range(seqs):
        grad, rows = middle_back(
            s, grad_back, back_table, grad_normed_two, middle, cotangent, mlp_gain[None], own_spread_a
        )
        grad_middle.append(grad)
        leaving.append(rows)

    arrived = [send(leaving[0])]
    arrived[0], leaving[1:] = lax.optimization_barrier((arrived[0], leaving[1:]))
    arrived += [send(rows) for rows in leaving[1:]]
    down_pieces, up_pieces = [], []
    input_grad = None
    for s in range(seqs):
        grad_attended, dots = out_back(
            s, arrived[s], to_slots, gate_rows, projected, near_full, output_column
        )
        dq, dk, dv = attend_back(s, query_rot, key_value, grad_attended, probs, cos_q, sin_q, cos_k, sin_k)
        if s == 0:
            arrived[1:], held, dk = lax.optimization_barrier((arrived[1:], held, dk))
            held = send(held)
        part, grad_low = last_grad(
            s, dk, dv, dq, collect_a, dots, weigh_a, mask, adapt_up, router_near, adapt_down, near_full,
            value_full, query_column,
        )
        if s + 1 < seqs:
            arrived[s + 1], held, part = lax.optimization_barrier((arrived[s + 1], held, part))
        grad_normed = lax.psum_scatter(part, "expert", scatter_dimension=0, tiled=True)
        input_grad = input_back(s, grad_normed, grad_middle[s], hidden_in, attn_gain[None], input_grad)
        first = adapter_index[s] * RANK
        down_pieces.append(lax.dynamic_slice_in_dim(mm(grad_low, normed_low[s], TN), first, RANK, 0))
        up_piece = jnp.concatenate([mm(low_rank[s], dk, TN), mm(low_rank[s], dv, TN)], axis=1)
        up_pieces.append(lax.dynamic_slice_in_dim(up_piece, first, RANK, 0))
    final = final + mm(own_collect_m[locals_ - 1], held)
    layer_out = final.astype(BF16).reshape(seqs, row_count, width)

    down_part = width // (groups * ranks)
    pieces = jnp.concatenate(
        [
            jnp.stack(down_pieces).reshape(seqs * RANK, groups, ranks, down_part),
            jnp.stack(up_pieces).reshape(seqs * RANK, groups, ranks, 2 * down_part),
        ],
        axis=-1,
    )
    pieces = pieces.transpose(1, 0, 2, 3).reshape(groups, seqs * RANK, 3 * ranks * down_part)
    pieces = lax.all_to_all(pieces, "dp", split_axis=0, concat_axis=0, tiled=True)
    pieces = pieces.reshape(groups * seqs, RANK, 3 * ranks * down_part)
    belongs = (adapters[:, None] == jnp.arange(NADAPT, dtype=jnp.int32)[None, :]).astype(F32)
    sums = jnp.einsum("qkf,qa->akf", pieces, belongs, precision=PRECISE)
    sums = sums.reshape(NADAPT * RANK, ranks, 3 * down_part).transpose(1, 0, 2)
    sums = jnp.sum(send(sums), axis=0).T
    return (layer_out, input_grad, sums[:down_part], sums[down_part:])


def solution(mesh):
    return jax.shard_map(
        per_device,
        mesh=mesh,
        in_specs=(
            P("dp", "expert", None),
            P("dp", "expert", None),
            P("dp", None),
            P("dp", "expert", None),
            P("dp", "expert", None),
            P("dp"),
            P(),
            P(),
            P(),
            P(),
            P("dp", None),
            P("expert", "dp", None),
            P("expert", "dp", None),
            P("expert", "dp", None),
            P("expert", "dp", None),
            P(),
            P(),
        ),
        out_specs=(
            P("dp", "expert", None),
            P("dp", "expert", None),
            P(("dp", "expert"), None),
            P(("dp", "expert"), None),
        ),
        check_vma=False,
    )
```
